128 devices in a mesh: dp: 2 (over y_lo), seq: 4 (over y_hi, core), mp: 16 (over x, z).
Axes of the slice: x: 4, y: 4 (y_hi: 2, y_lo: 2; y = y_hi * 2 + y_lo), z: 4, core: 2. Of those that a mesh axis runs over, the one named last changes fastest.
Arguments:
- tokens: bfloat16 [2, 1024, 2048], P('dp', 'seq', 'mp'), may hold values from -6 to 6
- doc_lengths: int32 [2, 4], P('dp'), may hold values from 1 to 896, 1024 in all within a row
- cotangent: bfloat16 [2, 1024, 2048], P('dp', 'seq', 'mp'), may hold values from -6 to 6
- norm_gains: bfloat16 [2, 2048], P(None, 'mp'), may hold values from 0.099609375 to 1.8984375
- w_branch: bfloat16 [2, 2048, 2816], P(None, None, 'mp'), may hold values from -0.125 to 0.125
- conv_weight: float32 [4, 2816], P(None, 'mp'), may hold values from -3 to 3
- lru_bias: float32 [3, 2816], P(None, 'mp'), may hold values from -4 to 4
- decay: float32 [2816], P('mp'), may hold values from -11.6 to -3.4
- gate_weights: bfloat16 [2, 16, 176, 176], P(None, 'mp'), may hold values from -0.4375 to 0.4375
- w_out: bfloat16 [2816, 2048], P('mp'), may hold values from -0.21875 to 0.21875
- w_up: bfloat16 [2, 2048, 6144], P(None, None, 'mp'), may hold values from -0.125 to 0.125
- w_down: bfloat16 [6144, 2048], P('mp'), may hold values from -0.109375 to 0.109375
Outputs:
- block_out: bfloat16 [2, 1024, 2048], P('dp', 'seq', 'mp')
- grad_tokens: float32 [2, 1024, 2048], P('dp', 'seq', 'mp')
- grad_gains: float32 [2, 2048], P(None, 'mp')
- grad_branch: float32 [2, 2048, 2816], P(None, ('dp', 'seq'), 'mp')
- grad_conv_weight: float32 [4, 2816], P(None, 'mp')
- grad_bias: float32 [3, 2816], P(None, 'mp')
- grad_decay: float32 [2816], P('mp')
- grad_gates: float32 [2, 16, 176, 176], P(None, 'mp')
- grad_out: float32 [2816, 2048], P('mp', ('dp', 'seq'))
- grad_up: float32 [2, 2048, 6144], P(None, ('dp', 'seq'), 'mp')
- grad_down: float32 [6144, 2048], P('mp', ('dp', 'seq'))
- block_states: float32 [2, 4, 2816], P('dp', 'seq', 'mp')
The draws below stay inside these ranges and needn't reach their ends.
Inputs may be any that keep to these rules, and one draw needn't show every extreme that they name: `doc_lengths`: each row's lengths sum to 1024, and each row has one document of exactly 896 tokens.
All inputs are finite; a program needn't handle non-finite values.
Results may differ from the reference program's by a relative error of at most 0.0096.
Values may be sent and summed in bfloat16 or wider, within the bound.
A program may use at most 128 MiB of HBM per device.

```python
import math
from functools import partial
import jax
import jax.numpy as jnp
import numpy as np
from jax import lax

D = 2048
R = 2816
NB = 16
FF = 6144
LEN = 1024
DOCS = 4
BW = 176
ROWS = 2
LONGEST = 896
N_SEQ = 4


def draw_decay(key, part):
    key = jax.random.fold_in(key, 7)
    lowest, upper_rate = (2e-05, 0.03)
    spread = jax.random.uniform(key, (R,), jnp.float32, jnp.log(lowest), jnp.log(upper_rate))
    return jnp.log(jnp.expm1(jnp.exp(spread)))


def steps_of(key, dims, shards, smallest, top_value):
    level = 1.0
    for dim, parts in shards:
        heights = jax.random.uniform(jax.random.fold_in(jax.random.fold_in(key, 6), dim), (parts,), jnp.float32, smallest / len(shards), top_value / len(shards))
        level = level * jnp.repeat(jnp.exp(heights), dims[dim] // parts).reshape((-1,) + (1,) * (len(dims) - 1 - dim))
    return level


def split_up(number_of, total, reach, skew):
    portions = [(1 << 20) // math.isqrt(grade ** skew) + 1 for grade in range(2, number_of + 1)]
    surplus, given = total - reach - (number_of - 1), [1] * (number_of - 1)
    while surplus > 0:
        candidates = [i for i in range(number_of - 1) if given[i] < reach]
        mass, budget = sum([portions[i] for i in candidates]), surplus
        for i in candidates:
            extra = min(reach - given[i], max(1, budget * portions[i] // mass), surplus)
            given[i] = given[i] + extra
            surplus = surplus - extra
    return np.array([reach] + given)


def ragged_sizes(own_key, number_of, total, reach, lean):
    if number_of == 2:
        one = jax.random.randint(own_key, (), max(1, total - reach), min(reach, total - 1) + 1)
        return jnp.stack([one, total - one])
    tallies = jnp.asarray(split_up(number_of, total, reach, lean), jnp.int32)
    pairs = (number_of - 1) // 2
    donor, sink = tallies[1:1 + 2 * pairs:2], tallies[2:2 + 2 * pairs:2]
    slack = jnp.minimum(donor - 1, reach - sink)
    passed = jax.random.randint(jax.random.fold_in(own_key, 1), (pairs,), 0, 1 << 20) % (slack + 1)
    tallies = tallies.at[1:1 + 2 * pairs:2].set(donor - passed).at[2:2 + 2 * pairs:2].set(sink + passed)
    return tallies[jax.random.permutation(jax.random.fold_in(own_key, 2), number_of)]


def noise(rng, dims, width, reach, shards=(), kind=jnp.bfloat16):
    array = jax.random.normal(rng, dims, jnp.float32) * width
    if len(shards) > 0:
        array = steps_of(rng, dims, shards, -0.22, 0.18) * array
    return jnp.clip(array, min=-reach, max=reach).astype(kind)


def setup_inputs(seed: int = 0) -> dict:
    seeds = jax.random.split(jax.random.key(seed), 13)
    tokens = noise(seeds[0], (ROWS, LEN, D), 1.0, 6.0, ((0, 2), (1, 4), (2, 16)))
    doc_lengths = jax.vmap(lambda own: ragged_sizes(own, DOCS, LEN, LONGEST, 0))(jax.random.split(seeds[1], ROWS)).reshape((ROWS, DOCS)).astype(jnp.int32)
    cotangent = noise(seeds[2], (ROWS, LEN, D), 1.0, 6.0, ((0, 2), (1, 4), (2, 16)))
    norm_gains = jnp.clip(1.0 + 0.18 * jax.random.normal(seeds[3], (2, D), jnp.float32), 0.099609375, 1.8984375).astype(jnp.bfloat16)
    w_branch = noise(seeds[4], (2, D, R), D ** -0.5, 0.125, ((2, 16),))
    conv_weight = noise(seeds[5], (4, R), 0.5, 3.0, ((1, 16),), jnp.float32)
    lru_bias = noise(seeds[6], (3, R), 1.0, 4.0, ((1, 16),), jnp.float32)
    decay = draw_decay(jax.random.fold_in(seeds[12], 71), 0)
    gate_weights = noise(seeds[8], (2, NB, BW, BW), BW ** -0.5, 0.4375, ((1, 16),))
    w_out = noise(seeds[9], (R, D), (R // 4) ** -0.5, 0.21875, ((0, 16),))
    w_up = noise(seeds[10], (2, D, FF), D ** -0.5, 0.125, ((2, 16),))
    w_down = noise(seeds[11], (FF, D), (FF // 2) ** -0.5, 0.109375, ((0, 16),))
    return {"tokens": tokens, "doc_lengths": doc_lengths, "cotangent": cotangent, "norm_gains": norm_gains, "w_branch": w_branch, "conv_weight": conv_weight, "lru_bias": lru_bias, "decay": decay, "gate_weights": gate_weights, "w_out": w_out, "w_up": w_up, "w_down": w_down}


@jax.custom_vjp
def low(v):
    return lax.optimization_barrier(v.astype(jnp.bfloat16)).astype(jnp.float32)

@jax.custom_vjp
def low_back(v):
    return v

def low_keep(v):
    return (low(v), None)

def low_pass(kept, grad):
    return (grad,)

def back_keep(v):
    return (v, None)

def back_low(kept, grad):
    return (low(grad),)
low.defvjp(low_keep, low_pass)
low_back.defvjp(back_keep, back_low)
eps = 1e-06
highest = lax.Precision.HIGHEST

def normed(values, gain):
    scale = lax.rsqrt(lax.optimization_barrier(jnp.mean(values * values, axis=-1, keepdims=True)) + eps)
    return values * scale * gain

def combine(earlier, later):
    return (earlier[0] * later[0], later[0] * earlier[1] + later[1])

def lru_inputs(resets, pre, conv, decay):
    rate = jax.nn.softplus(decay)
    log_coef = -8.0 * jax.nn.sigmoid(pre[0]) * rate
    coef = jnp.exp(log_coef) * (1.0 - resets)[..., None]
    drive = jnp.sqrt(1.0 - jnp.exp(2.0 * log_coef) + 0.001) * jax.nn.sigmoid(pre[1]) * conv
    return (coef, drive)

def layout(doc_lengths):
    starts = (jnp.cumsum(doc_lengths, axis=1) - doc_lengths).astype(jnp.int32)
    places = jnp.arange(LEN, dtype=jnp.int32)
    segment = lax.optimization_barrier(jnp.sum((places[None, :, None] >= starts[:, None, :]).astype(jnp.int32), axis=2))
    resets = jnp.any(places[None, :, None] == starts[:, None, :], axis=2).astype(jnp.float32)
    masks = []
    for back in range(1, 4):
        earlier = jnp.pad(segment, ((0, 0), (back, 0)), constant_values=-1)[:, :LEN]
        masks.append((earlier == segment).astype(jnp.float32))
    return (resets, masks)

def shifted(values, back):
    return jnp.pad(values, ((0, 0), (back, 0), (0, 0)))[:, :LEN]

def forward(resets, masks, tokens, gains, w_branch, conv_weight, lru_bias, decay, gate_weights, w_out, w_up, w_down):
    first = low(normed(tokens, gains[0]))
    proj = low_back(jnp.einsum('rld,kdc->krlc', first, w_branch, precision=highest))
    inner = low(proj[1])
    conv = lru_bias[0] + conv_weight[0] * inner
    for back in range(1, 4):
        conv = conv + conv_weight[back] * masks[back - 1][..., None] * shifted(inner, back)
    blocked = low(conv).reshape(ROWS, LEN, NB, BW)
    pre = jnp.einsum('rlnb,knbc->krlnc', blocked, gate_weights, precision=highest).reshape(2, ROWS, LEN, R)
    pre = low_back(pre + lru_bias[1:, None, None, :])
    coef, drive = lru_inputs(resets, pre, conv, decay)
    _, state = lax.associative_scan(combine, (coef, drive), axis=1)
    mixed = low(jax.nn.gelu(proj[0]) * state)
    branch = low_back(jnp.einsum('rlc,cd->rld', mixed, w_out, precision=highest))
    middle = tokens + branch
    second = low(normed(low(middle), gains[1]))
    pair = low_back(jnp.einsum('rld,kdf->krlf', second, w_up, precision=highest))
    hidden = low(jax.nn.gelu(pair[0]) * pair[1])
    result = middle + low_back(jnp.einsum('rlf,fd->rld', hidden, w_down, precision=highest))
    span = LEN // N_SEQ
    return (result, state[:, span - 1::span, :])

def reference(tokens, doc_lengths, cotangent, norm_gains, w_branch, conv_weight, lru_bias, decay, gate_weights, w_out, w_up, w_down):
    resets, masks = layout(doc_lengths)
    floats = [a.astype(jnp.float32) for a in (tokens, norm_gains, w_branch, conv_weight, lru_bias, decay, gate_weights, w_out, w_up, w_down)]
    (result, states), pullback = jax.vjp(partial(forward, resets, masks), *floats)
    grads = pullback((cotangent.astype(jnp.float32), jnp.zeros_like(states)))
    return (result.astype(jnp.bfloat16), grads[0], grads[1], grads[2], grads[3], grads[4], grads[5], grads[6], grads[7], grads[8], grads[9], states)
```

```python
import functools

import jax
import jax.numpy as jnp
from jax import lax
from jax.experimental import pallas as pl
from jax.experimental.pallas import tpu as pltpu
from jax.sharding import PartitionSpec as P

MESH = pl.DeviceIdType.MESH
f32, bf16 = jnp.float32, jnp.bfloat16

T, D, C, F, W = 256, 2048, 176, 384, 128
H = T // 2
EPS = 1e-06
N_SEMS = 288
Q = 16
ALPHA, CUBIC = 0.7978845608028654, 0.044715


def nn(a, b):
    return lax.dot_general(a, b, (((1,), (0,)), ((), ())), preferred_element_type=f32)


def nt(a, b):
    return lax.dot_general(a, b, (((1,), (1,)), ((), ())), preferred_element_type=f32)


def sigmoid(v):
    return 1.0 / (1.0 + jnp.exp(-v))


def gelu_both(v):
    square = v * v
    t = jnp.tanh(ALPHA * v * (1.0 + CUBIC * square))
    half = 0.5 * (1.0 + t)
    return v * half, half + 0.5 * v * (1.0 - t * t) * ALPHA * (1.0 + 3.0 * CUBIC * square)


def kernel(
    tokens, lengths, cot, gains, conv_w, bias, decay, hbm_branch, hbm_gates, hbm_out, hbm_up, hbm_down,
    o_block, o_tokens, o_gains, o_branch, o_conv, o_bias, o_decay, o_gates, o_out, o_up, o_down, o_states,
    w_branch, gates, w_out, w_up, w_down,
    tok_g, cot_g, mid_g, gm_g, first, second, cot_d, gm_d,
    part1, part2, part3, part4, rs_r1, rs_s2, rs_r2,
    ext, conv, aa, rr, ii, qq, coef, through, local, p0, p1, gel, dgel, state, prev, pad_a, pad_b, tp,
    pair, ghid, mid_own, gmid_own, scale1, scale2,
    g_down, g_up, g_out, g_branch, y_down, y_up, y_out, y_branch, r_pair,
    halo_s, halo_r, back_s, back_r, car_s, car_r, rev_s, rev_r,
    gg, gg_r, gg_y, gg_f, small, small_r, small_y,
    send_sems, recv_sems, copy_sems,
):
    me, seq, dp = lax.axis_index("mp"), lax.axis_index("seq"), lax.axis_index("dp")
    x, z = me // 4, me % 4
    core, y = seq % 2, (seq // 2) * 2 + dp

    def turn(value, by):
        return lax.rem(value + by + 4, 4)

    def on_x(d):
        return {"mp": turn(x, d) * 4 + z}

    def on_z(d):
        return {"mp": x * 4 + turn(z, d)}

    def on_y(d):
        there = turn(y, d)
        return {"dp": there % 2, "seq": (there // 2) * 2 + core}

    def on_seq(d):
        return {"seq": turn(seq, d)}

    other = {"seq": (seq // 2) * 2 + (1 - core)}

    count = [0]
    sent = []

    def send(src, dst, where):
        i = count[0]
        count[0] += 1
        copy = pltpu.make_async_remote_copy(
            src_ref=src, dst_ref=dst, send_sem=send_sems.at[i], recv_sem=recv_sems.at[i],
            device_id=where, device_id_type=MESH,
        )
        copy.start()
        sent.append(copy)
        return copy

    loads = []
    for i, (src, dst) in enumerate(
        ((hbm_branch, w_branch), (hbm_gates, gates), (hbm_out, w_out), (hbm_down, w_down), (hbm_up, w_up))
    ):
        load = pltpu.make_async_copy(src, dst, copy_sems.at[i])
        load.start()
        loads.append(load)

    barrier = pltpu.get_barrier_semaphore()
    partners = [on_x(d) for d in (1, 2, 3)] + [on_z(d) for d in (1, 2, 3)] + [on_y(d) for d in (1, 2, 3)]
    partners += [on_seq(d) for d in (1, 2, 3)]
    for where in partners:
        pl.semaphore_signal(barrier, inc=1, device_id=where, device_id_type=MESH)

    def axis_of(h, phase):
        return (on_x, on_z)[(h + phase) % 2]

    def place(h, first_hop, second_hop):
        if h == 0:
            return turn(x, -first_hop), turn(z, -second_hop)
        return turn(x, -second_hop), turn(z, -first_hop)

    ORDER = (1, 3, 2)

    def gather_start(buf, rows):
        arrivals = []

        def view(h, cx, cz):
            return buf.at[h, cx, cz, pl.ds(0, rows[h])]

        for d in ORDER:
            for h in range(2):
                ref = view(h, x, z)
                arrivals.append((h, d, send(ref, ref, axis_of(h, 0)(d))))
        last = []

        def pass_on(h, d):
            ref = view(h, *place(h, d, 0))
            for e in ORDER:
                last.append(send(ref, ref, axis_of(h, 1)(e)))

        for h in range(2):
            pass_on(h, 0)
        return arrivals, last, pass_on

    def gather_forward(gather):
        arrivals, _, pass_on = gather
        for h, d, copy in arrivals:
            copy.wait_recv()
            pass_on(h, d)

    def gather_end(gather):
        for copy in gather[1]:
            copy.wait_recv()

    def rider_tile(row):
        high = row.astype(bf16).astype(f32)
        index = lax.broadcasted_iota(jnp.int32, (Q, H), 0)
        return jnp.where(index == 0, high, jnp.where(index == 1, row - high, 0.0)).astype(bf16)

    def scatter_start(n, part, with_q):
        rows = 4 * H + (Q if with_q else 0)
        arrivals = []
        for d in (2, 1, 3):
            for h in range(2):
                there = turn((z, x)[h], d)
                src = part.at[h, there, pl.ds(0, rows)]
                arrivals.append(send(src, rs_r1.at[n, h, d - 1, pl.ds(0, rows)], axis_of(h, 1)(d)))
        return arrivals

    def scatter_middle(n, part, with_q, arrivals):
        rows = H + (Q if with_q else 0)
        for copy in arrivals:
            copy.wait_recv()
        last = []
        for h in range(2):
            mine = (z, x)[h]
            for c in range(4 + with_q):
                size = H if c < 4 else Q
                at = pl.ds(c * H, size)
                total = part[h, mine, at].astype(f32)
                for d in range(3):
                    total += rs_r1[n, h, d, at].astype(f32)
                if c < 4:
                    rs_s2[n, h, c, pl.ds(0, H)] = total.astype(bf16)
                else:
                    tile = rider_tile(jnp.sum(total, axis=0, keepdims=True))
                    for k in range(4):
                        rs_s2[n, h, k, pl.ds(H, Q)] = tile
        for d in (2, 1, 3):
            for h in range(2):
                there = turn((x, z)[h], d)
                src = rs_s2.at[n, h, there, pl.ds(0, rows)]
                last.append(send(src, rs_r2.at[n, h, d - 1, pl.ds(0, rows)], axis_of(h, 0)(d)))
        return last

    def scatter_end(n, with_q, last):
        for copy in last:
            copy.wait_recv()
        out, column = [], []
        for h in range(2):
            mine = (x, z)[h]
            total = rs_s2[n, h, mine, pl.ds(0, H)].astype(f32)
            for d in range(3):
                total += rs_r2[n, h, d, pl.ds(0, H)].astype(f32)
            out.append(total)
            if with_q:
                rider = rs_s2[n, h, mine, pl.ds(H, Q)].astype(f32)
                for d in range(3):
                    rider += rs_r2[n, h, d, pl.ds(H, Q)].astype(f32)
                row = jnp.sum(rider, axis=0, keepdims=True)
                column.append(jnp.broadcast_to(row, (H, H)).T)
        return jnp.concatenate(out, 0), (jnp.concatenate(column, 0) if with_q else None)

    def put_part(part, block, value):
        low = value.astype(bf16)
        for half_block in range(2):
            c = 2 * block + half_block
            cx, cz = c // 4, c % 4
            piece = low[:, half_block * W : (half_block + 1) * W]
            part[0, cz, pl.ds(cx * H, H)] = piece[:H]
            part[1, cx, pl.ds(cz * H, H)] = piece[H:]

    def put_rider(part, products):
        for h in range(2):
            row = jnp.sum(products[h * H : (h + 1) * H].T, axis=0, keepdims=True)
            tile = rider_tile(row)
            for t in range(4):
                part[h, t, pl.ds(4 * H, Q)] = tile

    def chunk(buf, c):
        return jnp.concatenate([buf[0, c // 4, c % 4, pl.ds(0, H)], buf[1, c // 4, c % 4, pl.ds(0, H)]], 0)

    def gain_row(k, c):
        return tok_g[0, c // 4, c % 4, pl.ds(H, Q)].astype(f32)[k : k + 1]

    def norm(buf, k, scale_ref, dst):
        total = jnp.zeros((T, W), f32)
        for c in range(16):
            v = chunk(buf, c).astype(f32)
            total += v * v
        scale = lax.rsqrt(jnp.sum(total, axis=1, keepdims=True) * (1.0 / D) + EPS)
        scale_ref[...] = jnp.broadcast_to(scale, (T, W))
        for c in range(16):
            v = chunk(buf, c).astype(f32)
            dst[:, c * W : (c + 1) * W] = (v * scale_ref[...] * gain_row(k, c)).astype(bf16)

    def dense(buf, dst):
        for c in range(16):
            dst[:, c * W : (c + 1) * W] = chunk(buf, c)

    def grad_start(g, rows, left, right):
        for there in range(4):
            for core_there in range(2):
                j = (there % 2) * 4 + (there // 2) * 2 + core_there
                g[core_there, there, pl.ds(0, rows)] = nn(left, right[:, j * 256 : (j + 1) * 256]).astype(bf16)

    def grad_pair(g, r):
        return send(g.at[1 - core], r, other)

    def grad_middle(g, r, into, copy):
        copy.wait_recv()
        for there in range(4):
            g[core, there] = (g[core, there].astype(f32) + r[there].astype(f32)).astype(bf16)
        return [send(g.at[core, turn(y, d)], into.at[d - 1], on_y(d)) for d in (2, 1, 3)]

    def grad_end(g, into, copies, at):
        for copy in copies:
            copy.wait_recv()
        total = g[core, y, at].astype(f32)
        for d in range(3):
            total += into[d, at].astype(f32)
        return total

    def transposed(value):
        tp[:, :C] = value
        return tp[...].T[:C]

    gain_tile = jnp.concatenate([gains[...].astype(f32), jnp.zeros((Q - 2, W), f32)], 0).astype(bf16)
    for h in range(2):
        tok_g[h, x, z, pl.ds(0, H)] = tokens[pl.ds(h * H, H)]
        cot_g[h, x, z] = cot[pl.ds(h * H, H)]
    tok_g[0, x, z, pl.ds(H, Q)] = gain_tile
    tp[...] = jnp.zeros_like(tp)
    pl.semaphore_wait(barrier, len(partners))
    tok_gather = gather_start(tok_g, (H + Q, H))
    gather_forward(tok_gather)
    cot_gather = gather_start(cot_g, (H, H))

    row = lax.broadcasted_iota(jnp.int32, (T, 1), 0)
    place_here = row + seq * T
    start, begins = 0, [0]
    for j in range(3):
        start = start + lengths[0, j]
        begins.append(start)

    def begin_at(p):
        hit = p == begins[0]
        for b in begins[1:]:
            hit = jnp.logical_or(hit, p == b)
        return hit

    fresh = [begin_at(place_here - k) for k in range(3)]
    not_reset = jnp.where(fresh[0], 0.0, 1.0)
    masks = [not_reset]
    for k in (1, 2):
        masks.append(masks[-1] * jnp.where(fresh[k], 0.0, 1.0))

    gather_end(tok_gather)
    norm(tok_g, 0, scale1, first)
    for load in loads[:2]:
        load.wait()

    value = nn(first[...], w_branch[1])
    p1[...] = value
    inner = value.astype(bf16).astype(f32)
    ext[pl.ds(8, T)] = inner
    halo_s[:, :C] = inner[T - 8 :]
    halo = send(halo_s, halo_r, on_seq(1))
    value = nn(first[...], w_branch[0])
    p0[...] = value
    act, slope = gelu_both(value)
    gel[...] = act
    dgel[...] = slope
    gather_forward(cot_gather)
    halo.wait_recv()
    ext[pl.ds(0, 8)] = halo_r[:, :C]
    total = bias[0:1] + conv_w[0:1] * ext[pl.ds(8, T)]
    for k in (1, 2, 3):
        total = total + conv_w[k : k + 1] * (masks[k - 1] * ext[pl.ds(8 - k, T)])
    conv[...] = total
    conv_low = total.astype(bf16)
    rate = jax.nn.softplus(decay[...])
    r_gate = sigmoid(nn(conv_low, gates[0, 0]) + bias[1:2])
    rr[...] = r_gate
    a = jnp.exp(-8.0 * r_gate * rate)
    aa[...] = a
    coef[...] = a * not_reset
    i_gate = sigmoid(nn(conv_low, gates[1, 0]) + bias[2:3])
    ii[...] = i_gate
    root = jnp.sqrt(1.0 - a * a + 0.001)
    qq[...] = root

    def scan(A, B, reverse):
        step = 1
        while step < T:
            for ref, v, fill in ((pad_a, A, 1.0), (pad_b, B, 0.0)):
                ref[pl.ds(H, T)] = v
                ref[pl.ds(H + T if reverse else 0, H)] = jnp.full((H, C), fill, f32)
            at = pl.ds(H + step if reverse else H - step, T)
            B = B + A * pad_b[at]
            A = A * pad_a[at]
            step *= 2
        return A, B

    A, B = scan(coef[...], root * i_gate * conv[...], False)
    through[...] = A
    local[...] = B
    car_s[0:1, :C] = A[T - 1 :]
    car_s[1:2, :C] = B[T - 1 :]
    carries = [send(car_s, car_r.at[d - 1], on_seq(d)) for d in (1, 2, 3)]
    gather_end(cot_gather)
    dense(cot_g, cot_d)
    for load in loads[2:]:
        load.wait()
    ghid[...] = nt(cot_d[...], w_down[...])
    for copy in carries:
        copy.wait_recv()

    def fold(got, own, reverse):
        carried = jnp.zeros((1, C), f32)
        for d in (3, 2, 1):
            here = (seq + d < 4) if reverse else (seq - d >= 0)
            slot = 4 - d if reverse else d
            new = got[slot - 1, 0:1, :C] * carried + got[slot - 1, 1:2, :C]
            carried = jnp.where(here, new, carried)
        return carried

    carried = fold(car_r, car_s, False)
    value = local[...] + through[...] * carried
    state[...] = value
    prev[pl.ds(8, T)] = value
    prev[7:8] = carried
    o_states[...] = value[T - 1 :]
    mixed = gel[...] * value
    mixed_low = mixed.astype(bf16)
    for j in range(8):
        put_part(part1, j, nn(mixed_low, w_out[:, j * 256 : (j + 1) * 256]))
    arrivals = scatter_start(0, part1, False)
    mixed_t = transposed(mixed).astype(bf16)
    last = scatter_middle(0, part1, False, arrivals)
    branch, _ = scatter_end(0, False, last)
    middle = tokens[...].astype(f32) + branch
    mid_own[...] = middle
    middle_low = middle.astype(bf16)
    for h in range(2):
        mid_g[h, x, z] = middle_low[h * H : (h + 1) * H]
    mid_gather = gather_start(mid_g, (H, H))
    gather_forward(mid_gather)
    gather_end(mid_gather)
    norm(mid_g, 1, scale2, second)

    pair0 = nn(second[...], w_up[0])
    pair1 = nn(second[...], w_up[1])
    act, slope = gelu_both(pair0)
    hidden = act * pair1
    gh = ghid[...]
    gp0 = slope * pair1 * gh
    gp1 = act * gh
    products = gp0 * pair0 + gp1 * pair1
    products = products[:, :W] + products[:, W : 2 * W] + products[:, 2 * W :]
    put_rider(part2, products)
    gp0_low, gp1_low = gp0.astype(bf16), gp1.astype(bf16)
    for j in range(8):
        at = slice(j * 256, (j + 1) * 256)
        put_part(part2, j, nt(gp0_low, w_up[0, at]) + nt(gp1_low, w_up[1, at]))
    arrivals = scatter_start(1, part2, True)
    hidden_low = hidden.astype(bf16)
    for j in range(8):
        put_part(part3, j, nn(hidden_low, w_down[:, j * 256 : (j + 1) * 256]))
    grad_start(g_down, F, hidden.T.astype(bf16), cot_d)
    down_pair = grad_pair(g_down, r_pair.at[:, pl.ds(0, F)])
    last = scatter_middle(1, part2, True, arrivals)
    for k, gp in ((0, gp0), (1, gp1)):
        left = gp.T.astype(bf16)
        for there in range(4):
            for core_there in range(2):
                j = (there % 2) * 4 + (there // 2) * 2 + core_there
                g_up[core_there, there, pl.ds(k * F, F)] = nn(
                    left, second[:, j * 256 : (j + 1) * 256]
                ).astype(bf16)
    up_pair = grad_pair(g_up, r_pair.at[:, pl.ds(F, 2 * F)])
    down_y = grad_middle(g_down, r_pair.at[:, pl.ds(0, F)], y_down, down_pair)

    grad_n, q = scatter_end(1, True, last)
    v = mid_own[...].astype(bf16).astype(f32)
    s = scale2[...]
    gain = gains[1:2].astype(f32)
    grad_middle_own = cot[...].astype(f32) + s * gain * grad_n - v * s * s * q * (1.0 / D)
    gmid_own[...] = grad_middle_own
    small[...] = jnp.zeros_like(small)
    small[1:2, :W] = jnp.sum(grad_n * v * s, axis=0, keepdims=True)
    low = grad_middle_own.astype(bf16)
    for h in range(2):
        gm_g[h, x, z] = low[h * H : (h + 1) * H]
    gm_gather = gather_start(gm_g, (H, H))
    up_y = grad_middle(g_up, r_pair.at[:, pl.ds(F, 2 * F)], y_up, up_pair)
    gather_forward(gm_gather)
    gather_end(gm_gather)
    out_arrivals = scatter_start(2, part3, False)
    dense(gm_g, gm_d)

    grad_mixed = nt(gm_d[...], w_out[...])
    grad_y = dgel[...] * state[...] * grad_mixed
    grad_state = gel[...] * grad_mixed
    pad_a[pl.ds(0, T)] = coef[...]
    pad_a[pl.ds(T, 8)] = jnp.ones((8, C), f32)
    A, B = scan(pad_a[pl.ds(1, T)], grad_state, True)
    rev_s[0:1, :C] = through[T - 1 :]
    rev_s[1:2, :C] = coef[0:1] * B[0:1]
    carries = [send(rev_s, rev_r.at[d - 1], on_seq(d)) for d in (1, 2, 3)]
    grad_start(g_out, C, mixed_t, gm_d)
    out_pair = grad_pair(g_out, r_pair.at[:, pl.ds(3 * F, C)])
    for copy in carries:
        copy.wait_recv()
    total = B + A * fold(rev_r, rev_s, True)
    a, r_gate, i_gate, root, cv = aa[...], rr[...], ii[...], qq[...], conv[...]
    t_i = total * i_gate
    d_log = total * prev[pl.ds(7, T)] * coef[...] - t_i * cv * (a * a / root)
    d_gate = d_log * r_gate
    small[9:10, :C] = -8.0 * sigmoid(decay[...]) * jnp.sum(d_gate, axis=0, keepdims=True)
    gpre0 = -8.0 * rate * d_gate * (1.0 - r_gate)
    direct = t_i * root
    gpre1 = direct * cv * (1.0 - i_gate)
    low0, low1 = gpre0.astype(bf16), gpre1.astype(bf16)
    small[7:8, :C] = jnp.sum(low0.astype(f32), axis=0, keepdims=True)
    small[8:9, :C] = jnp.sum(low1.astype(f32), axis=0, keepdims=True)
    grad_conv = direct + nt(low0, gates[0, 0]) + nt(low1, gates[1, 0])
    small[6:7, :C] = jnp.sum(grad_conv, axis=0, keepdims=True)
    edge = jnp.zeros((8, C), f32)
    grad_inner = jnp.zeros((T, C), f32)
    for k in range(4):
        weighted = grad_conv if k == 0 else masks[k - 1] * grad_conv
        small[2 + k : 3 + k, :C] = jnp.sum(weighted * ext[pl.ds(8 - k, T)], axis=0, keepdims=True)
        if k == 0:
            pad_a[pl.ds(0, 8)] = jnp.zeros((8, C), f32)
            pad_a[pl.ds(8 + T, 8)] = jnp.zeros((8, C), f32)
        pad_a[pl.ds(8, T)] = conv_w[k : k + 1] * weighted
        edge += pad_a[pl.ds(k, 8)]
        grad_inner += pad_a[pl.ds(8 + k, T)]
    back_s[:, :C] = edge
    back = send(back_s, back_r, on_seq(-1))
    cv_t = transposed(cv).astype(bf16)
    gg[0, :, :C] = nn(cv_t, low0).astype(bf16)
    gg[1, :, :C] = nn(cv_t, low1).astype(bf16)
    gg_pair = send(gg.at[1 - core], gg_r, other)
    out_last = scatter_middle(2, part3, False, out_arrivals)
    out_y = grad_middle(g_out, r_pair.at[:, pl.ds(3 * F, C)], y_out, out_pair)
    gy_t = transposed(grad_y).astype(bf16)
    grad_start(g_branch.at[0], C, gy_t, first)
    back.wait_recv()
    ext[pl.ds(0, T)] = grad_inner
    ext[pl.ds(T - 8, 8)] = grad_inner[T - 8 :] + back_r[:, :C]
    grad_inner = ext[pl.ds(0, T)]
    gpr0, gpr1 = grad_y.astype(bf16), grad_inner.astype(bf16)
    tp[:, :C] = grad_y * p0[...] + grad_inner * p1[...]
    put_rider(part4, tp[:, :W] + tp[:, W:])
    for j in range(8):
        at = slice(j * 256, (j + 1) * 256)
        put_part(part4, j, nt(gpr0, w_branch[0, at]) + nt(gpr1, w_branch[1, at]))
    arrivals = scatter_start(3, part4, True)
    gi_t = transposed(grad_inner).astype(bf16)
    grad_start(g_branch.at[1], C, gi_t, first)
    b0_pair = send(g_branch.at[0, 1 - core], r_pair.at[:, pl.ds(3 * F + C, C)], other)
    b1_pair = send(g_branch.at[1, 1 - core], r_pair.at[:, pl.ds(3 * F + 2 * C, C)], other)
    gg_pair.wait_recv()
    gg_y[y] = (gg[core].astype(f32) + gg_r[...].astype(f32)).astype(bf16)
    gg_copies = [send(gg_y.at[y], gg_y.at[y], on_y(d)) for d in (2, 1, 3)]
    last = scatter_middle(3, part4, True, arrivals)
    b0_y = grad_middle(g_branch.at[0], r_pair.at[:, pl.ds(3 * F + C, C)], y_branch.at[0], b0_pair)
    b1_y = grad_middle(g_branch.at[1], r_pair.at[:, pl.ds(3 * F + 2 * C, C)], y_branch.at[1], b1_pair)
    result, _ = scatter_end(2, False, out_last)
    o_block[...] = (mid_own[...] + result).astype(bf16)
    o_down[...] = grad_end(g_down, y_down, down_y, pl.ds(0, F))
    for k in range(2):
        total = grad_end(g_up, y_up, up_y if k == 0 else (), pl.ds(k * F, F))
        o_up[k] = total.T
    o_out[...] = grad_end(g_out, y_out, out_y, pl.ds(0, C))
    for copy in gg_copies:
        copy.wait_recv()
    total = gg_y[0].astype(f32) + gg_y[1].astype(f32) + gg_y[2].astype(f32) + gg_y[3].astype(f32)
    gg_f[core] = total
    gg_share = send(gg_f.at[core], gg_f.at[core], other)

    grad_n, q = scatter_end(3, True, last)
    v = tokens[...].astype(f32)
    s = scale1[...]
    gain = gains[0:1].astype(f32)
    o_tokens[...] = gmid_own[...] + s * gain * grad_n - v * s * s * q * (1.0 / D)
    small[0:1, :W] = jnp.sum(grad_n * v * s, axis=0, keepdims=True)
    small_pair = send(small, small_r, other)
    for k, copies in ((0, b0_y), (1, b1_y)):
        tp[pl.ds(0, C)] = grad_end(g_branch.at[k], y_branch.at[k], copies, pl.ds(0, C))
        o_branch[k] = tp[...].T[:, :C]
    small_pair.wait_recv()
    small_y[y] = small[...] + small_r[...]
    small_copies = [send(small_y.at[y], small_y.at[y], on_y(d)) for d in (2, 1, 3)]
    gg_share.wait_recv()
    for k in range(2):
        o_gates[k, 0] = gg_f[k, :, :C]
    for copy in small_copies:
        copy.wait_recv()
    total = small_y[0] + small_y[1] + small_y[2] + small_y[3]
    o_gains[...] = total[0:2, :W]
    o_conv[...] = total[2:6, :C]
    o_bias[...] = total[6:9, :C]
    o_decay[...] = total[9:10, :C]
    for copy in sent:
        copy.wait_send()


def on_device(
    tokens, doc_lengths, cotangent, norm_gains, w_branch, conv_weight, lru_bias, decay, gate_weights, w_out, w_up, w_down
):
    def shape(dims, kind=f32):
        return jax.ShapeDtypeStruct(dims, kind)

    def vmem(*dims, kind=f32):
        return pltpu.VMEM(dims, kind)

    def low(*dims):
        return pltpu.VMEM(dims, bf16)

    near, far = pl.BlockSpec(memory_space=pltpu.VMEM), pl.BlockSpec(memory_space=pl.ANY)
    rows = 3 * F + 3 * C
    scratch = (
        [low(2, D, C), low(2, 1, C, C), low(C, D), low(2, D, F), low(F, D)]
        + [low(2, 4, 4, H + Q, W)] + [low(2, 4, 4, H, W)] * 3 + [low(T, D)] * 4
        + [low(2, 4, 4 * H + Q, W)] * 4
        + [low(4, 2, 3, 4 * H + Q, W), low(4, 2, 4, H + Q, W), low(4, 2, 3, H + Q, W)]
        + [vmem(T + 8, C)] + [vmem(T, C)] * 13 + [vmem(T + 8, C), vmem(2 * H + T, C), vmem(2 * H + T, C), vmem(T, T)]
        + [vmem(8, W), vmem(T, F), vmem(T, W), vmem(T, W), vmem(T, W), vmem(T, W)]
        + [low(2, 4, F, 256), low(2, 4, 2 * F, 256), low(2, 4, C, 256), low(2, 2, 4, C, 256)]
        + [low(3, F, 256), low(3, 2 * F, 256), low(3, C, 256), low(2, 3, C, 256), low(4, rows, 256)]
        + [vmem(8, 256)] * 4 + [vmem(8, 256), vmem(3, 8, 256)] * 2
        + [low(2, C, 256), low(C, 256), low(4, C, 256), vmem(2, C, 256)]
        + [vmem(16, 256), vmem(16, 256), vmem(4, 16, 256)]
        + [pltpu.SemaphoreType.DMA((N_SEMS,)), pltpu.SemaphoreType.DMA((N_SEMS,)), pltpu.SemaphoreType.DMA((8,))]
    )
    outs = pl.pallas_call(
        kernel,
        out_shape=[
            shape((T, W), bf16), shape((T, W)), shape((2, W)), shape((2, 256, C)), shape((4, C)), shape((3, C)),
            shape((1, C)), shape((2, 1, C, C)), shape((C, 256)), shape((2, 256, F)), shape((F, 256)), shape((1, C)),
        ],
        in_specs=[near, pl.BlockSpec(memory_space=pltpu.SMEM)] + [near] * 5 + [far] * 5,
        out_specs=[near] * 12,
        scratch_shapes=scratch,
        compiler_params=pltpu.CompilerParams(
            collective_id=0, has_side_effects=True, vmem_limit_bytes=62 * 2**20
        ),
    )(
        tokens.reshape(T, W), doc_lengths, cotangent.reshape(T, W), norm_gains, conv_weight, lru_bias,
        decay.reshape(1, C), w_branch, gate_weights, w_out, w_up, w_down,
    )
    outs = list(outs)
    outs[0], outs[1] = outs[0].reshape(1, T, W), outs[1].reshape(1, T, W)
    outs[6], outs[11] = outs[6].reshape(C), outs[11].reshape(1, 1, C)
    return tuple(outs)


def solution(mesh):
    in_specs = (
        P("dp", "seq", "mp"), P("dp", None), P("dp", "seq", "mp"), P(None, "mp"), P(None, None, "mp"), P(None, "mp"),
        P(None, "mp"), P("mp"), P(None, "mp", None, None), P("mp", None), P(None, None, "mp"), P("mp", None),
    )
    out_specs = (
        P("dp", "seq", "mp"), P("dp", "seq", "mp"), P(None, "mp"), P(None, ("dp", "seq"), "mp"), P(None, "mp"),
        P(None, "mp"), P("mp"), P(None, "mp", None, None), P("mp", ("dp", "seq")), P(None, ("dp", "seq"), "mp"),
        P("mp", ("dp", "seq")), P("dp", "seq", "mp"),
    )
    return jax.shard_map(on_device, mesh=mesh, in_specs=in_specs, out_specs=out_specs, check_vma=False)
```

```python
import jax
import jax.numpy as jnp
from jax import lax
from jax.experimental import pallas as pl
from jax.experimental.pallas import tpu as pltpu
from jax.sharding import PartitionSpec as P

MESH = pl.DeviceIdType.MESH
f32, bf16 = jnp.float32, jnp.bfloat16

T, D, C, F, W = 256, 2048, 176, 384, 128
H = T // 2
EPS = 1e-06
N_SEMS, N_SENT = 104, 24
Q = 16
ALPHA, CUBIC = 0.7978845608028654, 0.044715
FAR_FIRST = (2, 1, 3)


def nn(a, b):
    return lax.dot_general(a, b, (((1,), (0,)), ((), ())), preferred_element_type=f32)


def nt(a, b):
    return lax.dot_general(a, b, (((1,), (1,)), ((), ())), preferred_element_type=f32)


def sigmoid(v):
    return 1.0 / (1.0 + jnp.exp(-v))


def gelu_both(v):
    square = v * v
    t = jnp.tanh(ALPHA * v * (1.0 + CUBIC * square))
    half = 0.5 * (1.0 + t)
    return v * half, half + 0.5 * v * (1.0 - t * t) * ALPHA * (1.0 + 3.0 * CUBIC * square)


def rider_tile(row):
    high = row.astype(bf16).astype(f32)
    index = lax.broadcasted_iota(jnp.int32, (Q, H), 0)
    return jnp.where(index == 0, high, jnp.where(index == 1, row - high, 0.0)).astype(bf16)


def kernel(
    lengths, gains, conv_w, bias, decay, hbm_tokens, hbm_cot, hbm_branch, hbm_gates, hbm_out, hbm_up, hbm_down,
    h_block, h_tokens, h_gains, h_branch, h_conv, h_bias, h_decay, h_gates, h_out, h_up, h_down, h_states,
    tokens, cot, w_branch, gates, w_out, w_up, w_down,
    o_block, o_tokens, o_gains, o_branch, o_conv, o_bias, o_decay, o_gates, o_out, o_up, o_down, o_states,
    tok_g, cot_g, mid_g, gm_g, first, second, cot_d, gm_d,
    part1, part2, part3, part4, rs_r1, rs_s2, rs_r2,
    ext, conv, aa, rr, ii, qq, coef, through, local, p0, p1, gel, dgel, state, prev, pad_a, pad_b, tp,
    ghid, mid_own, gmid_own, scale1, scale2,
    g_mlp, r_mlp, relay_mlp, y_mlp, g_rec, r_rec, relay_rec, y_rec,
    halo_s, halo_r, back_s, back_r, car_s, car_r, rev_s, rev_r,
    gg, gg_r, gg_y, gg_f, small, ruler,
    send_sems, recv_sems, copy_sems,
):
    me, seq, dp = lax.axis_index("mp"), lax.axis_index("seq"), lax.axis_index("dp")
    x, z = me // 4, me % 4
    core, y = seq % 2, (seq // 2) * 2 + dp

    def turn(value, by):
        return lax.rem(value + by + 4, 4)

    def on_x(d):
        return {"mp": turn(x, d) * 4 + z}

    def on_z(d):
        return {"mp": x * 4 + turn(z, d)}

    def on_y(d, same=True):
        there = turn(y, d)
        return {"dp": there % 2, "seq": (there // 2) * 2 + (core if same else 1 - core)}

    def on_seq(d):
        return {"seq": turn(seq, d)}

    other = on_y(0, False)

    groups, sources, stores = [], [], []

    def wait_bytes(sem, size):
        ref = ruler.at[pl.ds(0, size // (4 * W))]
        pltpu.make_async_copy(ref, ref, sem).wait()

    class Group:
        def __init__(self, kin=groups):
            self.i, self.size, self.done = len(kin), 0, False
            kin.append(self)

        def wait(self):
            if not self.done:
                self.done = True
                wait_bytes(recv_sems.at[self.i], self.size)

    def send(src, dst, where, group, source):
        size = src.dtype.itemsize
        for dim in src.shape:
            size *= dim
        group.size += size
        source.size += size
        pltpu.make_async_remote_copy(
            src_ref=src, dst_ref=dst, send_sem=send_sems.at[source.i], recv_sem=recv_sems.at[group.i],
            device_id=where, device_id_type=MESH,
        ).start()

    def send_one(src, dst, where):
        group = Group()
        send(src, dst, where, group, misc)
        return group

    misc = Group(sources)

    barrier = pltpu.get_barrier_semaphore()
    partners = [on_x(d) for d in (1, 2, 3)] + [on_z(d) for d in (1, 2, 3)] + [on_y(d) for d in (1, 2, 3)]
    partners += [on_y(d, False) for d in (0, 1, 2, 3)]
    for where in partners:
        pl.semaphore_signal(barrier, inc=1, device_id=where, device_id_type=MESH)

    loads = []

    def load(src, dst):
        copy = pltpu.make_async_copy(src, dst, copy_sems.at[len(loads)])
        copy.start()
        loads.append(copy)
        return copy

    def store(src, dst):
        copy = pltpu.make_async_copy(src, dst, copy_sems.at[16 + len(stores)])
        copy.start()
        stores.append(copy)

    load_tokens, load_cot = load(hbm_tokens, tokens), load(hbm_cot, cot)
    load_branch, load_gates, load_out = load(hbm_branch, w_branch), load(hbm_gates, gates), load(hbm_out, w_out)
    load_down, load_up = load(hbm_down, w_down), load(hbm_up, w_up)

    def finish():
        for group in groups:
            group.wait()
        for copy in stores:
            copy.wait()
        for source in sources:
            wait_bytes(send_sems.at[source.i], source.size)

    def axis_of(h, phase):
        return (on_x, on_z)[(h + phase) % 2]

    def place(h, first_hop, second_hop):
        return (turn(x, first_hop), turn(z, second_hop)) if h == 0 else (turn(x, second_hop), turn(z, first_hop))

    class Gather:
        def __init__(self, buf, rows):
            self.buf, self.rows = buf, rows
            self.arrivals, self.source = [], Group(sources)
            for d in (1, 3, 2):
                for h in range(2):
                    ref, group = self.view(h, x, z), Group()
                    send(ref, ref, axis_of(h, 0)(d), group, self.source)
                    self.arrivals.append((h, d, group))
            self.last = Group()
            for h in range(2):
                self.pass_on(h, 0)

        def view(self, h, cx, cz):
            return self.buf.at[h, cx, cz, pl.ds(0, self.rows[h])]

        def pass_on(self, h, d):
            ref = self.view(h, *place(h, -d, 0))
            for e in (1, 3, 2):
                send(ref, ref, axis_of(h, 1)(e), self.last, self.source)

        def forward(self):
            for h, d, group in self.arrivals:
                group.wait()
                self.pass_on(h, d)

        def end(self):
            self.last.wait()

    class Scatter:
        def __init__(self, n, part, rider):
            self.n, self.part, self.rider = n, part, rider
            self.source = Group(sources)
            self.hop1 = {(h, r): Group() for h in range(2) for r in range(4)}
            self.hop2 = [Group(), Group()]

        def rows(self, r):
            return pl.ds(0, H + Q if self.rider and r == 2 else H)

        def launch(self, g):
            n, part = self.n, self.part
            for d in FAR_FIRST:
                at = self.rows(g)
                src = part.at[0, turn(x, g), turn(z, d), at]
                send(src, rs_r1.at[n, 0, g, d - 1, at], on_z(d), self.hop1[0, g], self.source)
            if g:
                for r in FAR_FIRST + (0,):
                    at = self.rows(r)
                    src = part.at[1, turn(x, g), turn(z, r), at]
                    send(src, rs_r1.at[n, 1, r, g - 1, at], on_x(g), self.hop1[1, r], self.source)

        def produce(self, columns):
            for g in FAR_FIRST + (0,):
                there = turn(x, g)
                low = columns(pl.multiple_of(there * 512, 512)).astype(bf16)
                for c in range(4):
                    piece = low[:, c * W : (c + 1) * W]
                    self.part[0, there, c, pl.ds(0, H)] = piece[:H]
                    self.part[1, there, c, pl.ds(0, H)] = piece[H:]
                self.launch(g)

        def ride(self, products):
            for h in range(2):
                tile = rider_tile(jnp.sum(products[h * H : (h + 1) * H].T, axis=0, keepdims=True))
                if h == 0:
                    for c in range(4):
                        self.part[0, turn(x, 2), c, pl.ds(H, Q)] = tile
                else:
                    for c in range(4):
                        self.part[1, c, turn(z, 2), pl.ds(H, Q)] = tile

        def middle(self):
            n, part = self.n, self.part
            self.own, self.row = {}, {}
            for h, r in ((0, 2), (0, 1), (1, 2), (0, 3), (1, 1), (1, 3), (0, 0), (1, 0)):
                self.hop1[h, r].wait()
                spot = (turn(x, r), z) if h == 0 else (x, turn(z, r))
                total = part[h, *spot, pl.ds(0, H)].astype(f32)
                for d in range(3):
                    total += rs_r1[n, h, r, d, pl.ds(0, H)].astype(f32)
                if self.rider and r == 2:
                    rider = part[h, *spot, pl.ds(H, Q)].astype(f32)
                    for d in range(3):
                        rider += rs_r1[n, h, r, d, pl.ds(H, Q)].astype(f32)
                    self.row[h] = jnp.sum(rider, axis=0, keepdims=True)
                    tile = rider_tile(self.row[h])
                    for k in range(3):
                        rs_s2[n, h, k, pl.ds(H, Q)] = tile
                if r:
                    rs_s2[n, h, r - 1, pl.ds(0, H)] = total.astype(bf16)
                    at = pl.ds(0, H + Q if self.rider else H)
                    where = axis_of(h, 0)(r)
                    send(rs_s2.at[n, h, r - 1, at], rs_r2.at[n, h, r - 1, at], where, self.hop2[h], self.source)
                else:
                    self.own[h] = total

        def end(self):
            n, out, column = self.n, [], []
            for h in range(2):
                total, row = self.own[h], self.row.get(h)
                self.hop2[h].wait()
                for r in (1, 3, 2):
                    total += rs_r2[n, h, r - 1, pl.ds(0, H)].astype(f32)
                    if self.rider:
                        row += jnp.sum(rs_r2[n, h, r - 1, pl.ds(H, Q)].astype(f32), axis=0, keepdims=True)
                out.append(total)
                if self.rider:
                    column.append(jnp.broadcast_to(row, (H, H)).T)
            return jnp.concatenate(out, 0), (jnp.concatenate(column, 0) if self.rider else None)

    def chunk(buf, c):
        return jnp.concatenate([buf[0, c // 4, c % 4, pl.ds(0, H)], buf[1, c // 4, c % 4, pl.ds(0, H)]], 0)

    def gain_row(k, c):
        return tok_g[0, c // 4, c % 4, pl.ds(H, Q)].astype(f32)[k : k + 1]

    def norm(buf, k, scale_ref, dst):
        total = jnp.zeros((T, W), f32)
        for c in range(16):
            v = chunk(buf, c).astype(f32)
            total += v * v
        scale = lax.rsqrt(jnp.sum(total, axis=1, keepdims=True) * (1.0 / D) + EPS)
        scale_ref[...] = jnp.broadcast_to(scale, (T, W))
        for c in range(16):
            v = chunk(buf, c).astype(f32)
            dst[:, c * W : (c + 1) * W] = (v * scale_ref[...] * gain_row(k, c)).astype(bf16)

    def dense(buf, dst):
        for c in range(16):
            dst[:, c * W : (c + 1) * W] = chunk(buf, c)

    class WeightGrad:
        def __init__(self, g, r, relay, into, rows):
            self.g, self.r, self.relay, self.into, self.rows = g, r, relay, into, rows
            cut = rows // 32 * 16 + (16 if rows % 32 else 0)
            self.a, self.b = pl.ds(0, cut), pl.ds(cut, rows - cut)

        def compute(self, left, right):
            for there in range(4):
                for core_there in range(2):
                    j = (there % 2) * 4 + (there // 2) * 2 + core_there
                    self.g[core_there, there] = nn(left, right[:, j * 256 : (j + 1) * 256]).astype(bf16)

        def start(self):
            self.source = Group(sources)
            self.pair = Group()
            send(self.g.at[1 - core], self.r, other, self.pair, self.source)

        def add(self, there, at, other_part):
            g = self.g
            g[core, there, at] = (g[core, there, at].astype(f32) + other_part.astype(f32)).astype(bf16)

        def middle(self):
            self.pair.wait()
            g, a, b = self.g, self.a, self.b
            self.relayed, self.last = Group(), Group()
            far = turn(y, 2)
            self.add(far, pl.ds(0, self.rows), self.r[far])
            send(g.at[core, far, a], self.relay.at[a], on_y(1), self.relayed, self.source)
            send(g.at[core, far, b], self.relay.at[b], on_y(-1), self.relayed, self.source)
            for k, at in ((1, b), (-1, a)):
                there = turn(y, k)
                self.add(there, pl.ds(0, self.rows), self.r[there])
                send(g.at[core, there, at], self.into.at[(1 - k) // 2, at], on_y(k), self.last, self.source)
            self.add(y, pl.ds(0, self.rows), self.r[y])

        def pass_on(self):
            self.relayed.wait()
            for k, at in ((1, self.a), (-1, self.b)):
                there = turn(y, k)
                self.add(there, at, self.relay[at])
                send(self.g.at[core, there, at], self.into.at[(1 - k) // 2, at], on_y(k), self.last, self.source)

        def end(self):
            self.last.wait()
            return self.g[core, y].astype(f32) + self.into[0].astype(f32) + self.into[1].astype(f32)

    def transposed(value):
        tp[:, :C] = value
        return tp[...].T[:C]

    def weight_grad(i, rows):
        refs = (g_mlp, r_mlp, relay_mlp, y_mlp) if rows == F else (g_rec, r_rec, relay_rec, y_rec)
        return WeightGrad(*[ref.at[i] for ref in refs], rows)

    down, up = weight_grad(0, F), [weight_grad(1, F), weight_grad(2, F)]
    out, branches = weight_grad(0, C), [weight_grad(1, C), weight_grad(2, C)]

    gain_tile = jnp.concatenate([gains[...].astype(f32), jnp.zeros((Q - 2, W), f32)], 0).astype(bf16)
    tok_g[0, x, z, pl.ds(H, Q)] = gain_tile
    load_tokens.wait()
    load_cot.wait()
    for h in range(2):
        tok_g[h, x, z, pl.ds(0, H)] = tokens[pl.ds(h * H, H)]
        cot_g[h, x, z] = cot[pl.ds(h * H, H)]
    tp[...] = jnp.zeros_like(tp)
    pl.semaphore_wait(barrier, len(partners))
    tok_gather = Gather(tok_g, (H + Q, H))
    tok_gather.forward()
    cot_gather = Gather(cot_g, (H, H))

    place_here = lax.broadcasted_iota(jnp.int32, (T, 1), 0) + seq * T
    start, begins = 0, [0]
    for j in range(3):
        start = start + lengths[0, j]
        begins.append(start)

    def begin_at(p):
        hit = p == begins[0]
        for b in begins[1:]:
            hit = jnp.logical_or(hit, p == b)
        return hit

    not_reset = jnp.where(begin_at(place_here), 0.0, 1.0)
    masks = [not_reset]
    for k in (1, 2):
        masks.append(masks[-1] * jnp.where(begin_at(place_here - k), 0.0, 1.0))

    tok_gather.end()
    norm(tok_g, 0, scale1, first)
    load_branch.wait()
    load_gates.wait()

    value = nt(first[...], w_branch[1])
    p1[...] = value
    inner = value.astype(bf16).astype(f32)
    ext[pl.ds(8, T)] = inner
    halo_s[:, :C] = inner[T - 8 :]
    halo = send_one(halo_s, halo_r, on_seq(1))
    value = nt(first[...], w_branch[0])
    p0[...] = value
    act, slope = gelu_both(value)
    gel[...] = act
    dgel[...] = slope
    cot_gather.forward()
    halo.wait()
    ext[pl.ds(0, 8)] = halo_r[:, :C]
    total = bias[0:1] + conv_w[0:1] * ext[pl.ds(8, T)]
    for k in (1, 2, 3):
        total = total + conv_w[k : k + 1] * (masks[k - 1] * ext[pl.ds(8 - k, T)])
    conv[...] = total
    conv_low = total.astype(bf16)
    rate = jax.nn.softplus(decay[...])
    r_gate = sigmoid(nn(conv_low, gates[0, 0]) + bias[1:2])
    rr[...] = r_gate
    a = jnp.exp(-8.0 * r_gate * rate)
    aa[...] = a
    coef[...] = a * not_reset
    i_gate = sigmoid(nn(conv_low, gates[1, 0]) + bias[2:3])
    ii[...] = i_gate
    root = jnp.sqrt(1.0 - a * a + 0.001)
    qq[...] = root

    def scan(A, B, reverse):
        step = 1
        while step < T:
            for ref, v, fill in ((pad_a, A, 1.0), (pad_b, B, 0.0)):
                ref[pl.ds(H, T)] = v
                ref[pl.ds(H + T if reverse else 0, H)] = jnp.full((H, C), fill, f32)
            at = pl.ds(H + step if reverse else H - step, T)
            B = B + A * pad_b[at]
            A = A * pad_a[at]
            step *= 2
        return A, B

    A, B = scan(coef[...], root * i_gate * conv[...], False)
    through[...] = A
    local[...] = B
    car_s[0:1, :C] = A[T - 1 :]
    car_s[1:2, :C] = B[T - 1 :]
    carries = Group()
    for d in (2, 1, 3):
        send(car_s, car_r.at[d - 1], on_seq(d), carries, misc)
    cot_gather.end()
    dense(cot_g, cot_d)
    load_out.wait()
    load_down.wait()
    load_up.wait()
    ghid[...] = nt(cot_d[...], w_down[...])
    carries.wait()

    def fold(got, reverse):
        carried = jnp.zeros((1, C), f32)
        for d in (3, 2, 1):
            here = (seq + d < 4) if reverse else (seq - d >= 0)
            slot = 4 - d if reverse else d
            new = got[slot - 1, 0:1, :C] * carried + got[slot - 1, 1:2, :C]
            carried = jnp.where(here, new, carried)
        return carried

    carried = fold(car_r, False)
    value = local[...] + through[...] * carried
    state[...] = value
    prev[pl.ds(8, T)] = value
    prev[7:8] = carried
    mixed = gel[...] * value
    mixed_low = mixed.astype(bf16)
    scatter = Scatter(0, part1, False)
    scatter.produce(lambda at: nn(mixed_low, w_out[:, pl.ds(at, 512)]))
    o_states[...] = value[T - 1 :]
    store(o_states, h_states)
    mixed_t = transposed(mixed).astype(bf16)
    scatter.middle()
    branch, _ = scatter.end()
    middle = tokens[...].astype(f32) + branch
    mid_own[...] = middle
    middle_low = middle.astype(bf16)
    for h in range(2):
        mid_g[h, x, z] = middle_low[h * H : (h + 1) * H]
    gather = Gather(mid_g, (H, H))
    gather.forward()
    gather.end()
    norm(mid_g, 1, scale2, second)

    pair0 = nn(second[...], w_up[0])
    pair1 = nn(second[...], w_up[1])
    act, slope = gelu_both(pair0)
    hidden = act * pair1
    gh = ghid[...]
    gp0 = slope * pair1 * gh
    gp1 = act * gh
    products = gp0 * pair0 + gp1 * pair1
    products = products[:, :W] + products[:, W : 2 * W] + products[:, 2 * W :]
    gp0_low, gp1_low = gp0.astype(bf16), gp1.astype(bf16)
    scatter = Scatter(1, part2, True)
    scatter.ride(products)
    scatter.produce(lambda at: nt(gp0_low, w_up[0, pl.ds(at, 512)]) + nt(gp1_low, w_up[1, pl.ds(at, 512)]))
    down.compute(hidden.T.astype(bf16), cot_d)
    down.start()
    up[0].compute(gp0.T.astype(bf16), second)
    up[0].start()
    down.middle()
    scatter.middle()
    up[1].compute(gp1.T.astype(bf16), second)
    up[1].start()
    up[0].middle()

    grad_n, q = scatter.end()
    v = mid_own[...].astype(bf16).astype(f32)
    s = scale2[...]
    gain = gains[1:2].astype(f32)
    grad_middle_own = cot[...].astype(f32) + s * gain * grad_n - v * s * s * q * (1.0 / D)
    gmid_own[...] = grad_middle_own
    low = grad_middle_own.astype(bf16)
    for h in range(2):
        gm_g[h, x, z] = low[h * H : (h + 1) * H]
    gather = Gather(gm_g, (H, H))
    mine = small.at[dp * 4 + seq]
    mine[...] = jnp.zeros((16, 256), f32)
    mine[1:2, :W] = jnp.sum(grad_n * v * s, axis=0, keepdims=True)
    gather.forward()
    down.pass_on()
    up[1].middle()
    up[0].pass_on()
    hidden_low = hidden.astype(bf16)
    gather.end()
    dense(gm_g, gm_d)

    grad_mixed = nt(gm_d[...], w_out[...])
    grad_y = dgel[...] * state[...] * grad_mixed
    grad_state = gel[...] * grad_mixed
    pad_a[pl.ds(0, T)] = coef[...]
    pad_a[pl.ds(T, 8)] = jnp.ones((8, C), f32)
    A, B = scan(pad_a[pl.ds(1, T)], grad_state, True)
    rev_s[0:1, :C] = through[T - 1 :]
    rev_s[1:2, :C] = coef[0:1] * B[0:1]
    carries = Group()
    for d in (2, 1, 3):
        send(rev_s, rev_r.at[d - 1], on_seq(d), carries, misc)
    scatter_out = Scatter(2, part3, False)
    scatter_out.produce(lambda at: nn(hidden_low, w_down[:, pl.ds(at, 512)]))
    out.compute(mixed_t, gm_d)
    out.start()
    carries.wait()
    total = B + A * fold(rev_r, True)
    a, r_gate, i_gate, root, cv = aa[...], rr[...], ii[...], qq[...], conv[...]
    t_i = total * i_gate
    d_log = total * prev[pl.ds(7, T)] * coef[...] - t_i * cv * (a * a / root)
    d_gate = d_log * r_gate
    mine[9:10, :C] = -8.0 * sigmoid(decay[...]) * jnp.sum(d_gate, axis=0, keepdims=True)
    gpre0 = -8.0 * rate * d_gate * (1.0 - r_gate)
    direct = t_i * root
    gpre1 = direct * cv * (1.0 - i_gate)
    low0, low1 = gpre0.astype(bf16), gpre1.astype(bf16)
    mine[7:8, :C] = jnp.sum(low0.astype(f32), axis=0, keepdims=True)
    mine[8:9, :C] = jnp.sum(low1.astype(f32), axis=0, keepdims=True)
    grad_conv = direct + nt(low0, gates[0, 0]) + nt(low1, gates[1, 0])
    mine[6:7, :C] = jnp.sum(grad_conv, axis=0, keepdims=True)
    edge = jnp.zeros((8, C), f32)
    grad_inner = jnp.zeros((T, C), f32)
    for k in range(4):
        weighted = grad_conv if k == 0 else masks[k - 1] * grad_conv
        mine[2 + k : 3 + k, :C] = jnp.sum(weighted * ext[pl.ds(8 - k, T)], axis=0, keepdims=True)
        if k == 0:
            pad_a[pl.ds(0, 8)] = jnp.zeros((8, C), f32)
            pad_a[pl.ds(8 + T, 8)] = jnp.zeros((8, C), f32)
        pad_a[pl.ds(8, T)] = conv_w[k : k + 1] * weighted
        edge += pad_a[pl.ds(k, 8)]
        grad_inner += pad_a[pl.ds(8 + k, T)]
    back_s[:, :C] = edge
    back = send_one(back_s, back_r, on_seq(-1))
    cv_t = transposed(cv).astype(bf16)
    gg[0, :, :C] = nn(cv_t, low0).astype(bf16)
    gg[1, :, :C] = nn(cv_t, low1).astype(bf16)
    gg_pair = send_one(gg.at[1 - core], gg_r, other)
    up[1].pass_on()
    scatter_out.middle()
    out.middle()
    branches[0].compute(transposed(grad_y).astype(bf16), first)
    branches[0].start()
    back.wait()
    ext[pl.ds(0, T)] = grad_inner
    ext[pl.ds(T - 8, 8)] = grad_inner[T - 8 :] + back_r[:, :C]
    grad_inner = ext[pl.ds(0, T)]
    gpr0, gpr1 = grad_y.astype(bf16), grad_inner.astype(bf16)
    tp[:, :C] = grad_y * p0[...] + grad_inner * p1[...]
    scatter = Scatter(3, part4, True)
    scatter.ride(tp[:, :W] + tp[:, W:])
    scatter.produce(lambda at: nn(gpr0, w_branch[0, :, pl.ds(at, 512)]) + nn(gpr1, w_branch[1, :, pl.ds(at, 512)]))
    branches[1].compute(transposed(grad_inner).astype(bf16), first)
    branches[1].start()
    branches[0].middle()
    gg_pair.wait()
    gg_y[y] = (gg[core].astype(f32) + gg_r[...].astype(f32)).astype(bf16)
    gg_all = Group()
    for d in FAR_FIRST:
        send(gg_y.at[y], gg_y.at[y], on_y(d), gg_all, misc)
    out.pass_on()
    scatter.middle()
    branches[1].middle()
    branches[0].pass_on()
    result, _ = scatter_out.end()
    o_block[...] = (mid_own[...] + result).astype(bf16)
    store(o_block, h_block)
    o_down[...] = down.end()
    store(o_down, h_down)
    for k in range(2):
        o_up[k] = up[k].end().T
    store(o_up, h_up)
    branches[1].pass_on()
    o_out[...] = out.end()
    store(o_out, h_out)
    gg_all.wait()
    gg_f[core] = gg_y[0].astype(f32) + gg_y[1].astype(f32) + gg_y[2].astype(f32) + gg_y[3].astype(f32)
    gg_share = send_one(gg_f.at[core], gg_f.at[core], other)

    grad_n, q = scatter.end()
    v = tokens[...].astype(f32)
    s = scale1[...]
    gain = gains[0:1].astype(f32)
    mine[0:1, :W] = jnp.sum(grad_n * v * s, axis=0, keepdims=True)
    smalls = Group()
    for d, same in ((2, False), (2, True), (1, False), (1, True), (3, False), (3, True), (0, False)):
        send(mine, mine, on_y(d, same), smalls, misc)
    o_tokens[...] = gmid_own[...] + s * gain * grad_n - v * s * s * q * (1.0 / D)
    store(o_tokens, h_tokens)
    for k in range(2):
        o_branch[k] = branches[k].end()
    store(o_branch, h_branch)
    gg_share.wait()
    for k in range(2):
        o_gates[k, 0] = gg_f[k, :, :C]
    store(o_gates, h_gates)
    smalls.wait()
    total = small[0]
    for j in range(1, 8):
        total += small[j]
    o_gains[...] = total[0:2, :W]
    o_conv[...] = total[2:6, :C]
    o_bias[...] = total[6:9, :C]
    o_decay[...] = total[9:10, :C]
    for src, dst in ((o_gains, h_gains), (o_conv, h_conv), (o_bias, h_bias), (o_decay, h_decay)):
        store(src, dst)
    finish()


def hand_over(*refs):
    n = 12
    ins, outs, held, (in_sems, out_sems) = refs[:n], refs[n : 2 * n], refs[2 * n : 3 * n], refs[3 * n :]
    copies = [pltpu.make_async_copy(ins[i], held[i], in_sems.at[i]) for i in range(n)]
    for copy in copies:
        copy.start()
    stores = []
    for i in range(n):
        copies[i].wait()
        stores.append(pltpu.make_async_copy(held[i], outs[i], out_sems.at[i]))
        stores[i].start()
    for copy in stores:
        copy.wait()


def on_device(
    tokens, doc_lengths, cotangent, norm_gains, w_branch, conv_weight, lru_bias, decay, gate_weights, w_out, w_up, w_down
):
    def shape(dims, kind=f32):
        return jax.ShapeDtypeStruct(dims, kind)

    def vmem(*dims):
        return pltpu.VMEM(dims, f32)

    def low(*dims):
        return pltpu.VMEM(dims, bf16)

    near, far = pl.BlockSpec(memory_space=pltpu.VMEM), pl.BlockSpec(memory_space=pl.ANY)
    outs = [
        shape((T, W), bf16), shape((T, W)), shape((2, W)), shape((2, C, 256)), shape((4, C)), shape((3, C)),
        shape((1, C)), shape((2, 1, C, C)), shape((C, 256)), shape((2, 256, F)), shape((F, 256)), shape((1, C)),
    ]
    scratch = (
        [low(T, W), low(T, W), low(2, C, D), low(2, 1, C, C), low(C, D), low(2, D, F), low(F, D)]
        + [pltpu.VMEM(o.shape, o.dtype) for o in outs]
        + [low(2, 4, 4, H + Q, W)] + [low(2, 4, 4, H, W)] * 3 + [low(T, D)] * 4
        + [low(2, 4, 4, H + Q, W)] * 4
        + [low(4, 2, 4, 3, H + Q, W), low(4, 2, 3, H + Q, W), low(4, 2, 3, H + Q, W)]
        + [vmem(T + 8, C)] + [vmem(T, C)] * 13 + [vmem(T + 8, C), vmem(2 * H + T, C), vmem(2 * H + T, C), vmem(T, T)]
        + [vmem(T, F), vmem(T, W), vmem(T, W), vmem(T, W), vmem(T, W)]
        + [low(3, 2, 4, F, 256), low(3, 4, F, 256), low(3, F, 256), low(3, 2, F, 256)]
        + [low(3, 2, 4, C, 256), low(3, 4, C, 256), low(3, C, 256), low(3, 2, C, 256)]
        + [vmem(8, 256)] * 4 + [vmem(8, 256), vmem(3, 8, 256)] * 2
        + [low(2, C, 256), low(C, 256), low(4, C, 256), vmem(2, C, 256)]
        + [vmem(8, 16, 256), vmem(6144, W)]
        + [pltpu.SemaphoreType.DMA((N_SENT,)), pltpu.SemaphoreType.DMA((N_SEMS,)), pltpu.SemaphoreType.DMA((32,))]
    )
    made = pl.pallas_call(
        kernel,
        out_shape=outs,
        in_specs=[pl.BlockSpec(memory_space=pltpu.SMEM)] + [near] * 4 + [far] * 7,
        out_specs=[far] * 12,
        scratch_shapes=scratch,
        compiler_params=pltpu.CompilerParams(
            collective_id=0, has_side_effects=True, vmem_limit_bytes=62 * 2**20
        ),
    )(
        doc_lengths, norm_gains, conv_weight, lru_bias, decay.reshape(1, C), tokens.reshape(T, W),
        cotangent.reshape(T, W), jnp.swapaxes(w_branch, 1, 2), gate_weights, w_out, w_up, w_down,
    )
    made = list(pl.pallas_call(
        hand_over,
        out_shape=outs,
        in_specs=[far] * 12,
        out_specs=[far] * 12,
        scratch_shapes=[pltpu.VMEM(o.shape, o.dtype) for o in outs] + [pltpu.SemaphoreType.DMA((12,))] * 2,
        compiler_params=pltpu.CompilerParams(vmem_limit_bytes=62 * 2**20),
    )(*made))
    made[0], made[1] = made[0].reshape(1, T, W), made[1].reshape(1, T, W)
    made[3] = jnp.swapaxes(made[3], 1, 2)
    made[6], made[11] = made[6].reshape(C), made[11].reshape(1, 1, C)
    return tuple(made)


def solution(mesh):
    in_specs = (
        P("dp", "seq", "mp"), P("dp", None), P("dp", "seq", "mp"), P(None, "mp"), P(None, None, "mp"), P(None, "mp"),
        P(None, "mp"), P("mp"), P(None, "mp", None, None), P("mp", None), P(None, None, "mp"), P("mp", None),
    )
    out_specs = (
        P("dp", "seq", "mp"), P("dp", "seq", "mp"), P(None, "mp"), P(None, ("dp", "seq"), "mp"), P(None, "mp"),
        P(None, "mp"), P("mp"), P(None, "mp", None, None), P("mp", ("dp", "seq")), P(None, ("dp", "seq"), "mp"),
        P("mp", ("dp", "seq")), P("dp", "seq", "mp"),
    )
    return jax.shard_map(on_device, mesh=mesh, in_specs=in_specs, out_specs=out_specs, check_vma=False)
```

```python
import jax
import jax.numpy as jnp
from jax import lax
from jax.experimental import pallas as pl
from jax.experimental.pallas import tpu as pltpu
from jax.sharding import PartitionSpec as P

MESH = pl.DeviceIdType.MESH
f32, bf16 = jnp.float32, jnp.bfloat16

T, D, C, F, W = 256, 2048, 176, 384, 128
H = T // 2
EPS = 1e-06
N_SEMS, N_SENT = 112, 28
CP = 256
LATE = 16
Q = 16
ALPHA, CUBIC = 0.7978845608028654, 0.044715
FAR_FIRST = (2, 1, 3)


def nn(a, b):
    return lax.dot_general(a, b, (((1,), (0,)), ((), ())), preferred_element_type=f32)


def nt(a, b):
    return lax.dot_general(a, b, (((1,), (1,)), ((), ())), preferred_element_type=f32)


def sigmoid(v):
    return 1.0 / (1.0 + jnp.exp(-v))


def gelu_both(v):
    square = v * v
    t = jnp.tanh(ALPHA * v * (1.0 + CUBIC * square))
    half = 0.5 * (1.0 + t)
    return v * half, half + 0.5 * v * (1.0 - t * t) * ALPHA * (1.0 + 3.0 * CUBIC * square)


def rider_tile(row):
    high = row.astype(bf16).astype(f32)
    index = lax.broadcasted_iota(jnp.int32, (Q, H), 0)
    return jnp.where(index == 0, high, jnp.where(index == 1, row - high, 0.0)).astype(bf16)


def kernel(
    lengths, gains, conv_w, bias, decay, hbm_tokens, hbm_cot, hbm_branch, hbm_gates, hbm_out, hbm_up, hbm_down,
    o_block, o_tokens, o_gains, o_branch, o_conv, o_bias, o_decay, o_gates, o_out, o_up, o_down, o_states,
    tokens, cot, w_branch, gates, w_out, w_up, w_down,
    tok_g, cot_g, mid_g, gm_g, first, second, cot_d, gm_d,
    part1, part2, part3, part4, rs_r1, rs_s2, rs_r2,
    ext, conv, aa, rr, ii, qq, coef, through, local, p0, p1, gel, dgel, state, prev, pad_a, pad_b, tp,
    ghid, mid_own, gmid_own, scale1, scale2,
    blocks, left_mlp, g_mlp, relay_mlp, y_mlp, left_rec, g_rec, relay_rec, y_rec, lhs,
    halo_s, halo_r, back_s, back_r, car_s, car_r, rev_s, rev_r,
    gg, gg_r, gg_y, gg_f, small, gain_one, ruler,
    send_sems, recv_sems, copy_sems,
):
    me, seq, dp = lax.axis_index("mp"), lax.axis_index("seq"), lax.axis_index("dp")
    x, z = me // 4, me % 4
    core, y = seq % 2, (seq // 2) * 2 + dp

    def turn(value, by):
        return lax.rem(value + by + 4, 4)

    def on_x(d):
        return {"mp": turn(x, d) * 4 + z}

    def on_z(d):
        return {"mp": x * 4 + turn(z, d)}

    def on_y(d, same=True):
        there = turn(y, d)
        return {"dp": there % 2, "seq": (there // 2) * 2 + (core if same else 1 - core)}

    def on_seq(d):
        return {"seq": turn(seq, d)}

    other = on_y(0, False)

    groups, sources = [], []

    def wait_bytes(sem, size):
        ref = ruler.at[pl.ds(0, size // (4 * W))]
        pltpu.make_async_copy(ref, ref, sem).wait()

    class Group:
        def __init__(self, kin=groups):
            self.i, self.size, self.done = len(kin), 0, False
            kin.append(self)

        def wait(self):
            if not self.done:
                self.done = True
                wait_bytes(recv_sems.at[self.i], self.size)

    def send(src, dst, where, group, source):
        size = src.dtype.itemsize
        for dim in src.shape:
            size *= dim
        group.size += size
        source.size += size
        pltpu.make_async_remote_copy(
            src_ref=src, dst_ref=dst, send_sem=send_sems.at[source.i], recv_sem=recv_sems.at[group.i],
            device_id=where, device_id_type=MESH,
        ).start()

    def send_one(src, dst, where):
        group = Group()
        send(src, dst, where, group, misc)
        return group

    misc = Group(sources)

    barrier = pltpu.get_barrier_semaphore()
    partners = [on_x(d) for d in (1, 2, 3)] + [on_z(d) for d in (1, 2, 3)] + [on_y(d) for d in (1, 2, 3)]
    partners += [on_y(d, False) for d in (0, 1, 2, 3)]
    for where in partners:
        pl.semaphore_signal(barrier, inc=1, device_id=where, device_id_type=MESH)

    loads = []

    def load(src, dst):
        copy = pltpu.make_async_copy(src, dst, copy_sems.at[len(loads)])
        copy.start()
        loads.append(copy)
        return copy

    load_tokens, load_cot = load(hbm_tokens, tokens), load(hbm_cot, cot)
    load_branch = [load(hbm_branch.at[k], w_branch.at[pl.ds(k * CP, C)]) for k in range(2)]
    load_gates, load_out = load(hbm_gates, gates), load(hbm_out, w_out.at[pl.ds(0, C)])
    load_down = load(hbm_down, w_down)
    load_up = [load(hbm_up.at[k], w_up.at[:, pl.ds(k * F, F)]) for k in range(2)]
    for rows in (w_branch.at[pl.ds(C, CP - C)], w_branch.at[pl.ds(CP + C, CP - C)], w_out.at[pl.ds(C, CP - C)], lhs):
        rows[...] = jnp.zeros(rows.shape, bf16)

    def finish():
        for group in groups:
            group.wait()
        for source in sources:
            wait_bytes(send_sems.at[source.i], source.size)

    def axis_of(h, phase):
        return (on_x, on_z)[(h + phase) % 2]

    def place(h, first_hop, second_hop):
        return (turn(x, first_hop), turn(z, second_hop)) if h == 0 else (turn(x, second_hop), turn(z, first_hop))

    class Gather:
        def __init__(self, buf, rows):
            self.buf, self.rows = buf, rows
            self.arrivals, self.source = [], Group(sources)
            for d in (1, 3, 2):
                for h in range(2):
                    ref, group = self.view(h, x, z), Group()
                    send(ref, ref, axis_of(h, 0)(d), group, self.source)
                    self.arrivals.append((h, d, group))
            self.last = Group()
            for h in range(2):
                self.pass_on(h, 0)

        def view(self, h, cx, cz):
            return self.buf.at[h, cx, cz, pl.ds(0, self.rows[h])]

        def pass_on(self, h, d):
            ref = self.view(h, *place(h, -d, 0))
            for e in (1, 3, 2):
                send(ref, ref, axis_of(h, 1)(e), self.last, self.source)

        def forward(self):
            for h, d, group in self.arrivals:
                group.wait()
                self.pass_on(h, d)

        def end(self):
            self.last.wait()

    class Scatter:
        def __init__(self, n, part, rider=False, late=False):
            self.n, self.part, self.rider, self.late = n, part, rider, late
            self.source = Group(sources)
            self.hop1 = {(h, r): Group() for h in range(2) for r in range(4)}
            self.hop2 = {h: Group() for h in range(2)}
            if late:
                self.hop1.update({(2, r): Group() for r in range(4)})
                self.hop2[2] = Group()
            self.own, self.row = {}, {}

        def rows(self, h, rider):
            first, size = ((0, H), (0, H - LATE if self.late else H), (H - LATE, LATE))[h]
            return pl.ds(first, size + (Q if rider and self.rides(h) else 0))

        def rides(self, h):
            return self.rider and h in ((0, 2) if self.late else (0, 1))

        def launch(self, g, halves):
            n, part = self.n, self.part
            for h in halves:
                if h == 0:
                    for d in FAR_FIRST:
                        at = self.rows(h, g == 2)
                        src = part.at[0, turn(x, g), turn(z, d), at]
                        send(src, rs_r1.at[n, 0, g, d - 1, at], on_z(d), self.hop1[0, g], self.source)
                elif g:
                    for r in FAR_FIRST + (0,):
                        at = self.rows(h, r == 2)
                        src = part.at[1, turn(x, g), turn(z, r), at]
                        send(src, rs_r1.at[n, 1, r, g - 1, at], on_x(g), self.hop1[h, r], self.source)

        def produce(self, columns, halfway=None, launch=True):
            for g in FAR_FIRST + (0,):
                if g == 3 and halfway:
                    halfway()
                there = turn(x, g)
                low = columns(pl.multiple_of(there * 512, 512)).astype(bf16)
                for c in range(4):
                    piece = low[:, c * W : (c + 1) * W]
                    self.part[0, there, c, pl.ds(0, H)] = piece[:H]
                    at = self.rows(1, False)
                    self.part[1, there, c, at] = piece[H : H + at.size]
                if launch:
                    self.launch(g, (0, 1))

        def produce_late(self, columns):
            for g in FAR_FIRST + (0,):
                there = turn(x, g)
                low = columns(pl.multiple_of(there * 512, 512)).astype(bf16)
                for c in range(4):
                    self.part[1, there, c, self.rows(2, False)] = low[:, c * W : (c + 1) * W]
                self.launch(g, (2,))

        def ride(self, h, products):
            tile = rider_tile(jnp.sum(products.T, axis=0, keepdims=True))
            for c in range(4):
                spot = (0, turn(x, 2), c) if h == 0 else (1, c, turn(z, 2))
                self.part[*spot, pl.ds(H, Q)] = tile

        def step(self, h, r):
            n, part = self.n, self.part
            self.hop1[h, r].wait()
            half = min(h, 1)
            spot = (turn(x, r), z) if half == 0 else (x, turn(z, r))
            at = self.rows(h, False)
            total = part[half, *spot, at].astype(f32)
            for d in range(3):
                total += rs_r1[n, half, r, d, at].astype(f32)
            if r == 2 and self.rides(h):
                rider = part[half, *spot, pl.ds(H, Q)].astype(f32)
                for d in range(3):
                    rider += rs_r1[n, half, r, d, pl.ds(H, Q)].astype(f32)
                self.row[half] = jnp.sum(rider, axis=0, keepdims=True)
                tile = rider_tile(self.row[half])
                for k in range(3):
                    rs_s2[n, half, k, pl.ds(H, Q)] = tile
            if r:
                rs_s2[n, half, r - 1, at] = total.astype(bf16)
                at = self.rows(h, True)
                src, dst = rs_s2.at[n, half, r - 1, at], rs_r2.at[n, half, r - 1, at]
                send(src, dst, axis_of(half, 0)(r), self.hop2[h], self.source)
            else:
                self.own[h] = total

        def middle(self, between=()):
            order = ((0, 2), (0, 1), (1, 2), (0, 3), (1, 1), (1, 3), (0, 0), (1, 0))
            if self.late:
                order += ((2, 2), (2, 1), (2, 3), (2, 0))
            for i, (h, r) in enumerate(order):
                self.step(h, r)
                for work in between:
                    if work[0] == i:
                        for call in work[1:]:
                            call()

        def end(self):
            n, out, column = self.n, [], []
            for h in sorted(self.hop2):
                half, at = min(h, 1), self.rows(h, False)
                self.hop2[h].wait()
                total = self.own[h]
                for r in range(3):
                    total += rs_r2[n, half, r, at].astype(f32)
                out.append(total)
                if self.rides(h):
                    row = self.row[half]
                    for r in range(3):
                        row += jnp.sum(rs_r2[n, half, r, pl.ds(H, Q)].astype(f32), axis=0, keepdims=True)
                    column.append(jnp.broadcast_to(row, (H, H)).T)
            return jnp.concatenate(out, 0), (jnp.concatenate(column, 0) if column else None)

    def chunk(buf, c):
        return jnp.concatenate([buf[0, c // 4, c % 4, pl.ds(0, H)], buf[1, c // 4, c % 4, pl.ds(0, H)]], 0)

    def gain_row(k, c):
        return tok_g[0, c // 4, c % 4, pl.ds(H, Q)].astype(f32)[k : k + 1]

    def norm(buf, k, scale_ref, dst):
        total = jnp.zeros((T, W), f32)
        for c in range(16):
            v = chunk(buf, c).astype(f32)
            total += v * v
        scale = lax.rsqrt(jnp.sum(total, axis=1, keepdims=True) * (1.0 / D) + EPS)
        scale_ref[...] = jnp.broadcast_to(scale, (T, W))
        for c in range(16):
            v = chunk(buf, c).astype(f32)
            dst[:, c * W : (c + 1) * W] = (v * scale_ref[...] * gain_row(k, c)).astype(bf16)

    def dense(buf, dst):
        for c in range(16):
            dst[:, c * W : (c + 1) * W] = chunk(buf, c)

    def block_at(there, core_there):
        return pl.multiple_of(((there % 2) * 4 + (there // 2) * 2 + core_there) * 256, 256)

    class Columns:
        def __init__(self, i, array):
            self.i, self.array, self.blocks = i, array, blocks.at[i]

        def start(self):
            self.group, source = Group(), Group(sources)
            for there in range(4):
                src = self.array.at[:, pl.ds(block_at(there, 1 - core), 256)]
                send(src, self.blocks.at[there, pl.ds(T, T)], other, self.group, source)
                src = self.array.at[:, pl.ds(block_at(there, core), 256)]
                pltpu.make_async_copy(src, self.blocks.at[there, pl.ds(0, T)], copy_sems.at[8 + self.i]).start()

        def ready(self):
            if not self.group.done:
                wait_bytes(copy_sems.at[8 + self.i], self.group.size)
            self.group.wait()

    class WeightGrad:
        def __init__(self, columns, left, g, relay, into):
            self.columns, self.left = columns, left
            self.g, self.relay, self.into, rows = g, relay, into, left.shape[0]
            cut = rows // 32 * 16 + (16 if rows % 32 else 0)
            self.a, self.b = pl.ds(0, cut), pl.ds(cut, rows - cut)

        def start(self, left):
            mine, peer = self.left.at[:, pl.ds(0, T)], self.left.at[:, pl.ds(T, T)]
            mine[...] = left
            self.source, self.pair = Group(sources), Group()
            send(mine, peer, other, self.pair, self.source)

        def make(self, k):
            there = turn(y, k)
            self.g[there] = nn(self.left[...], self.columns.blocks[there]).astype(bf16)
            return there

        def ready(self):
            self.pair.wait()
            self.columns.ready()
            self.last = Group()

        def compute(self):
            self.ready()
            self.relayed = Group()
            far = self.make(2)
            send(self.g.at[far, self.a], self.relay.at[self.a], on_y(1), self.relayed, self.source)
            send(self.g.at[far, self.b], self.relay.at[self.b], on_y(-1), self.relayed, self.source)
            for k, at in ((1, self.b), (-1, self.a)):
                there = self.make(k)
                send(self.g.at[there, at], self.into.at[(1 - k) // 2, at], on_y(k), self.last, self.source)
            self.make(0)

        def pass_on(self):
            self.relayed.wait()
            for k, at in ((1, self.a), (-1, self.b)):
                there = turn(y, k)
                self.g[there, at] = (self.g[there, at].astype(f32) + self.relay[at].astype(f32)).astype(bf16)
                send(self.g.at[there, at], self.into.at[(1 - k) // 2, at], on_y(k), self.last, self.source)

        def end(self):
            self.last.wait()
            return self.g[y].astype(f32) + self.into[0].astype(f32) + self.into[1].astype(f32)

        def compute_direct(self):
            self.ready()
            for k in FAR_FIRST:
                there = self.make(k)
                send(self.g.at[there], self.into.at[k - 1], on_y(k), self.last, self.source)
            self.make(0)

        def end_direct(self):
            return self.end() + self.into[2].astype(f32)

    def transposed(value):
        tp[:, :C] = value
        return tp[...].T[:C]

    columns_cot, columns_second, columns_gm, columns_first = [
        Columns(i, array) for i, array in enumerate((cot_d, second, gm_d, first))
    ]

    def weight_grad(columns, i, rows):
        refs = (left_mlp, g_mlp, relay_mlp, y_mlp) if rows == F else (left_rec, g_rec, relay_rec, y_rec)
        return WeightGrad(columns, *[ref.at[i] for ref in refs])

    down, up = weight_grad(columns_cot, 0, F), [weight_grad(columns_second, 1 + k, F) for k in range(2)]
    out, branches = weight_grad(columns_gm, 0, C), [weight_grad(columns_first, 1 + k, C) for k in range(2)]

    gain_tile = jnp.concatenate([gains[...].astype(f32), jnp.zeros((Q - 2, W), f32)], 0).astype(bf16)
    tok_g[0, x, z, pl.ds(H, Q)] = gain_tile
    load_tokens.wait()
    load_cot.wait()
    for h in range(2):
        tok_g[h, x, z, pl.ds(0, H)] = tokens[pl.ds(h * H, H)]
        cot_g[h, x, z] = cot[pl.ds(h * H, H)]
    tp[...] = jnp.zeros_like(tp)
    pl.semaphore_wait(barrier, len(partners))
    tok_gather = Gather(tok_g, (H + Q, H))
    tok_gather.forward()
    cot_gather = Gather(cot_g, (H, H))

    place_here = lax.broadcasted_iota(jnp.int32, (T, 1), 0) + seq * T
    start, begins = 0, [0]
    for j in range(3):
        start = start + lengths[0, j]
        begins.append(start)

    def begin_at(p):
        hit = p == begins[0]
        for b in begins[1:]:
            hit = jnp.logical_or(hit, p == b)
        return hit

    not_reset = jnp.where(begin_at(place_here), 0.0, 1.0)
    masks = [not_reset]
    for k in (1, 2):
        masks.append(masks[-1] * jnp.where(begin_at(place_here - k), 0.0, 1.0))

    tok_gather.end()
    norm(tok_g, 0, scale1, first)
    columns_first.start()
    for copy in load_branch + [load_gates]:
        copy.wait()

    value = nt(first[...], w_branch[pl.ds(CP, CP)])[:, :C]
    p1[...] = value
    inner = value.astype(bf16).astype(f32)
    ext[pl.ds(8, T)] = inner
    halo_s[:, :C] = inner[T - 8 :]
    halo = send_one(halo_s, halo_r, on_seq(1))
    cot_gather.forward()
    value = nt(first[...], w_branch[pl.ds(0, CP)])[:, :C]
    p0[...] = value
    act, slope = gelu_both(value)
    gel[...] = act
    dgel[...] = slope
    halo.wait()
    ext[pl.ds(0, 8)] = halo_r[:, :C]
    total = bias[0:1] + conv_w[0:1] * ext[pl.ds(8, T)]
    for k in (1, 2, 3):
        total = total + conv_w[k : k + 1] * (masks[k - 1] * ext[pl.ds(8 - k, T)])
    conv[...] = total
    conv_low = total.astype(bf16)
    rate = jax.nn.softplus(decay[...])
    r_gate = sigmoid(nn(conv_low, gates[0, 0]) + bias[1:2])
    rr[...] = r_gate
    a = jnp.exp(-8.0 * r_gate * rate)
    aa[...] = a
    coef[...] = a * not_reset
    i_gate = sigmoid(nn(conv_low, gates[1, 0]) + bias[2:3])
    ii[...] = i_gate
    root = jnp.sqrt(1.0 - a * a + 0.001)
    qq[...] = root

    def scan(A, B, reverse):
        step = 1
        while step < T:
            for ref, v, fill in ((pad_a, A, 1.0), (pad_b, B, 0.0)):
                ref[pl.ds(H, T)] = v
                ref[pl.ds(H + T if reverse else 0, H)] = jnp.full((H, C), fill, f32)
            at = pl.ds(H + step if reverse else H - step, T)
            B = B + A * pad_b[at]
            A = A * pad_a[at]
            step *= 2
        return A, B

    A, B = scan(coef[...], root * i_gate * conv[...], False)
    through[...] = A
    local[...] = B
    car_s[0:1, :C] = A[T - 1 :]
    car_s[1:2, :C] = B[T - 1 :]
    carries = Group()
    for d in (2, 1, 3):
        send(car_s, car_r.at[d - 1], on_seq(d), carries, misc)
    for copy in [load_out, load_down] + load_up:
        copy.wait()
    carries.wait()

    def fold(got, reverse):
        carried = jnp.zeros((1, C), f32)
        for d in (3, 2, 1):
            here = (seq + d < 4) if reverse else (seq - d >= 0)
            slot = 4 - d if reverse else d
            new = got[slot - 1, 0:1, :C] * carried + got[slot - 1, 1:2, :C]
            carried = jnp.where(here, new, carried)
        return carried

    carried = fold(car_r, False)
    value = local[...] + through[...] * carried
    state[...] = value
    prev[pl.ds(8, T)] = value
    prev[7:8] = carried
    mixed = gel[...] * value
    lhs[:, :C] = mixed.astype(bf16)
    scatter = Scatter(0, part1)
    scatter.produce(lambda at: nn(lhs[:, :CP], w_out[:, pl.ds(at, 512)]))
    o_states[...] = value[T - 1 :]
    mixed_t = transposed(mixed).astype(bf16)
    cot_gather.end()
    dense(cot_g, cot_d)
    columns_cot.start()

    scatter.middle()
    ghid[...] = nt(cot_d[...], w_down[...])
    branch, _ = scatter.end()
    middle = tokens[...].astype(f32) + branch
    mid_own[...] = middle
    middle_low = middle.astype(bf16)
    for h in range(2):
        mid_g[h, x, z] = middle_low[h * H : (h + 1) * H]
    gather = Gather(mid_g, (H, H))
    gather.forward()
    gather.end()
    norm(mid_g, 1, scale2, second)

    pair = nn(second[...], w_up[...])
    pair0, pair1 = pair[:, :F], pair[:, F:]
    act, slope = gelu_both(pair0)
    hidden = act * pair1
    gh = ghid[...]
    gp0 = slope * pair1 * gh
    gp1 = act * gh
    products = gp0 * pair0 + gp1 * pair1
    products = products[:, :W] + products[:, W : 2 * W] + products[:, 2 * W :]
    gp_low = jnp.concatenate([gp0.astype(bf16), gp1.astype(bf16)], 1)
    scatter = Scatter(1, part2, True)
    for h in range(2):
        scatter.ride(h, products[h * H : (h + 1) * H])

    down.start(hidden.T.astype(bf16))

    def halfway():
        up[0].start(gp0.T.astype(bf16))
        columns_second.start()
        up[1].start(gp1.T.astype(bf16))

    scatter.produce(lambda at: nt(gp_low, w_up[pl.ds(at, 512)]), halfway)
    down.compute()
    up[0].compute()
    scatter.middle(((3, up[1].compute), (7, down.pass_on)))

    grad_n, q = scatter.end()
    v = mid_own[...].astype(bf16).astype(f32)
    s = scale2[...]
    gain = gains[1:2].astype(f32)
    grad_middle_own = cot[...].astype(f32) + s * gain * grad_n - v * s * s * q * (1.0 / D)
    gmid_own[...] = grad_middle_own
    low = grad_middle_own.astype(bf16)
    for h in range(2):
        gm_g[h, x, z] = low[h * H : (h + 1) * H]
    gather = Gather(gm_g, (H, H))
    mine = small.at[dp * 4 + seq]
    mine[...] = jnp.zeros((16, 256), f32)
    mine[1:2, :W] = jnp.sum(grad_n * v * s, axis=0, keepdims=True)
    gather.forward()
    up[0].pass_on()
    hidden_low = hidden.astype(bf16)
    scatter_out = Scatter(2, part3)
    scatter_out.produce(lambda at: nn(hidden_low, w_down[:, pl.ds(at, 512)]), launch=False)
    up[1].pass_on()
    gather.end()
    for g in FAR_FIRST + (0,):
        scatter_out.launch(g, (0, 1))
    dense(gm_g, gm_d)
    columns_gm.start()

    grad_mixed = nt(gm_d[...], w_out[...])[:, :C]
    grad_y = dgel[...] * state[...] * grad_mixed
    grad_state = gel[...] * grad_mixed
    pad_a[pl.ds(0, T)] = coef[...]
    pad_a[pl.ds(T, 8)] = jnp.ones((8, C), f32)
    A, B = scan(pad_a[pl.ds(1, T)], grad_state, True)
    rev_s[0:1, :C] = through[T - 1 :]
    rev_s[1:2, :C] = coef[0:1] * B[0:1]
    carries = Group()
    for d in (2, 1, 3):
        send(rev_s, rev_r.at[d - 1], on_seq(d), carries, misc)
    out.start(mixed_t)
    branches[0].start(transposed(grad_y).astype(bf16))
    out.compute()
    branches[0].compute()
    cv_t = transposed(conv[...]).astype(bf16)
    carries.wait()
    total = B + A * fold(rev_r, True)
    a, r_gate, i_gate, root, cv = aa[...], rr[...], ii[...], qq[...], conv[...]
    t_i = total * i_gate
    d_log = total * prev[pl.ds(7, T)] * coef[...] - t_i * cv * (a * a / root)
    d_gate = d_log * r_gate
    mine[9:10, :C] = -8.0 * sigmoid(decay[...]) * jnp.sum(d_gate, axis=0, keepdims=True)
    gpre0 = -8.0 * rate * d_gate * (1.0 - r_gate)
    direct = t_i * root
    gpre1 = direct * cv * (1.0 - i_gate)
    low0, low1 = gpre0.astype(bf16), gpre1.astype(bf16)
    mine[7:8, :C] = jnp.sum(low0.astype(f32), axis=0, keepdims=True)
    mine[8:9, :C] = jnp.sum(low1.astype(f32), axis=0, keepdims=True)
    grad_conv = direct + nt(low0, gates[0, 0]) + nt(low1, gates[1, 0])
    mine[6:7, :C] = jnp.sum(grad_conv, axis=0, keepdims=True)
    edge = jnp.zeros((8, C), f32)
    grad_inner = jnp.zeros((T, C), f32)
    for k in range(4):
        weighted = grad_conv if k == 0 else masks[k - 1] * grad_conv
        mine[2 + k : 3 + k, :C] = jnp.sum(weighted * ext[pl.ds(8 - k, T)], axis=0, keepdims=True)
        if k == 0:
            pad_a[pl.ds(0, 8)] = jnp.zeros((8, C), f32)
            pad_a[pl.ds(8 + T, 8)] = jnp.zeros((8, C), f32)
        pad_a[pl.ds(8, T)] = conv_w[k : k + 1] * weighted
        edge += pad_a[pl.ds(k, 8)]
        grad_inner += pad_a[pl.ds(8 + k, T)]
    back_s[:, :C] = edge
    back = send_one(back_s, back_r, on_seq(-1))
    lhs[:, :C] = grad_y.astype(bf16)
    lhs[:, CP : CP + C] = grad_inner.astype(bf16)
    scatter = Scatter(3, part4, True, True)
    tp[:, :C] = grad_y * p0[...] + grad_inner * p1[...]
    scatter.ride(0, tp[pl.ds(0, H), :W] + tp[pl.ds(0, H), W:])

    scatter.produce(lambda at: nn(lhs[...], w_branch[:, pl.ds(at, 512)]))
    gg[0, :, :C] = nn(cv_t, low0).astype(bf16)
    gg[1, :, :C] = nn(cv_t, low1).astype(bf16)
    gg_pair = send_one(gg.at[1 - core], gg_r, other)
    gg_all = Group()
    mine = small.at[dp * 4 + seq]
    others = ((2, False), (2, True), (1, False), (1, True), (3, False), (3, True), (0, False))
    smalls, gain_sums = Group(), Group()
    for d, same in others:
        send(mine, mine, on_y(d, same), smalls, misc)
    out.pass_on()
    branches[0].pass_on()
    back.wait()
    ext[pl.ds(0, T)] = grad_inner
    ext[pl.ds(T - 8, 8)] = grad_inner[T - 8 :] + back_r[:, :C]
    grad_inner = ext[pl.ds(0, T)]
    tp[:, :C] = grad_y * p0[...] + grad_inner * p1[...]
    scatter.ride(1, tp[pl.ds(H, H), :W] + tp[pl.ds(H, H), W:])
    late = pl.ds(T - LATE, LATE)
    lhs[late, CP : CP + C] = grad_inner[T - LATE :].astype(bf16)
    scatter.produce_late(lambda at: nn(lhs[late], w_branch[:, pl.ds(at, 512)]))
    branches[1].start(transposed(grad_inner).astype(bf16))
    def gates_middle():
        gg_pair.wait()
        gg_y[y] = (gg[core].astype(f32) + gg_r[...].astype(f32)).astype(bf16)
        for d in FAR_FIRST:
            send(gg_y.at[y], gg_y.at[y], on_y(d), gg_all, misc)

    scatter.middle((
        (0, gates_middle), (1, branches[1].compute_direct),
    ))
    scatter_out.middle()
    o_down[...] = down.end()
    for k in range(2):
        o_up[k] = up[k].end().T

    grad_n, q = scatter.end()
    v = tokens[...].astype(f32)
    s = scale1[...]
    gain = gains[0:1].astype(f32)
    mine = gain_one.at[dp * 4 + seq]
    mine[...] = jnp.broadcast_to(jnp.sum(grad_n * v * s, axis=0, keepdims=True), (8, W))
    for d, same in others:
        send(mine, mine, on_y(d, same), gain_sums, misc)
    gg_all.wait()
    gg_f[core] = gg_y[0].astype(f32) + gg_y[1].astype(f32) + gg_y[2].astype(f32) + gg_y[3].astype(f32)
    gg_share = send_one(gg_f.at[core], gg_f.at[core], other)
    o_tokens[...] = gmid_own[...] + s * gain * grad_n - v * s * s * q * (1.0 / D)
    o_out[...] = out.end()
    result, _ = scatter_out.end()
    o_block[...] = (mid_own[...] + result).astype(bf16)
    o_branch[0] = branches[0].end()
    o_branch[1] = branches[1].end_direct()
    gg_share.wait()
    for k in range(2):
        o_gates[k, 0] = gg_f[k, :, :C]
    smalls.wait()
    total = small[0]
    for j in range(1, 8):
        total += small[j]
    o_gains[1:2] = total[1:2, :W]
    o_conv[...] = total[2:6, :C]
    o_bias[...] = total[6:9, :C]
    o_decay[...] = total[9:10, :C]
    gain_sums.wait()
    total = gain_one[0, 0:1]
    for j in range(1, 8):
        total += gain_one[j, 0:1]
    o_gains[0:1] = total
    finish()


def hand_over(*refs):
    n = 12
    copies = [pltpu.make_async_copy(refs[i], refs[n + i], refs[-1].at[i]) for i in range(n)]
    for copy in copies:
        copy.start()
    for copy in copies:
        copy.wait()


def on_device(
    tokens, doc_lengths, cotangent, norm_gains, w_branch, conv_weight, lru_bias, decay, gate_weights, w_out, w_up, w_down
):
    def shape(dims, kind=f32):
        return jax.ShapeDtypeStruct(dims, kind)

    def vmem(*dims):
        return pltpu.VMEM(dims, f32)

    def low(*dims):
        return pltpu.VMEM(dims, bf16)

    near, far = pl.BlockSpec(memory_space=pltpu.VMEM), pl.BlockSpec(memory_space=pl.ANY)
    outs = [
        shape((T, W), bf16), shape((T, W)), shape((2, W)), shape((2, C, 256)), shape((4, C)), shape((3, C)),
        shape((1, C)), shape((2, 1, C, C)), shape((C, 256)), shape((2, 256, F)), shape((F, 256)), shape((1, C)),
    ]
    scratch = (
        [low(T, W), low(T, W), low(2 * CP, D), low(2, 1, C, C), low(CP, D), low(D, 2 * F), low(F, D)]
        + [low(2, 4, 4, H + Q, W)] + [low(2, 4, 4, H, W)] * 3 + [low(T, D)] * 4
        + [low(2, 4, 4, H + Q, W)] * 4
        + [low(4, 2, 4, 3, H + Q, W), low(4, 2, 3, H + Q, W), low(4, 2, 3, H + Q, W)]
        + [vmem(T + 8, C)] + [vmem(T, C)] * 13 + [vmem(T + 8, C), vmem(2 * H + T, C), vmem(2 * H + T, C), vmem(T, T)]
        + [vmem(T, F), vmem(T, W), vmem(T, W), vmem(T, W), vmem(T, W)]
        + [low(4, 4, 2 * T, 256)]
        + [low(3, F, 2 * T), low(3, 4, F, 256), low(3, F, 256), low(3, 2, F, 256)]
        + [low(3, C, 2 * T), low(3, 4, C, 256), low(3, C, 256), low(3, 3, C, 256), low(T, 2 * CP)]
        + [vmem(8, 256)] * 4 + [vmem(8, 256), vmem(3, 8, 256)] * 2
        + [low(2, C, 256), low(C, 256), low(4, C, 256), vmem(2, C, 256)]
        + [vmem(8, 16, 256), vmem(8, 8, W), vmem(6144, W)]
        + [pltpu.SemaphoreType.DMA((N_SENT,)), pltpu.SemaphoreType.DMA((N_SEMS,)), pltpu.SemaphoreType.DMA((12,))]
    )
    made = pl.pallas_call(
        kernel,
        out_shape=[pltpu.VMEM(o.shape, o.dtype) for o in outs],
        in_specs=[pl.BlockSpec(memory_space=pltpu.SMEM)] + [near] * 4 + [far] * 7,
        out_specs=[near] * 12,
        scratch_shapes=scratch,
        compiler_params=pltpu.CompilerParams(
            collective_id=0, has_side_effects=True, vmem_limit_bytes=56 * 2**20
        ),
    )(
        doc_lengths, norm_gains, conv_weight, lru_bias, decay.reshape(1, C), tokens.reshape(T, W),
        cotangent.reshape(T, W), jnp.swapaxes(w_branch, 1, 2), gate_weights, w_out, w_up, w_down,
    )
    made = list(pl.pallas_call(
        hand_over,
        out_shape=outs,
        in_specs=[near] * 12,
        out_specs=[far] * 12,
        scratch_shapes=[pltpu.SemaphoreType.DMA((12,))],
        compiler_params=pltpu.CompilerParams(vmem_limit_bytes=2 * 2**20),
    )(*made))
    made[0], made[1] = made[0].reshape(1, T, W), made[1].reshape(1, T, W)
    made[3] = jnp.swapaxes(made[3], 1, 2)
    made[6], made[11] = made[6].reshape(C), made[11].reshape(1, 1, C)
    return tuple(made)


def solution(mesh):
    in_specs = (
        P("dp", "seq", "mp"), P("dp", None), P("dp", "seq", "mp"), P(None, "mp"), P(None, None, "mp"), P(None, "mp"),
        P(None, "mp"), P("mp"), P(None, "mp", None, None), P("mp", None), P(None, None, "mp"), P("mp", None),
    )
    out_specs = (
        P("dp", "seq", "mp"), P("dp", "seq", "mp"), P(None, "mp"), P(None, ("dp", "seq"), "mp"), P(None, "mp"),
        P(None, "mp"), P("mp"), P(None, "mp", None, None), P("mp", ("dp", "seq")), P(None, ("dp", "seq"), "mp"),
        P("mp", ("dp", "seq")), P("dp", "seq", "mp"),
    )
    return jax.shard_map(on_device, mesh=mesh, in_specs=in_specs, out_specs=out_specs, check_vma=False)
```

```python
import jax
import jax.numpy as jnp
from jax import lax
from jax.experimental import pallas as pl
from jax.experimental.pallas import tpu as pltpu
from jax.sharding import PartitionSpec as P

MESH = pl.DeviceIdType.MESH
f32, bf16 = jnp.float32, jnp.bfloat16

T, D, C, F, W = 256, 2048, 176, 384, 128
H = T // 2
S = T // 4
EPS = 1e-06
N_SEMS, N_SENT = 152, 24
CP = 256
LATE = 16
Q = 16
ALPHA, CUBIC = 0.7978845608028654, 0.044715
FAR_FIRST = (2, 1, 3)


def nn(a, b):
    return lax.dot_general(a, b, (((1,), (0,)), ((), ())), preferred_element_type=f32)


def nt(a, b):
    return lax.dot_general(a, b, (((1,), (1,)), ((), ())), preferred_element_type=f32)


def sigmoid(v):
    return 1.0 / (1.0 + jnp.exp(-v))


def gelu_both(v):
    square = v * v
    t = jnp.tanh(ALPHA * v * (1.0 + CUBIC * square))
    half = 0.5 * (1.0 + t)
    return v * half, half + 0.5 * v * (1.0 - t * t) * ALPHA * (1.0 + 3.0 * CUBIC * square)


def rider_tile(row):
    if row.shape[1] < W:
        row = jnp.concatenate([row, jnp.zeros((1, W - row.shape[1]), f32)], 1)
    high = row.astype(bf16).astype(f32)
    index = lax.broadcasted_iota(jnp.int32, (Q, W), 0)
    return jnp.where(index == 0, high, jnp.where(index == 1, row - high, 0.0)).astype(bf16)


def kernel(
    lengths, gains, conv_w, bias, decay, hbm_tokens, hbm_cot, hbm_branch, hbm_gates, hbm_out, hbm_up, hbm_down,
    o_block, o_tokens, o_gains, o_branch, o_conv, o_bias, o_decay, o_gates, o_out, o_up, o_down, o_states,
    tokens, cot, w_branch, gates, w_out, w_up, w_down,
    tok_g, cot_g, mid_g, gm_g, tok_v, cot_v, mid_v, gm_v, first, second, cot_d, gm_d,
    part_s, r1_s, s2_s, r2_s, part_b, r1_b, s2_b, r2_b, hidden_low, grad_y_s, grad_state_s,
    ext, conv, aa, rr, ii, qq, coef, through, local, p0, p1, gel, dgel, state, prev, pad_a, pad_b, tp,
    ghid, mid_own, gmid_own, scale1, scale2,
    blocks, left_mlp, g_mlp, relay_mlp, y_mlp, left_rec, g_rec, relay_rec, y_rec, lhs,
    halo_s, halo_r, back_s, back_r, car_s, car_r, rev_s, rev_r,
    gg, gg_r, gg_y, gg_f, small_own, small_mate, small, gain_one, ruler,
    send_sems, recv_sems, copy_sems,
):
    me, seq, dp = lax.axis_index("mp"), lax.axis_index("seq"), lax.axis_index("dp")
    x, z = me // 4, me % 4
    core, y = seq % 2, (seq // 2) * 2 + dp

    def turn(value, by):
        return lax.rem(value + by + 4, 4)

    mate = (seq // 2) * 2 + (1 - core)

    def on_x(d):
        return {"mp": turn(x, d) * 4 + z, "seq": mate}

    def on_z(d):
        return {"mp": x * 4 + turn(z, d), "seq": mate}

    def on_y(d, same=True):
        there = turn(y, d)
        return {"dp": there % 2, "seq": (there // 2) * 2 + (core if same else 1 - core)}

    def on_seq(d):
        return {"seq": turn(seq, d)}

    other = on_y(0, False)

    groups, sources = [], []

    def wait_bytes(sem, size):
        ref = ruler.at[pl.ds(0, size // (4 * W))]
        pltpu.make_async_copy(ref, ref, sem).wait()

    class Group:
        def __init__(self, kin=groups):
            self.i, self.size, self.done = len(kin), 0, False
            kin.append(self)

        def wait(self):
            if not self.done:
                self.done = True
                wait_bytes(recv_sems.at[self.i], self.size)

    def send(src, dst, where, group, source):
        size = src.dtype.itemsize
        for dim in src.shape:
            size *= dim
        group.size += size
        source.size += size
        pltpu.make_async_remote_copy(
            src_ref=src, dst_ref=dst, send_sem=send_sems.at[source.i], recv_sem=recv_sems.at[group.i],
            device_id=where, device_id_type=MESH,
        ).start()

    def send_one(src, dst, where):
        group = Group()
        send(src, dst, where, group, misc)
        return group

    misc = Group(sources)

    barrier = pltpu.get_barrier_semaphore()
    partners = [on_x(d) for d in (1, 2, 3)] + [on_z(d) for d in (1, 2, 3)] + [on_y(d) for d in (1, 2, 3)]
    partners += [on_y(d, False) for d in (0, 1, 2, 3)]
    for where in partners:
        pl.semaphore_signal(barrier, inc=1, device_id=where, device_id_type=MESH)

    loads = []

    def load(src, dst):
        copy = pltpu.make_async_copy(src, dst, copy_sems.at[len(loads)])
        copy.start()
        loads.append(copy)
        return copy

    load_tokens, load_cot = load(hbm_tokens, tokens), load(hbm_cot, cot)
    load_branch = [load(hbm_branch.at[k], w_branch.at[pl.ds(k * CP, C)]) for k in range(2)]
    load_gates, load_out = load(hbm_gates, gates), load(hbm_out, w_out.at[pl.ds(0, C)])
    load_down = load(hbm_down, w_down)
    load_up = [load(hbm_up.at[k], w_up.at[:, pl.ds(k * F, F)]) for k in range(2)]
    for rows in (w_branch.at[pl.ds(C, CP - C)], w_branch.at[pl.ds(CP + C, CP - C)], w_out.at[pl.ds(C, CP - C)], lhs):
        rows[...] = jnp.zeros(rows.shape, bf16)

    def finish():
        for group in groups:
            group.wait()
        for source in sources:
            wait_bytes(send_sems.at[source.i], source.size)

    def axis_of(h, phase):
        return (on_x, on_z)[(h + phase) % 2]

    def place(h, first_hop):
        return (turn(x, first_hop), z) if h == 0 else (x, turn(z, first_hop))

    class Gather:
        def __init__(self, buf, via, rows):
            self.buf, self.via, self.rows = buf, via, rows
            self.arrivals, self.last, self.source = [], Group(), Group(sources)
            for d in (1, 3, 2, 0):
                for h in range(2):
                    group = Group()
                    send(self.view(buf, h, 0), self.view(via, h, 0), axis_of(h, 0)(d), group, self.source)
                    self.arrivals.append((h, d, group))

        def view(self, buf, h, d):
            return buf.at[h, *place(h, -d), pl.ds(0, self.rows[h])]

        def forward(self):
            for h, d, group in self.arrivals[-2:] + self.arrivals[:-2]:
                group.wait()
                src, dst = self.view(self.via, h, d), self.view(self.buf, h, d)
                for e in (1, 3, 2):
                    send(src, dst, axis_of(h, 1)(e), self.last, self.source)
                if d:
                    send(src, dst, other, self.last, self.source)

        def end(self):
            self.last.wait()

    class Scatter:
        def __init__(self, refs, rider=False, late=False):
            self.part, self.r1, self.s2, self.r2 = refs
            self.size = self.part.shape[3] - Q
            self.rider, self.late = rider, late
            self.source = Group(sources)
            self.hop1 = {(h, r): Group() for h in range(2) for r in range(4)}
            self.hop2 = {h: Group() for h in range(2)}
            if late:
                self.hop1.update({(2, r): Group() for r in range(4)})
                self.hop2[2] = Group()

        def rows(self, h, rider):
            first, size = ((0, self.size), (0, self.size - LATE if self.late else self.size), (self.size - LATE, LATE))[h]
            return pl.ds(first, size + (Q if rider and self.rides(h) else 0))

        def rides(self, h):
            return self.rider and h in ((0, 2) if self.late else (0, 1))

        def launch(self, g, halves):
            for h in halves:
                for k in FAR_FIRST + (0,):
                    if h == 0 or k:
                        r, d = (g, k) if h == 0 else (k, g)
                        self.pass_part(h, r, d)
            if g == 0 and not (self.late and 0 in halves):
                for h in (1, 2) if self.late else (1,):
                    for k in FAR_FIRST + (0,):
                        self.pass_part(h, 0, k)

        def pass_part(self, h, r, d):
            half = min(h, 1)
            spot = (turn(x, r), turn(z, d)) if half == 0 else (turn(x, d), turn(z, r))
            at = self.rows(h, r == 2)
            src, dst = self.part.at[half, *spot, at], self.r1.at[half, r, d, at]
            send(src, dst, axis_of(half, 1)(d), self.hop1[h, r], self.source)

        def produce(self, columns, halfway=None, launch=True):
            for g in FAR_FIRST + (0,):
                if g == 3 and halfway:
                    halfway()
                there = turn(x, g)
                low = columns(pl.multiple_of(there * 512, 512)).astype(bf16)
                for c in range(4):
                    piece = low[:, c * W : (c + 1) * W]
                    self.part[0, there, c, pl.ds(0, self.size)] = piece[: self.size]
                    at = self.rows(1, False)
                    self.part[1, there, c, at] = piece[self.size : self.size + at.size]
                if launch and g in (1, 0):
                    for k in (2, 1) if g == 1 else (3, 0):
                        self.launch(k, (0, 1))

        def produce_late(self, columns):
            for g in FAR_FIRST + (0,):
                there = turn(x, g)
                low = columns(pl.multiple_of(there * 512, 512)).astype(bf16)
                for c in range(4):
                    self.part[1, there, c, self.rows(2, False)] = low[:, c * W : (c + 1) * W]
                self.launch(g, (2,))

        def ride(self, h, products):
            tile = rider_tile(jnp.sum(products.T, axis=0, keepdims=True))
            for c in range(4):
                spot = (0, turn(x, 2), c) if h == 0 else (1, c, turn(z, 2))
                self.part[*spot, pl.ds(self.size, Q)] = tile

        def step(self, h, r):
            half, extra = min(h, 1), pl.ds(self.size, Q)
            self.hop1[h, r].wait()

            def total(at):
                parts = [self.r1[half, r, d, at].astype(f32) for d in range(4)]
                return (parts[0] + parts[1]) + (parts[2] + parts[3])

            if r == 2 and self.rides(h):
                tile = rider_tile(jnp.sum(total(extra), axis=0, keepdims=True))
                for k in range(4):
                    self.s2[half, k, extra] = tile
            at = self.rows(h, False)
            self.s2[half, r, at] = total(at).astype(bf16)
            at = self.rows(h, True)
            send(self.s2.at[half, r, at], self.r2.at[half, r, at], axis_of(half, 0)(r), self.hop2[h], self.source)

        def middle(self, between=()):
            order = ((0, 2), (0, 1), (1, 2), (0, 3), (1, 1), (1, 3))
            if self.late:
                order += ((2, 2), (2, 1), (2, 3), (2, 0))
            order += ((0, 0), (1, 0))
            for i, (h, r) in enumerate(order):
                self.step(h, r)
                for work in between:
                    if work[0] == i:
                        for call in work[1:]:
                            call()

        def end(self):
            out, column = [], []
            for h in sorted(self.hop2):
                half, at = min(h, 1), self.rows(h, False)
                self.hop2[h].wait()
                parts = [self.r2[half, r, at].astype(f32) for r in range(4)]
                out.append((parts[0] + parts[1]) + (parts[2] + parts[3]))
                if self.rides(h):
                    rider = self.r2[half, 0, pl.ds(self.size, Q)].astype(f32)
                    for r in range(1, 4):
                        rider += self.r2[half, r, pl.ds(self.size, Q)].astype(f32)
                    row = jnp.sum(rider, axis=0, keepdims=True)
                    column.append(jnp.broadcast_to(row, (W, W)).T[: self.size])
            return jnp.concatenate(out, 0), (jnp.concatenate(column, 0) if column else None)

    def chunk(buf, c):
        size = min(buf.shape[3], H)
        return jnp.concatenate([buf[h, c // 4, c % 4, pl.ds(0, size)] for h in range(2)], 0)

    def gain_row(k, c):
        return tok_g[0, c // 4, c % 4, pl.ds(H, Q)].astype(f32)[k : k + 1]

    def norm(buf, k, at):
        scale_ref, dst = ((scale1, first), (scale2, second))[k]
        total = jnp.zeros((at.size, W), f32)
        for c in range(16):
            v = chunk(buf, c).astype(f32)
            total += v * v
        scale = lax.rsqrt(jnp.sum(total, axis=1, keepdims=True) * (1.0 / D) + EPS)
        scale_ref[at] = jnp.broadcast_to(scale, (at.size, W))
        for c in range(16):
            v = chunk(buf, c).astype(f32)
            dst[at, c * W : (c + 1) * W] = (v * scale_ref[at] * gain_row(k, c)).astype(bf16)

    def dense(buf, dst, at):
        for c in range(16):
            dst[at, c * W : (c + 1) * W] = chunk(buf, c)

    everything, streams = pl.ds(0, T), [pl.ds(0, H), pl.ds(H, H)]

    def block_at(there, core_there):
        return pl.multiple_of(((there % 2) * 4 + (there // 2) * 2 + core_there) * 256, 256)

    class Columns:
        def __init__(self, i, array):
            self.i, self.array, self.blocks = i, array, blocks.at[i]

        def start(self):
            self.group, source = Group(), Group(sources)
            for there in range(4):
                src = self.array.at[:, pl.ds(block_at(there, 1 - core), 256)]
                send(src, self.blocks.at[there, pl.ds(T, T)], other, self.group, source)
                src = self.array.at[:, pl.ds(block_at(there, core), 256)]
                pltpu.make_async_copy(src, self.blocks.at[there, pl.ds(0, T)], copy_sems.at[8 + self.i]).start()

        def ready(self):
            if not self.group.done:
                wait_bytes(copy_sems.at[8 + self.i], self.group.size)
            self.group.wait()

    class WeightGrad:
        def __init__(self, columns, left, g, relay, into):
            self.columns, self.left = columns, left
            self.g, self.relay, self.into, rows = g, relay, into, left.shape[0]
            cut = rows // 32 * 16 + (16 if rows % 32 else 0)
            self.a, self.b = pl.ds(0, cut), pl.ds(cut, rows - cut)

        def start(self, left=None):
            mine, peer = self.left.at[:, pl.ds(0, T)], self.left.at[:, pl.ds(T, T)]
            if left is not None:
                mine[...] = left
            self.source, self.pair = Group(sources), Group()
            send(mine, peer, other, self.pair, self.source)

        def make(self):
            self.pair.wait()
            self.columns.ready()
            self.last = Group()
            for there in range(4):
                self.g[there] = nn(self.left[...], self.columns.blocks[there]).astype(bf16)

        def compute(self):
            self.make()
            self.relayed = Group()
            far = turn(y, 2)
            send(self.g.at[far, self.a], self.relay.at[self.a], on_y(1), self.relayed, self.source)
            send(self.g.at[far, self.b], self.relay.at[self.b], on_y(-1), self.relayed, self.source)
            for k, at in ((1, self.b), (-1, self.a)):
                src = self.g.at[turn(y, k), at]
                send(src, self.into.at[(1 - k) // 2, at], on_y(k), self.last, self.source)

        def pass_on(self):
            self.relayed.wait()
            for k, at in ((1, self.a), (-1, self.b)):
                there = turn(y, k)
                self.g[there, at] = (self.g[there, at].astype(f32) + self.relay[at].astype(f32)).astype(bf16)
                send(self.g.at[there, at], self.into.at[(1 - k) // 2, at], on_y(k), self.last, self.source)

        def end(self):
            self.last.wait()
            return self.g[y].astype(f32) + self.into[0].astype(f32) + self.into[1].astype(f32)

        def compute_direct(self):
            self.make()
            for k in FAR_FIRST:
                send(self.g.at[turn(y, k)], self.into.at[k - 1], on_y(k), self.last, self.source)

        def end_direct(self):
            return self.end() + self.into[2].astype(f32)

    def transposed(value):
        tp[:, :C] = value
        return tp[...].T[:C]

    columns_cot, columns_second, columns_gm, columns_first = [
        Columns(i, array) for i, array in enumerate((cot_d, second, gm_d, first))
    ]

    def weight_grad(columns, i, rows):
        refs = (left_mlp, g_mlp, relay_mlp, y_mlp) if rows == F else (left_rec, g_rec, relay_rec, y_rec)
        return WeightGrad(columns, *[ref.at[i] for ref in refs])

    down, up = weight_grad(columns_cot, 0, F), [weight_grad(columns_second, 1 + k, F) for k in range(2)]
    out, branches = weight_grad(columns_gm, 0, C), [weight_grad(columns_first, 1 + k, C) for k in range(2)]

    gain_tile = jnp.concatenate([gains[...].astype(f32), jnp.zeros((Q - 2, W), f32)], 0).astype(bf16)
    tok_g[0, x, z, pl.ds(H, Q)] = gain_tile
    load_tokens.wait()
    load_cot.wait()
    for h in range(2):
        tok_g[h, x, z, pl.ds(0, H)] = tokens[pl.ds(h * H, H)]
        cot_g[h, x, z] = cot[pl.ds(h * H, H)]
    tp[...] = jnp.zeros_like(tp)
    pl.semaphore_wait(barrier, len(partners))
    tok_gather = Gather(tok_g, tok_v, (H + Q, H))
    tok_gather.forward()
    cot_gather = Gather(cot_g, cot_v, (H, H))

    place_here = lax.broadcasted_iota(jnp.int32, (T, 1), 0) + seq * T
    start, begins = 0, [0]
    for j in range(3):
        start = start + lengths[0, j]
        begins.append(start)

    def begin_at(p):
        hit = p == begins[0]
        for b in begins[1:]:
            hit = jnp.logical_or(hit, p == b)
        return hit

    not_reset = jnp.where(begin_at(place_here), 0.0, 1.0)
    masks = [not_reset]
    for k in (1, 2):
        masks.append(masks[-1] * jnp.where(begin_at(place_here - k), 0.0, 1.0))

    tok_gather.end()
    norm(tok_g, 0, everything)
    columns_first.start()
    for copy in load_branch + [load_gates]:
        copy.wait()

    value = nt(first[...], w_branch[pl.ds(CP, CP)])[:, :C]
    p1[...] = value
    inner = value.astype(bf16).astype(f32)
    ext[pl.ds(8, T)] = inner
    halo_s[:, :C] = inner[T - 8 :]
    halo = send_one(halo_s, halo_r, on_seq(1))
    cot_gather.forward()
    value = nt(first[...], w_branch[pl.ds(0, CP)])[:, :C]
    p0[...] = value
    act, slope = gelu_both(value)
    gel[...] = act
    dgel[...] = slope
    halo.wait()
    ext[pl.ds(0, 8)] = halo_r[:, :C]
    total = bias[0:1] + conv_w[0:1] * ext[pl.ds(8, T)]
    for k in (1, 2, 3):
        total = total + conv_w[k : k + 1] * (masks[k - 1] * ext[pl.ds(8 - k, T)])
    conv[...] = total
    conv_low = total.astype(bf16)
    rate = jax.nn.softplus(decay[...])
    r_gate = sigmoid(nn(conv_low, gates[0, 0]) + bias[1:2])
    rr[...] = r_gate
    a = jnp.exp(-8.0 * r_gate * rate)
    aa[...] = a
    coef[...] = a * not_reset
    i_gate = sigmoid(nn(conv_low, gates[1, 0]) + bias[2:3])
    ii[...] = i_gate
    root = jnp.sqrt(1.0 - a * a + 0.001)
    qq[...] = root

    def scan(A, B, reverse):
        step = 1
        while step < T:
            for ref, v, fill in ((pad_a, A, 1.0), (pad_b, B, 0.0)):
                ref[pl.ds(H, T)] = v
                ref[pl.ds(H + T if reverse else 0, H)] = jnp.full((H, C), fill, f32)
            at = pl.ds(H + step if reverse else H - step, T)
            B = B + A * pad_b[at]
            A = A * pad_a[at]
            step *= 2
        return A, B

    A, B = scan(coef[...], root * i_gate * conv[...], False)
    through[...] = A
    local[...] = B
    car_s[0:1, :C] = A[T - 1 :]
    car_s[1:2, :C] = B[T - 1 :]
    carries = Group()
    for d in (2, 1, 3):
        send(car_s, car_r.at[d - 1], on_seq(d), carries, misc)
    for copy in [load_out, load_down] + load_up:
        copy.wait()
    carries.wait()

    def fold(got, reverse):
        carried = jnp.zeros((1, C), f32)
        for d in (3, 2, 1):
            here = (seq + d < 4) if reverse else (seq - d >= 0)
            slot = 4 - d if reverse else d
            new = got[slot - 1, 0:1, :C] * carried + got[slot - 1, 1:2, :C]
            carried = jnp.where(here, new, carried)
        return carried

    carried = fold(car_r, False)
    value = local[...] + through[...] * carried
    state[...] = value
    prev[pl.ds(8, T)] = value
    prev[7:8] = carried
    mixed = gel[...] * value
    lhs[:, :C] = mixed.astype(bf16)

    def stream_refs(i):
        return [ref.at[i] for ref in (part_s, r1_s, s2_s, r2_s)]

    def part_refs(i):
        return [ref.at[i] for ref in (part_b, r1_b, s2_b, r2_b)]

    sums = [Scatter(stream_refs(i)) for i in range(2)]
    for at, scatter in zip(streams, sums):
        scatter.produce(lambda c: nn(lhs[at, :CP], w_out[:, pl.ds(c, 512)]))
    o_states[...] = value[T - 1 :]
    mixed_t = transposed(mixed).astype(bf16)
    cot_gather.end()
    dense(cot_g, cot_d, everything)
    sums[0].middle()
    columns_cot.start()
    sums[1].middle()
    gathers = []
    for i, at in enumerate(streams):
        branch, _ = sums[i].end()
        middle = tokens[at].astype(f32) + branch
        mid_own[at] = middle
        middle_low = middle.astype(bf16)
        for h in range(2):
            mid_g[i, h, x, z] = middle_low[h * S : (h + 1) * S]
        gathers.append(Gather(mid_g.at[i], mid_v.at[i], (S, S)))
    gathers[0].forward()
    ghid[...] = nt(cot_d[...], w_down[...])
    gathers[1].forward()

    sums = [Scatter(stream_refs(2 + i), True) for i in range(2)]
    for i, at in enumerate(streams):
        gathers[i].end()
        norm(mid_g.at[i], 1, at)
        pair = nn(second[at], w_up[...])
        pair0, pair1 = pair[:, :F], pair[:, F:]
        act, slope = gelu_both(pair0)
        hidden = act * pair1
        gh = ghid[at]
        gp0 = slope * pair1 * gh
        gp1 = act * gh
        products = gp0 * pair0 + gp1 * pair1
        products = products[:, :W] + products[:, W : 2 * W] + products[:, 2 * W :]
        gp_low = jnp.concatenate([gp0.astype(bf16), gp1.astype(bf16)], 1)
        for h in range(2):
            sums[i].ride(h, products[h * S : (h + 1) * S])
        sums[i].produce(lambda c: nt(gp_low, w_up[pl.ds(c, 512)]))
        hidden_low[at] = hidden.astype(bf16)
        for grad, left in ((down, hidden), (up[0], gp0), (up[1], gp1)):
            grad.left[:, at] = left.T.astype(bf16)
    down.start()
    columns_second.start()
    for grad in up:
        grad.start()
    sums[0].middle()
    down.compute()
    sums[1].middle()
    up[0].compute()

    gathers, gain_sum = [], jnp.zeros((1, W), f32)
    gain = gains[1:2].astype(f32)
    for i, at in enumerate(streams):
        grad_n, q = sums[i].end()
        v = mid_own[at].astype(bf16).astype(f32)
        s = scale2[at]
        grad_middle_own = cot[at].astype(f32) + s * gain * grad_n - v * s * s * q * (1.0 / D)
        gmid_own[at] = grad_middle_own
        low = grad_middle_own.astype(bf16)
        for h in range(2):
            gm_g[i, h, x, z] = low[h * S : (h + 1) * S]
        gathers.append(Gather(gm_g.at[i], gm_v.at[i], (S, S)))
        gain_sum += jnp.sum(grad_n * v * s, axis=0, keepdims=True)
    mine = small_own
    mine[...] = jnp.zeros((16, 256), f32)
    mine[1:2, :W] = gain_sum
    gathers[0].forward()
    up[1].compute()
    down.pass_on()
    gathers[1].forward()
    up[0].pass_on()
    scatter_out = Scatter(part_refs(0))
    scatter_out.produce(lambda c: nn(hidden_low[...], w_down[:, pl.ds(c, 512)]), launch=False)
    for i, at in enumerate(streams):
        gathers[i].end()
        dense(gm_g.at[i], gm_d, at)
        grad_mixed = nt(gm_d[at], w_out[...])[:, :C]
        grad_y_s[at] = dgel[at] * state[at] * grad_mixed
        grad_state_s[at] = gel[at] * grad_mixed
        if i == 0:
            for g in FAR_FIRST + (0,):
                scatter_out.launch(g, (0, 1))
    grad_y, grad_state = grad_y_s[...], grad_state_s[...]

    pad_a[pl.ds(0, T)] = coef[...]
    pad_a[pl.ds(T, 8)] = jnp.ones((8, C), f32)
    A, B = scan(pad_a[pl.ds(1, T)], grad_state, True)
    rev_s[0:1, :C] = through[T - 1 :]
    rev_s[1:2, :C] = coef[0:1] * B[0:1]
    carries = Group()
    for d in (2, 1, 3):
        send(rev_s, rev_r.at[d - 1], on_seq(d), carries, misc)
    columns_gm.start()
    up[1].pass_on()
    out.start(mixed_t)
    branches[0].start(transposed(grad_y).astype(bf16))
    out.compute()
    branches[0].compute()
    cv_t = transposed(conv[...]).astype(bf16)
    carries.wait()
    total = B + A * fold(rev_r, True)
    a, r_gate, i_gate, root, cv = aa[...], rr[...], ii[...], qq[...], conv[...]
    t_i = total * i_gate
    d_log = total * prev[pl.ds(7, T)] * coef[...] - t_i * cv * (a * a / root)
    d_gate = d_log * r_gate
    mine[9:10, :C] = -8.0 * sigmoid(decay[...]) * jnp.sum(d_gate, axis=0, keepdims=True)
    gpre0 = -8.0 * rate * d_gate * (1.0 - r_gate)
    direct = t_i * root
    gpre1 = direct * cv * (1.0 - i_gate)
    low0, low1 = gpre0.astype(bf16), gpre1.astype(bf16)
    mine[7:8, :C] = jnp.sum(low0.astype(f32), axis=0, keepdims=True)
    mine[8:9, :C] = jnp.sum(low1.astype(f32), axis=0, keepdims=True)
    grad_conv = direct + nt(low0, gates[0, 0]) + nt(low1, gates[1, 0])
    mine[6:7, :C] = jnp.sum(grad_conv, axis=0, keepdims=True)
    edge = jnp.zeros((8, C), f32)
    grad_inner = jnp.zeros((T, C), f32)
    for k in range(4):
        weighted = grad_conv if k == 0 else masks[k - 1] * grad_conv
        mine[2 + k : 3 + k, :C] = jnp.sum(weighted * ext[pl.ds(8 - k, T)], axis=0, keepdims=True)
        if k == 0:
            pad_a[pl.ds(0, 8)] = jnp.zeros((8, C), f32)
            pad_a[pl.ds(8 + T, 8)] = jnp.zeros((8, C), f32)
        pad_a[pl.ds(8, T)] = conv_w[k : k + 1] * weighted
        edge += pad_a[pl.ds(k, 8)]
        grad_inner += pad_a[pl.ds(8 + k, T)]
    back_s[:, :C] = edge
    back = send_one(back_s, back_r, on_seq(-1))
    gg[0, :, :C] = nn(cv_t, low0).astype(bf16)
    gg[1, :, :C] = nn(cv_t, low1).astype(bf16)
    gg_pair = send_one(gg.at[1 - core], gg_r, other)
    gg_all = Group()
    lhs[:, :C] = grad_y.astype(bf16)
    lhs[:, CP : CP + C] = grad_inner.astype(bf16)
    scatter = Scatter(part_refs(1), True, True)
    tp[:, :C] = grad_y * p0[...] + grad_inner * p1[...]
    scatter.ride(0, tp[pl.ds(0, H), :W] + tp[pl.ds(0, H), W:])

    scatter.produce(lambda at: nn(lhs[...], w_branch[:, pl.ds(at, 512)]))
    small_pair = send_one(small_own, small_mate, other)
    gg_pair.wait()
    gg_y[y] = (gg[core].astype(f32) + gg_r[...].astype(f32)).astype(bf16)
    for d in FAR_FIRST:
        send(gg_y.at[y], gg_y.at[y], on_y(d), gg_all, misc)
    back.wait()
    ext[pl.ds(0, T)] = grad_inner
    ext[pl.ds(T - 8, 8)] = grad_inner[T - 8 :] + back_r[:, :C]
    grad_inner = ext[pl.ds(0, T)]
    tp[:, :C] = grad_y * p0[...] + grad_inner * p1[...]
    scatter.ride(1, tp[pl.ds(H, H), :W] + tp[pl.ds(H, H), W:])
    late = pl.ds(T - LATE, LATE)
    lhs[late, CP : CP + C] = grad_inner[T - LATE :].astype(bf16)
    scatter.produce_late(lambda at: nn(lhs[late], w_branch[:, pl.ds(at, 512)]))
    branches[1].start(transposed(grad_inner).astype(bf16))
    others = ((2, False), (2, True), (1, False), (1, True), (3, False), (3, True), (0, False))
    smalls, gain_sums = Group(), Group()
    out.pass_on()
    branches[0].pass_on()
    small_pair.wait()
    small[y] = small_own[...] + small_mate[...]
    for d in FAR_FIRST:
        send(small.at[y], small.at[y], on_y(d), smalls, misc)
    scatter.middle(((1, branches[1].compute_direct),))
    scatter_out.middle()
    o_down[...] = down.end()
    for k in range(2):
        o_up[k] = up[k].end().T


    grad_n, q = scatter.end()
    v = tokens[...].astype(f32)
    s = scale1[...]
    gain = gains[0:1].astype(f32)
    mine = gain_one.at[dp * 4 + seq]
    mine[...] = jnp.broadcast_to(jnp.sum(grad_n * v * s, axis=0, keepdims=True), (8, W))
    for d, same in others:
        send(mine, mine, on_y(d, same), gain_sums, misc)
    gg_all.wait()
    gg_f[core] = gg_y[0].astype(f32) + gg_y[1].astype(f32) + gg_y[2].astype(f32) + gg_y[3].astype(f32)
    gg_share = send_one(gg_f.at[core], gg_f.at[core], other)
    o_tokens[...] = gmid_own[...] + s * gain * grad_n - v * s * s * q * (1.0 / D)
    o_out[...] = out.end()
    result, _ = scatter_out.end()
    o_block[...] = (mid_own[...] + result).astype(bf16)
    o_branch[0] = branches[0].end()
    o_branch[1] = branches[1].end_direct()
    gg_share.wait()
    for k in range(2):
        o_gates[k, 0] = gg_f[k, :, :C]
    smalls.wait()
    total = small[0]
    for j in range(1, 4):
        total += small[j]
    o_gains[1:2] = total[1:2, :W]
    o_conv[...] = total[2:6, :C]
    o_bias[...] = total[6:9, :C]
    o_decay[...] = total[9:10, :C]
    gain_sums.wait()
    total = gain_one[0, 0:1]
    for j in range(1, 8):
        total += gain_one[j, 0:1]
    o_gains[0:1] = total
    finish()


def hand_over(*refs):
    n = 12
    copies = [pltpu.make_async_copy(refs[i], refs[n + i], refs[-1].at[i]) for i in range(n)]
    for copy in copies:
        copy.start()
    for copy in copies:
        copy.wait()


def on_device(
    tokens, doc_lengths, cotangent, norm_gains, w_branch, conv_weight, lru_bias, decay, gate_weights, w_out, w_up, w_down
):
    def shape(dims, kind=f32):
        return jax.ShapeDtypeStruct(dims, kind)

    def vmem(*dims):
        return pltpu.VMEM(dims, f32)

    def low(*dims):
        return pltpu.VMEM(dims, bf16)

    near, far = pl.BlockSpec(memory_space=pltpu.VMEM), pl.BlockSpec(memory_space=pl.ANY)
    outs = [
        shape((T, W), bf16), shape((T, W)), shape((2, W)), shape((2, C, 256)), shape((4, C)), shape((3, C)),
        shape((1, C)), shape((2, 1, C, C)), shape((C, 256)), shape((2, 256, F)), shape((F, 256)), shape((1, C)),
    ]
    scratch = (
        [low(T, W), low(T, W), low(2 * CP, D), low(2, 1, C, C), low(CP, D), low(D, 2 * F), low(F, D)]
        + ([low(2, 4, 4, H + Q, W), low(2, 4, 4, H, W)] + [low(2, 2, 4, 4, S, W)] * 2) * 2 + [low(T, D)] * 4
        + [low(4, 2, 4, 4, S + Q, W)] * 2 + [low(4, 2, 4, S + Q, W)] * 2
        + [low(2, 2, 4, 4, H + Q, W)] * 2 + [low(2, 2, 4, H + Q, W)] * 2
        + [low(T, F), vmem(T, C), vmem(T, C)]
        + [vmem(T + 8, C)] + [vmem(T, C)] * 13 + [vmem(T + 8, C), vmem(2 * H + T, C), vmem(2 * H + T, C), vmem(T, T)]
        + [vmem(T, F), vmem(T, W), vmem(T, W), vmem(T, W), vmem(T, W)]
        + [low(4, 4, 2 * T, 256)]
        + [low(3, F, 2 * T), low(3, 4, F, 256), low(3, F, 256), low(3, 2, F, 256)]
        + [low(3, C, 2 * T), low(3, 4, C, 256), low(3, C, 256), low(3, 3, C, 256), low(T, 2 * CP)]
        + [vmem(8, 256)] * 4 + [vmem(8, 256), vmem(3, 8, 256)] * 2
        + [low(2, C, 256), low(C, 256), low(4, C, 256), vmem(2, C, 256)]
        + [vmem(16, 256), vmem(16, 256), vmem(4, 16, 256), vmem(8, 8, W), vmem(6144, W)]
        + [pltpu.SemaphoreType.DMA((N_SENT,)), pltpu.SemaphoreType.DMA((N_SEMS,)), pltpu.SemaphoreType.DMA((12,))]
    )
    made = pl.pallas_call(
        kernel,
        out_shape=[pltpu.VMEM(o.shape, o.dtype) for o in outs],
        in_specs=[pl.BlockSpec(memory_space=pltpu.SMEM)] + [near] * 4 + [far] * 7,
        out_specs=[near] * 12,
        scratch_shapes=scratch,
        compiler_params=pltpu.CompilerParams(
            collective_id=0, has_side_effects=True, vmem_limit_bytes=56 * 2**20
        ),
    )(
        doc_lengths, norm_gains, conv_weight, lru_bias, decay.reshape(1, C), tokens.reshape(T, W),
        cotangent.reshape(T, W), jnp.swapaxes(w_branch, 1, 2), gate_weights, w_out, w_up, w_down,
    )
    made = list(pl.pallas_call(
        hand_over,
        out_shape=outs,
        in_specs=[near] * 12,
        out_specs=[far] * 12,
        scratch_shapes=[pltpu.SemaphoreType.DMA((12,))],
        compiler_params=pltpu.CompilerParams(vmem_limit_bytes=2 * 2**20),
    )(*made))
    made[0], made[1] = made[0].reshape(1, T, W), made[1].reshape(1, T, W)
    made[3] = jnp.swapaxes(made[3], 1, 2)
    made[6], made[11] = made[6].reshape(C), made[11].reshape(1, 1, C)
    return tuple(made)


def solution(mesh):
    in_specs = (
        P("dp", "seq", "mp"), P("dp", None), P("dp", "seq", "mp"), P(None, "mp"), P(None, None, "mp"), P(None, "mp"),
        P(None, "mp"), P("mp"), P(None, "mp", None, None), P("mp", None), P(None, None, "mp"), P("mp", None),
    )
    out_specs = (
        P("dp", "seq", "mp"), P("dp", "seq", "mp"), P(None, "mp"), P(None, ("dp", "seq"), "mp"), P(None, "mp"),
        P(None, "mp"), P("mp"), P(None, "mp", None, None), P("mp", ("dp", "seq")), P(None, ("dp", "seq"), "mp"),
        P("mp", ("dp", "seq")), P("dp", "seq", "mp"),
    )
    return jax.shard_map(on_device, mesh=mesh, in_specs=in_specs, out_specs=out_specs, check_vma=False)
```

```python
import jax
import jax.numpy as jnp
from jax import lax
from jax.experimental import pallas as pl
from jax.experimental.pallas import tpu as pltpu
from jax.sharding import PartitionSpec as P

MESH = pl.DeviceIdType.MESH
f32, bf16 = jnp.float32, jnp.bfloat16

T, D, C, F, W = 256, 2048, 176, 384, 128
H = T // 2
S = T // 4
EPS = 1e-06
N_SEMS, N_SENT = 160, 24
CP = 256
LATE = 16
Q = 16
ALPHA, CUBIC = 0.7978845608028654, 0.044715
FAR_FIRST = (2, 1, 3)


def nn(a, b):
    return lax.dot_general(a, b, (((1,), (0,)), ((), ())), preferred_element_type=f32)


def nt(a, b):
    return lax.dot_general(a, b, (((1,), (1,)), ((), ())), preferred_element_type=f32)


def sigmoid(v):
    return 1.0 / (1.0 + jnp.exp(-v))


def gelu_both(v):
    square = v * v
    t = jnp.tanh(ALPHA * v * (1.0 + CUBIC * square))
    half = 0.5 * (1.0 + t)
    return v * half, half + 0.5 * v * (1.0 - t * t) * ALPHA * (1.0 + 3.0 * CUBIC * square)


def rider_tile(row):
    if row.shape[1] < W:
        row = jnp.concatenate([row, jnp.zeros((1, W - row.shape[1]), f32)], 1)
    high = row.astype(bf16).astype(f32)
    index = lax.broadcasted_iota(jnp.int32, (Q, W), 0)
    return jnp.where(index == 0, high, jnp.where(index == 1, row - high, 0.0)).astype(bf16)


def kernel(
    lengths, gains, conv_w, bias, decay, hbm_tokens, hbm_cot, hbm_branch, hbm_gates, hbm_out, hbm_up, hbm_down,
    o_block, o_tokens, o_gains, o_branch, o_conv, o_bias, o_decay, o_gates, o_out, o_up, o_down, o_states,
    tokens, cot, w_branch, gates, w_out, w_up, w_down,
    tok_g, cot_g, mid_g, gm_g, tok_v, cot_v, mid_v, gm_v, first, second, cot_d, gm_d,
    part_s, r1_s, s2_s, r2_s, part_b, r1_b, s2_b, r2_b, hidden_low, grad_y_s, grad_state_s,
    ext, conv, aa, rr, ii, qq, coef, through, local, p0, p1, gel, dgel, state, prev, pad_a, pad_b, tp,
    ghid, mid_own, gmid_own, scale1, scale2,
    blocks, left_mlp, g_mlp, relay_mlp, y_mlp, left_rec, g_rec, relay_rec, y_rec, lhs,
    halo_s, halo_r, back_s, back_r, car_s, car_r, rev_s, rev_r,
    gg, gg_r, gg_y, gg_f, small_own, small_mate, small, gain_one, ruler,
    send_sems, recv_sems, copy_sems,
):
    me, seq, dp = lax.axis_index("mp"), lax.axis_index("seq"), lax.axis_index("dp")
    x, z = me // 4, me % 4
    core, y = seq % 2, (seq // 2) * 2 + dp

    def turn(value, by):
        return lax.rem(value + by + 4, 4)

    mate = (seq // 2) * 2 + (1 - core)

    def on_x(d):
        return {"mp": turn(x, d) * 4 + z, "seq": mate}

    def on_z(d):
        return {"mp": x * 4 + turn(z, d), "seq": mate}

    def on_y(d, same=True):
        there = turn(y, d)
        return {"dp": there % 2, "seq": (there // 2) * 2 + (core if same else 1 - core)}

    def on_seq(d):
        return {"seq": turn(seq, d)}

    other = on_y(0, False)

    groups, sources = [], []

    def wait_bytes(sem, size):
        ref = ruler.at[pl.ds(0, size // (4 * W))]
        pltpu.make_async_copy(ref, ref, sem).wait()

    class Group:
        def __init__(self, kin=groups):
            self.i, self.size, self.done = len(kin), 0, False
            kin.append(self)

        def wait(self):
            if not self.done:
                self.done = True
                wait_bytes(recv_sems.at[self.i], self.size)

    def send(src, dst, where, group, source):
        size = src.dtype.itemsize
        for dim in src.shape:
            size *= dim
        group.size += size
        source.size += size
        pltpu.make_async_remote_copy(
            src_ref=src, dst_ref=dst, send_sem=send_sems.at[source.i], recv_sem=recv_sems.at[group.i],
            device_id=where, device_id_type=MESH,
        ).start()

    def send_one(src, dst, where):
        group = Group()
        send(src, dst, where, group, misc)
        return group

    misc = Group(sources)

    barrier = pltpu.get_barrier_semaphore()
    partners = [on_x(d) for d in (1, 2, 3)] + [on_z(d) for d in (1, 2, 3)] + [on_y(d) for d in (1, 2, 3)]
    partners += [on_y(d, False) for d in (0, 1, 2, 3)]
    for where in partners:
        pl.semaphore_signal(barrier, inc=1, device_id=where, device_id_type=MESH)

    loads = []

    def load(src, dst):
        copy = pltpu.make_async_copy(src, dst, copy_sems.at[len(loads)])
        copy.start()
        loads.append(copy)
        return copy

    load_tokens, load_cot = load(hbm_tokens, tokens), load(hbm_cot, cot)
    load_branch = [load(hbm_branch.at[k], w_branch.at[pl.ds(k * CP, C)]) for k in range(2)]
    load_gates, load_out = load(hbm_gates, gates), load(hbm_out, w_out.at[pl.ds(0, C)])
    load_down = load(hbm_down, w_down)
    load_up = [load(hbm_up.at[k], w_up.at[:, pl.ds(k * F, F)]) for k in range(2)]
    for rows in (w_branch.at[pl.ds(C, CP - C)], w_branch.at[pl.ds(CP + C, CP - C)], w_out.at[pl.ds(C, CP - C)], lhs):
        rows[...] = jnp.zeros(rows.shape, bf16)

    def finish():
        for group in groups:
            group.wait()
        for source in sources:
            wait_bytes(send_sems.at[source.i], source.size)

    def axis_of(h, phase):
        return (on_x, on_z)[(h + phase) % 2]

    def place(h, first_hop):
        return (turn(x, first_hop), z) if h == 0 else (x, turn(z, first_hop))

    class Gather:
        def __init__(self, buf, via, rows):
            self.buf, self.via, self.rows = buf, via, rows
            self.arrivals, self.last, self.source = [], Group(), Group(sources)
            for d in (1, 3, 2, 0):
                for h in range(2):
                    group = Group()
                    send(self.view(buf, h, 0), self.view(via, h, 0), axis_of(h, 0)(d), group, self.source)
                    self.arrivals.append((h, d, group))

        def view(self, buf, h, d):
            return buf.at[h, *place(h, -d), pl.ds(0, self.rows[h])]

        def forward(self):
            for h, d, group in self.arrivals[-2:] + self.arrivals[:-2]:
                group.wait()
                src, dst = self.view(self.via, h, d), self.view(self.buf, h, d)
                for e in (1, 3, 2):
                    send(src, dst, axis_of(h, 1)(e), self.last, self.source)
                if d:
                    send(src, dst, other, self.last, self.source)

        def end(self):
            self.last.wait()

    class Scatter:
        def __init__(self, refs, rider=False, late=False):
            self.part, self.r1, self.s2, self.r2 = refs
            self.size = self.part.shape[3] - Q
            self.rider, self.late = rider, late
            self.source = Group(sources)
            self.hop1 = {(h, r): Group() for h in range(2) for r in range(4)}
            self.hop2 = {h: Group() for h in range(2)}
            if late:
                self.hop1.update({(2, r): Group() for r in range(4)})
                self.hop2[2] = Group()

        def rows(self, h, rider):
            first, size = ((0, self.size), (0, self.size - LATE if self.late else self.size), (self.size - LATE, LATE))[h]
            return pl.ds(first, size + (Q if rider and self.rides(h) else 0))

        def rides(self, h):
            return self.rider and h in ((0, 2) if self.late else (0, 1))

        def launch(self, g, halves):
            for h in halves:
                for k in FAR_FIRST + (0,):
                    if h == 0 or k:
                        r, d = (g, k) if h == 0 else (k, g)
                        self.pass_part(h, r, d)
            if g == 0 and not (self.late and 0 in halves):
                for h in (1, 2) if self.late else (1,):
                    for k in FAR_FIRST + (0,):
                        self.pass_part(h, 0, k)

        def pass_part(self, h, r, d):
            half = min(h, 1)
            spot = (turn(x, r), turn(z, d)) if half == 0 else (turn(x, d), turn(z, r))
            at = self.rows(h, r == 2)
            src, dst = self.part.at[half, *spot, at], self.r1.at[half, r, d, at]
            send(src, dst, axis_of(half, 1)(d), self.hop1[h, r], self.source)

        def produce(self, columns, halfway=None, launch=True):
            for g in FAR_FIRST + (0,):
                if g == 1 and halfway:
                    halfway()
                there = turn(x, g)
                low = columns(pl.multiple_of(there * 512, 512)).astype(bf16)
                for c in range(4):
                    piece = low[:, c * W : (c + 1) * W]
                    self.part[0, there, c, pl.ds(0, self.size)] = piece[: self.size]
                    at = self.rows(1, False)
                    self.part[1, there, c, at] = piece[self.size : self.size + at.size]
                if launch and g in (2, 0):
                    for k in (2,) if g == 2 else (1, 3, 0):
                        self.launch(k, (0, 1))

        def produce_late(self, columns):
            for g in FAR_FIRST + (0,):
                there = turn(x, g)
                low = columns(pl.multiple_of(there * 512, 512)).astype(bf16)
                for c in range(4):
                    self.part[1, there, c, self.rows(2, False)] = low[:, c * W : (c + 1) * W]
                self.launch(g, (2,))

        def ride(self, h, products):
            tile = rider_tile(jnp.sum(products.T, axis=0, keepdims=True))
            for c in range(4):
                spot = (0, turn(x, 2), c) if h == 0 else (1, c, turn(z, 2))
                self.part[*spot, pl.ds(self.size, Q)] = tile

        def step(self, h, r):
            half, extra = min(h, 1), pl.ds(self.size, Q)
            self.hop1[h, r].wait()

            def total(at):
                parts = [self.r1[half, r, d, at].astype(f32) for d in range(4)]
                return (parts[0] + parts[1]) + (parts[2] + parts[3])

            if r == 2 and self.rides(h):
                tile = rider_tile(jnp.sum(total(extra), axis=0, keepdims=True))
                for k in range(4):
                    self.s2[half, k, extra] = tile
            at = self.rows(h, False)
            self.s2[half, r, at] = total(at).astype(bf16)
            at = self.rows(h, True)
            send(self.s2.at[half, r, at], self.r2.at[half, r, at], axis_of(half, 0)(r), self.hop2[h], self.source)

        def middle(self, between=()):
            order = ((0, 2), (0, 1), (1, 2), (0, 3), (1, 1), (1, 3))
            if self.late:
                order += ((2, 2), (2, 1), (2, 3), (2, 0))
            order += ((0, 0), (1, 0))
            for i, (h, r) in enumerate(order):
                self.step(h, r)
                for work in between:
                    if work[0] == i:
                        for call in work[1:]:
                            call()

        def end(self):
            out, column = [], []
            for h in sorted(self.hop2):
                half, at = min(h, 1), self.rows(h, False)
                self.hop2[h].wait()
                parts = [self.r2[half, r, at].astype(f32) for r in range(4)]
                out.append((parts[0] + parts[1]) + (parts[2] + parts[3]))
                if self.rides(h):
                    rider = self.r2[half, 0, pl.ds(self.size, Q)].astype(f32)
                    for r in range(1, 4):
                        rider += self.r2[half, r, pl.ds(self.size, Q)].astype(f32)
                    row = jnp.sum(rider, axis=0, keepdims=True)
                    column.append(jnp.broadcast_to(row, (W, W)).T[: self.size])
            return jnp.concatenate(out, 0), (jnp.concatenate(column, 0) if column else None)

    def chunk(buf, c, size):
        return jnp.concatenate([buf[h, c // 4, c % 4, pl.ds(0, size)] for h in range(2)], 0)

    def gain_row(k, c):
        return tok_g[1, 0, c // 4, c % 4, pl.ds(S, Q)].astype(f32)[k : k + 1]

    def norm(buf, k, at):
        scale_ref, dst = ((scale1, first), (scale2, second))[k]
        total = jnp.zeros((at.size, W), f32)
        for c in range(16):
            v = chunk(buf, c, at.size // 2).astype(f32)
            total += v * v
        scale = lax.rsqrt(jnp.sum(total, axis=1, keepdims=True) * (1.0 / D) + EPS)
        scale_ref[at] = jnp.broadcast_to(scale, (at.size, W))
        for c in range(16):
            v = chunk(buf, c, at.size // 2).astype(f32)
            dst[at, c * W : (c + 1) * W] = (v * scale_ref[at] * gain_row(k, c)).astype(bf16)

    def dense(buf, dst, at):
        for c in range(16):
            dst[at, c * W : (c + 1) * W] = chunk(buf, c, at.size // 2)

    everything, streams = pl.ds(0, T), [pl.ds(0, H), pl.ds(H, H)]

    def block_at(there, core_there):
        return pl.multiple_of(((there % 2) * 4 + (there // 2) * 2 + core_there) * 256, 256)

    class Columns:
        def __init__(self, i, array):
            self.i, self.array, self.blocks = i, array, blocks.at[i]

        def start(self):
            self.group, source = Group(), Group(sources)
            for there in range(4):
                src = self.array.at[:, pl.ds(block_at(there, 1 - core), 256)]
                send(src, self.blocks.at[there, pl.ds(T, T)], other, self.group, source)
                src = self.array.at[:, pl.ds(block_at(there, core), 256)]
                pltpu.make_async_copy(src, self.blocks.at[there, pl.ds(0, T)], copy_sems.at[8 + self.i]).start()

        def ready(self):
            if not self.group.done:
                wait_bytes(copy_sems.at[8 + self.i], self.group.size)
            self.group.wait()

    class WeightGrad:
        def __init__(self, columns, left, g, relay, into):
            self.columns, self.left = columns, left
            self.g, self.relay, self.into, rows = g, relay, into, left.shape[0]
            cut = rows // 32 * 16 + (16 if rows % 32 else 0)
            self.a, self.b = pl.ds(0, cut), pl.ds(cut, rows - cut)

        def start(self, left=None):
            mine, peer = self.left.at[:, pl.ds(0, T)], self.left.at[:, pl.ds(T, T)]
            if left is not None:
                mine[...] = left
            self.source, self.pair = Group(sources), Group()
            send(mine, peer, other, self.pair, self.source)

        def make(self):
            self.pair.wait()
            self.columns.ready()
            self.last = Group()
            for there in range(4):
                self.g[there] = nn(self.left[...], self.columns.blocks[there]).astype(bf16)

        def compute(self):
            self.make()
            self.relayed = Group()
            far = turn(y, 2)
            send(self.g.at[far, self.a], self.relay.at[self.a], on_y(1), self.relayed, self.source)
            send(self.g.at[far, self.b], self.relay.at[self.b], on_y(-1), self.relayed, self.source)
            for k, at in ((1, self.b), (-1, self.a)):
                src = self.g.at[turn(y, k), at]
                send(src, self.into.at[(1 - k) // 2, at], on_y(k), self.last, self.source)

        def pass_on(self):
            self.relayed.wait()
            for k, at in ((1, self.a), (-1, self.b)):
                there = turn(y, k)
                self.g[there, at] = (self.g[there, at].astype(f32) + self.relay[at].astype(f32)).astype(bf16)
                send(self.g.at[there, at], self.into.at[(1 - k) // 2, at], on_y(k), self.last, self.source)

        def end(self):
            self.last.wait()
            return self.g[y].astype(f32) + self.into[0].astype(f32) + self.into[1].astype(f32)

        def compute_direct(self):
            self.make()
            for k in FAR_FIRST:
                send(self.g.at[turn(y, k)], self.into.at[k - 1], on_y(k), self.last, self.source)

        def end_direct(self):
            return self.end() + self.into[2].astype(f32)

    def transposed(value):
        tp[:, :C] = value
        return tp[...].T[:C]

    columns_cot, columns_second, columns_gm, columns_first = [
        Columns(i, array) for i, array in enumerate((cot_d, second, gm_d, first))
    ]

    def weight_grad(columns, i, rows):
        refs = (left_mlp, g_mlp, relay_mlp, y_mlp) if rows == F else (left_rec, g_rec, relay_rec, y_rec)
        return WeightGrad(columns, *[ref.at[i] for ref in refs])

    down, up = weight_grad(columns_cot, 0, F), [weight_grad(columns_second, 1 + k, F) for k in range(2)]
    out, branches = weight_grad(columns_gm, 0, C), [weight_grad(columns_first, 1 + k, C) for k in range(2)]

    gain_tile = jnp.concatenate([gains[...].astype(f32), jnp.zeros((Q - 2, W), f32)], 0).astype(bf16)
    tok_g[1, 0, x, z, pl.ds(S, Q)] = gain_tile
    load_tokens.wait()
    load_cot.wait()
    for h in range(2):
        for i in range(2):
            tok_g[i, h, x, z, pl.ds(0, S)] = tokens[pl.ds(i * H + h * S, S)]
        cot_g[h, x, z] = cot[pl.ds(h * H, H)]
    tp[...] = jnp.zeros_like(tp)
    pl.semaphore_wait(barrier, len(partners))
    tok_gathers = {i: Gather(tok_g.at[i], tok_v.at[i], (S + Q if i else S, S)) for i in (1, 0)}
    for i in (1, 0):
        tok_gathers[i].forward()
    cot_gather = Gather(cot_g, cot_v, (H, H))

    place_here = lax.broadcasted_iota(jnp.int32, (T, 1), 0) + seq * T
    start, begins = 0, [0]
    for j in range(3):
        start = start + lengths[0, j]
        begins.append(start)

    def begin_at(p):
        hit = p == begins[0]
        for b in begins[1:]:
            hit = jnp.logical_or(hit, p == b)
        return hit

    not_reset = jnp.where(begin_at(place_here), 0.0, 1.0)
    masks = [not_reset]
    for k in (1, 2):
        masks.append(masks[-1] * jnp.where(begin_at(place_here - k), 0.0, 1.0))

    for i in (1, 0):
        tok_gathers[i].end()
        at = streams[i]
        norm(tok_g.at[i], 0, at)
        if i:
            for copy in load_branch + [load_gates]:
                copy.wait()
        value = nt(first[at], w_branch[pl.ds(CP, CP)])[:, :C]
        p1[at] = value
        inner = value.astype(bf16).astype(f32)
        ext[pl.ds(8 + i * H, H)] = inner
        if i:
            halo_s[:, :C] = inner[H - 8 :]
            halo = send_one(halo_s, halo_r, on_seq(1))
    cot_gather.forward()
    columns_first.start()
    halo.wait()
    ext[pl.ds(0, 8)] = halo_r[:, :C]
    total = bias[0:1] + conv_w[0:1] * ext[pl.ds(8, T)]
    for k in (1, 2, 3):
        total = total + conv_w[k : k + 1] * (masks[k - 1] * ext[pl.ds(8 - k, T)])
    conv[...] = total
    conv_low = total.astype(bf16)
    rate = jax.nn.softplus(decay[...])
    r_gate = sigmoid(nn(conv_low, gates[0, 0]) + bias[1:2])
    rr[...] = r_gate
    a = jnp.exp(-8.0 * r_gate * rate)
    aa[...] = a
    coef[...] = a * not_reset
    i_gate = sigmoid(nn(conv_low, gates[1, 0]) + bias[2:3])
    ii[...] = i_gate
    root = jnp.sqrt(1.0 - a * a + 0.001)
    qq[...] = root

    def scan(A, B, reverse):
        step = 1
        while step < T:
            for ref, v, fill in ((pad_a, A, 1.0), (pad_b, B, 0.0)):
                ref[pl.ds(H, T)] = v
                ref[pl.ds(H + T if reverse else 0, H)] = jnp.full((H, C), fill, f32)
            at = pl.ds(H + step if reverse else H - step, T)
            B = B + A * pad_b[at]
            A = A * pad_a[at]
            step *= 2
        return A, B

    A, B = scan(coef[...], root * i_gate * conv[...], False)
    through[...] = A
    local[...] = B
    car_s[0:1, :C] = A[T - 1 :]
    car_s[1:2, :C] = B[T - 1 :]
    carries = Group()
    for d in (2, 1, 3):
        send(car_s, car_r.at[d - 1], on_seq(d), carries, misc)
    value = nt(first[...], w_branch[pl.ds(0, CP)])[:, :C]
    p0[...] = value
    act, slope = gelu_both(value)
    gel[...] = act
    dgel[...] = slope
    for copy in [load_out, load_down] + load_up:
        copy.wait()
    carries.wait()

    def fold(got, reverse):
        carried = jnp.zeros((1, C), f32)
        for d in (3, 2, 1):
            here = (seq + d < 4) if reverse else (seq - d >= 0)
            slot = 4 - d if reverse else d
            new = got[slot - 1, 0:1, :C] * carried + got[slot - 1, 1:2, :C]
            carried = jnp.where(here, new, carried)
        return carried

    carried = fold(car_r, False)
    value = local[...] + through[...] * carried
    state[...] = value
    prev[pl.ds(8, T)] = value
    prev[7:8] = carried
    mixed = gel[...] * value
    lhs[:, :C] = mixed.astype(bf16)

    def stream_refs(i):
        return [ref.at[i] for ref in (part_s, r1_s, s2_s, r2_s)]

    def part_refs(i):
        return [ref.at[i] for ref in (part_b, r1_b, s2_b, r2_b)]

    sums = [Scatter(stream_refs(i)) for i in range(2)]
    for at, scatter in zip(streams, sums):
        scatter.produce(lambda c: nn(lhs[at, :CP], w_out[:, pl.ds(c, 512)]))
    o_states[...] = value[T - 1 :]
    mixed_t = transposed(mixed).astype(bf16)
    cot_gather.end()
    dense(cot_g, cot_d, everything)
    sums[0].middle()
    columns_cot.start()
    sums[1].middle()
    gathers = []
    for i, at in enumerate(streams):
        branch, _ = sums[i].end()
        middle = tokens[at].astype(f32) + branch
        mid_own[at] = middle
        middle_low = middle.astype(bf16)
        for h in range(2):
            mid_g[i, h, x, z] = middle_low[h * S : (h + 1) * S]
        gathers.append(Gather(mid_g.at[i], mid_v.at[i], (S, S)))
    gathers[0].forward()
    ghid[...] = nt(cot_d[...], w_down[...])
    gathers[1].forward()

    sums = [Scatter(stream_refs(2 + i), True) for i in range(2)]
    for i, at in enumerate(streams):
        gathers[i].end()
        norm(mid_g.at[i], 1, at)
        pair = nn(second[at], w_up[...])
        pair0, pair1 = pair[:, :F], pair[:, F:]
        act, slope = gelu_both(pair0)
        hidden = act * pair1
        gh = ghid[at]
        gp0 = slope * pair1 * gh
        gp1 = act * gh
        products = gp0 * pair0 + gp1 * pair1
        products = products[:, :W] + products[:, W : 2 * W] + products[:, 2 * W :]
        gp_low = jnp.concatenate([gp0.astype(bf16), gp1.astype(bf16)], 1)
        for h in range(2):
            sums[i].ride(h, products[h * S : (h + 1) * S])
        sums[i].produce(lambda c: nt(gp_low, w_up[pl.ds(c, 512)]))
        hidden_low[at] = hidden.astype(bf16)
        for grad, left in ((down, hidden), (up[0], gp0), (up[1], gp1)):
            grad.left[:, at] = left.T.astype(bf16)
    down.start()
    columns_second.start()
    for grad in up:
        grad.start()
    sums[0].middle()
    down.compute()
    sums[1].middle()
    up[0].compute()

    gathers, gain_sum = [], jnp.zeros((1, W), f32)
    gain = gains[1:2].astype(f32)
    for i, at in enumerate(streams):
        grad_n, q = sums[i].end()
        v = mid_own[at].astype(bf16).astype(f32)
        s = scale2[at]
        grad_middle_own = cot[at].astype(f32) + s * gain * grad_n - v * s * s * q * (1.0 / D)
        gmid_own[at] = grad_middle_own
        low = grad_middle_own.astype(bf16)
        for h in range(2):
            gm_g[i, h, x, z] = low[h * S : (h + 1) * S]
        gathers.append(Gather(gm_g.at[i], gm_v.at[i], (S, S)))
        gain_sum += jnp.sum(grad_n * v * s, axis=0, keepdims=True)
    mine = small_own
    mine[...] = jnp.zeros((16, 256), f32)
    mine[1:2, :W] = gain_sum
    gathers[0].forward()
    up[1].compute()
    down.pass_on()
    gathers[1].forward()
    up[0].pass_on()
    scatter_out = Scatter(part_refs(0))
    scatter_out.produce(lambda c: nn(hidden_low[...], w_down[:, pl.ds(c, 512)]), launch=False)
    for i, at in enumerate(streams):
        gathers[i].end()
        dense(gm_g.at[i], gm_d, at)
        grad_mixed = nt(gm_d[at], w_out[...])[:, :C]
        grad_y_s[at] = dgel[at] * state[at] * grad_mixed
        grad_state_s[at] = gel[at] * grad_mixed
        if i == 0:
            for g in FAR_FIRST + (0,):
                scatter_out.launch(g, (0, 1))
    grad_y, grad_state = grad_y_s[...], grad_state_s[...]

    pad_a[pl.ds(0, T)] = coef[...]
    pad_a[pl.ds(T, 8)] = jnp.ones((8, C), f32)
    A, B = scan(pad_a[pl.ds(1, T)], grad_state, True)
    rev_s[0:1, :C] = through[T - 1 :]
    rev_s[1:2, :C] = coef[0:1] * B[0:1]
    carries = Group()
    for d in (2, 1, 3):
        send(rev_s, rev_r.at[d - 1], on_seq(d), carries, misc)
    columns_gm.start()
    up[1].pass_on()
    out.start(mixed_t)
    branches[0].start(transposed(grad_y).astype(bf16))
    out.compute()
    branches[0].compute()
    cv_t = transposed(conv[...]).astype(bf16)
    carries.wait()
    total = B + A * fold(rev_r, True)
    a, r_gate, i_gate, root, cv = aa[...], rr[...], ii[...], qq[...], conv[...]
    t_i = total * i_gate
    d_log = total * prev[pl.ds(7, T)] * coef[...] - t_i * cv * (a * a / root)
    d_gate = d_log * r_gate
    mine[9:10, :C] = -8.0 * sigmoid(decay[...]) * jnp.sum(d_gate, axis=0, keepdims=True)
    gpre0 = -8.0 * rate * d_gate * (1.0 - r_gate)
    direct = t_i * root
    gpre1 = direct * cv * (1.0 - i_gate)
    low0, low1 = gpre0.astype(bf16), gpre1.astype(bf16)
    mine[7:8, :C] = jnp.sum(low0.astype(f32), axis=0, keepdims=True)
    mine[8:9, :C] = jnp.sum(low1.astype(f32), axis=0, keepdims=True)
    grad_conv = direct + nt(low0, gates[0, 0]) + nt(low1, gates[1, 0])
    mine[6:7, :C] = jnp.sum(grad_conv, axis=0, keepdims=True)
    edge = jnp.zeros((8, C), f32)
    grad_inner = jnp.zeros((T, C), f32)
    for k in range(4):
        weighted = grad_conv if k == 0 else masks[k - 1] * grad_conv
        mine[2 + k : 3 + k, :C] = jnp.sum(weighted * ext[pl.ds(8 - k, T)], axis=0, keepdims=True)
        if k == 0:
            pad_a[pl.ds(0, 8)] = jnp.zeros((8, C), f32)
            pad_a[pl.ds(8 + T, 8)] = jnp.zeros((8, C), f32)
        pad_a[pl.ds(8, T)] = conv_w[k : k + 1] * weighted
        edge += pad_a[pl.ds(k, 8)]
        grad_inner += pad_a[pl.ds(8 + k, T)]
    back_s[:, :C] = edge
    back = send_one(back_s, back_r, on_seq(-1))
    lhs[:, :C] = grad_y.astype(bf16)
    lhs[:, CP : CP + C] = grad_inner.astype(bf16)
    scatter = Scatter(part_refs(1), True, True)
    tp[:, :C] = grad_y * p0[...] + grad_inner * p1[...]
    scatter.ride(0, tp[pl.ds(0, H), :W] + tp[pl.ds(0, H), W:])

    gg_pairs, gg_all = [], Group()

    def gates_grad():
        gg[0, :, :C] = nn(cv_t, low0).astype(bf16)
        gg[1, :, :C] = nn(cv_t, low1).astype(bf16)
        gg_pairs.append(send_one(gg.at[1 - core], gg_r, other))

    scatter.produce(lambda at: nn(lhs[...], w_branch[:, pl.ds(at, 512)]), gates_grad)
    small_pair = send_one(small_own, small_mate, other)
    gg_pairs[0].wait()
    gg_y[y] = (gg[core].astype(f32) + gg_r[...].astype(f32)).astype(bf16)
    for d in FAR_FIRST:
        send(gg_y.at[y], gg_y.at[y], on_y(d), gg_all, misc)
    back.wait()
    ext[pl.ds(0, T)] = grad_inner
    ext[pl.ds(T - 8, 8)] = grad_inner[T - 8 :] + back_r[:, :C]
    grad_inner = ext[pl.ds(0, T)]
    tp[:, :C] = grad_y * p0[...] + grad_inner * p1[...]
    scatter.ride(1, tp[pl.ds(H, H), :W] + tp[pl.ds(H, H), W:])
    late = pl.ds(T - LATE, LATE)
    lhs[late, CP : CP + C] = grad_inner[T - LATE :].astype(bf16)
    scatter.produce_late(lambda at: nn(lhs[late], w_branch[:, pl.ds(at, 512)]))
    branches[1].start(transposed(grad_inner).astype(bf16))
    others = ((2, False), (2, True), (1, False), (1, True), (3, False), (3, True), (0, False))
    smalls, gain_sums = Group(), Group()
    out.pass_on()
    branches[0].pass_on()
    small_pair.wait()
    small[y] = small_own[...] + small_mate[...]
    for d in FAR_FIRST:
        send(small.at[y], small.at[y], on_y(d), smalls, misc)
    scatter.middle(((3, branches[1].compute_direct),))
    scatter_out.middle()
    o_down[...] = down.end()
    for k in range(2):
        o_up[k] = up[k].end().T


    grad_n, q = scatter.end()
    v = tokens[...].astype(f32)
    s = scale1[...]
    gain = gains[0:1].astype(f32)
    mine = gain_one.at[dp * 4 + seq]
    mine[...] = jnp.broadcast_to(jnp.sum(grad_n * v * s, axis=0, keepdims=True), (8, W))
    for d, same in others:
        send(mine, mine, on_y(d, same), gain_sums, misc)
    gg_all.wait()
    gg_f[core] = gg_y[0].astype(f32) + gg_y[1].astype(f32) + gg_y[2].astype(f32) + gg_y[3].astype(f32)
    gg_share = send_one(gg_f.at[core], gg_f.at[core], other)
    o_tokens[...] = gmid_own[...] + s * gain * grad_n - v * s * s * q * (1.0 / D)
    o_out[...] = out.end()
    result, _ = scatter_out.end()
    o_block[...] = (mid_own[...] + result).astype(bf16)
    o_branch[0] = branches[0].end()
    o_branch[1] = branches[1].end_direct()
    gg_share.wait()
    for k in range(2):
        o_gates[k, 0] = gg_f[k, :, :C]
    smalls.wait()
    total = small[0]
    for j in range(1, 4):
        total += small[j]
    o_gains[1:2] = total[1:2, :W]
    o_conv[...] = total[2:6, :C]
    o_bias[...] = total[6:9, :C]
    o_decay[...] = total[9:10, :C]
    gain_sums.wait()
    total = gain_one[0, 0:1]
    for j in range(1, 8):
        total += gain_one[j, 0:1]
    o_gains[0:1] = total
    finish()


def hand_over(*refs):
    n = 12
    copies = [pltpu.make_async_copy(refs[i], refs[n + i], refs[-1].at[i]) for i in range(n)]
    for copy in copies:
        copy.start()
    for copy in copies:
        copy.wait()


def on_device(
    tokens, doc_lengths, cotangent, norm_gains, w_branch, conv_weight, lru_bias, decay, gate_weights, w_out, w_up, w_down
):
    def shape(dims, kind=f32):
        return jax.ShapeDtypeStruct(dims, kind)

    def vmem(*dims):
        return pltpu.VMEM(dims, f32)

    def low(*dims):
        return pltpu.VMEM(dims, bf16)

    near, far = pl.BlockSpec(memory_space=pltpu.VMEM), pl.BlockSpec(memory_space=pl.ANY)
    outs = [
        shape((T, W), bf16), shape((T, W)), shape((2, W)), shape((2, C, 256)), shape((4, C)), shape((3, C)),
        shape((1, C)), shape((2, 1, C, C)), shape((C, 256)), shape((2, 256, F)), shape((F, 256)), shape((1, C)),
    ]
    scratch = (
        [low(T, W), low(T, W), low(2 * CP, D), low(2, 1, C, C), low(CP, D), low(D, 2 * F), low(F, D)]
        + ([low(2, 2, 4, 4, S + Q, W), low(2, 4, 4, H, W)] + [low(2, 2, 4, 4, S, W)] * 2) * 2 + [low(T, D)] * 4
        + [low(4, 2, 4, 4, S + Q, W)] * 2 + [low(4, 2, 4, S + Q, W)] * 2
        + [low(2, 2, 4, 4, H + Q, W)] * 2 + [low(2, 2, 4, H + Q, W)] * 2
        + [low(T, F), vmem(T, C), vmem(T, C)]
        + [vmem(T + 8, C)] + [vmem(T, C)] * 13 + [vmem(T + 8, C), vmem(2 * H + T, C), vmem(2 * H + T, C), vmem(T, T)]
        + [vmem(T, F), vmem(T, W), vmem(T, W), vmem(T, W), vmem(T, W)]
        + [low(4, 4, 2 * T, 256)]
        + [low(3, F, 2 * T), low(3, 4, F, 256), low(3, F, 256), low(3, 2, F, 256)]
        + [low(3, C, 2 * T), low(3, 4, C, 256), low(3, C, 256), low(3, 3, C, 256), low(T, 2 * CP)]
        + [vmem(8, 256)] * 4 + [vmem(8, 256), vmem(3, 8, 256)] * 2
        + [low(2, C, 256), low(C, 256), low(4, C, 256), vmem(2, C, 256)]
        + [vmem(16, 256), vmem(16, 256), vmem(4, 16, 256), vmem(8, 8, W), vmem(3072, W)]
        + [pltpu.SemaphoreType.DMA((N_SENT,)), pltpu.SemaphoreType.DMA((N_SEMS,)), pltpu.SemaphoreType.DMA((12,))]
    )
    made = pl.pallas_call(
        kernel,
        out_shape=[pltpu.VMEM(o.shape, o.dtype) for o in outs],
        in_specs=[pl.BlockSpec(memory_space=pltpu.SMEM)] + [near] * 4 + [far] * 7,
        out_specs=[near] * 12,
        scratch_shapes=scratch,
        compiler_params=pltpu.CompilerParams(
            collective_id=0, has_side_effects=True, vmem_limit_bytes=56 * 2**20
        ),
    )(
        doc_lengths, norm_gains, conv_weight, lru_bias, decay.reshape(1, C), tokens.reshape(T, W),
        cotangent.reshape(T, W), jnp.swapaxes(w_branch, 1, 2), gate_weights, w_out, w_up, w_down,
    )
    made = list(pl.pallas_call(
        hand_over,
        out_shape=outs,
        in_specs=[near] * 12,
        out_specs=[far] * 12,
        scratch_shapes=[pltpu.SemaphoreType.DMA((12,))],
        compiler_params=pltpu.CompilerParams(vmem_limit_bytes=2 * 2**20),
    )(*made))
    made[0], made[1] = made[0].reshape(1, T, W), made[1].reshape(1, T, W)
    made[3] = jnp.swapaxes(made[3], 1, 2)
    made[6], made[11] = made[6].reshape(C), made[11].reshape(1, 1, C)
    return tuple(made)


def solution(mesh):
    in_specs = (
        P("dp", "seq", "mp"), P("dp", None), P("dp", "seq", "mp"), P(None, "mp"), P(None, None, "mp"), P(None, "mp"),
        P(None, "mp"), P("mp"), P(None, "mp", None, None), P("mp", None), P(None, None, "mp"), P("mp", None),
    )
    out_specs = (
        P("dp", "seq", "mp"), P("dp", "seq", "mp"), P(None, "mp"), P(None, ("dp", "seq"), "mp"), P(None, "mp"),
        P(None, "mp"), P("mp"), P(None, "mp", None, None), P("mp", ("dp", "seq")), P(None, ("dp", "seq"), "mp"),
        P("mp", ("dp", "seq")), P("dp", "seq", "mp"),
    )
    return jax.shard_map(on_device, mesh=mesh, in_specs=in_specs, out_specs=out_specs, check_vma=False)
```

```python
import jax
import jax.numpy as jnp
from jax import lax
from jax.experimental import pallas as pl
from jax.experimental.pallas import tpu as pltpu
from jax.sharding import PartitionSpec as P

MESH = pl.DeviceIdType.MESH
f32, bf16 = jnp.float32, jnp.bfloat16

T, D, C, F, W = 256, 2048, 176, 384, 128
H = T // 2
S = T // 4
EPS = 1e-06
N_SEMS, N_SENT = 126, 24
CP = 256
LATE = 16
Q = 16
ALPHA, CUBIC = 0.7978845608028654, 0.044715
FAR_FIRST = (2, 1, 3)


def nn(a, b):
    return lax.dot_general(a, b, (((1,), (0,)), ((), ())), preferred_element_type=f32)


def nt(a, b):
    return lax.dot_general(a, b, (((1,), (1,)), ((), ())), preferred_element_type=f32)


def sigmoid(v):
    return 1.0 / (1.0 + jnp.exp(-v))


def gelu_both(v):
    square = v * v
    t = jnp.tanh(ALPHA * v * (1.0 + CUBIC * square))
    half = 0.5 * (1.0 + t)
    return v * half, half + 0.5 * v * (1.0 - t * t) * ALPHA * (1.0 + 3.0 * CUBIC * square)


def rider_tile(row):
    if row.shape[1] < W:
        row = jnp.concatenate([row, jnp.zeros((1, W - row.shape[1]), f32)], 1)
    high = row.astype(bf16).astype(f32)
    index = lax.broadcasted_iota(jnp.int32, (Q, W), 0)
    return jnp.where(index == 0, high, jnp.where(index == 1, row - high, 0.0)).astype(bf16)


def kernel(
    lengths, gains, conv_w, bias, decay, hbm_tokens, hbm_cot, hbm_branch, hbm_gates, hbm_out, hbm_up, hbm_down,
    o_block, o_tokens, o_gains, o_branch, o_conv, o_bias, o_decay, o_gates, o_out, o_up, o_down, o_states,
    tokens, cot, w_branch, gates, w_out, w_up, w_down,
    tok_g, cot_g, mid_g, gm_g, tok_v, cot_v, mid_v, gm_v, first, second, cot_d, gm_d,
    part_s, r1_s, s2_s, r2_s, part_b, r1_b, s2_b, r2_b, hidden_low, grad_y_s, grad_state_s,
    ext, conv, aa, rr, ii, qq, coef, through, local, p0, p1, gel, dgel, state, prev, pad_a, pad_b, tp,
    ghid, mid_own, gmid_own, scale1, scale2,
    blocks, left_mlp, g_mlp, relay_mlp, y_mlp, left_rec, g_rec, relay_rec, y_rec, lhs,
    halo_s, halo_r, back_s, back_r, car_s, car_r, rev_s, rev_r,
    gg, gg_r, gg_y, gg_f, small_own, small_mate, small, gain_one, ruler,
    send_sems, recv_sems, copy_sems,
):
    me, seq, dp = lax.axis_index("mp"), lax.axis_index("seq"), lax.axis_index("dp")
    x, z = me // 4, me % 4
    core, y = seq % 2, (seq // 2) * 2 + dp

    def turn(value, by):
        return lax.rem(value + by + 4, 4)

    mate = (seq // 2) * 2 + (1 - core)

    def on_x(d):
        return {"mp": turn(x, d) * 4 + z, "seq": mate}

    def on_z(d):
        return {"mp": x * 4 + turn(z, d), "seq": mate}

    def on_y(d, same=True):
        there = turn(y, d)
        return {"dp": there % 2, "seq": (there // 2) * 2 + (core if same else 1 - core)}

    def on_seq(d):
        return {"seq": turn(seq, d)}

    other = on_y(0, False)

    groups, sources = [], []

    def wait_bytes(sem, size):
        ref = ruler.at[pl.ds(0, size // (4 * W))]
        pltpu.make_async_copy(ref, ref, sem).wait()

    class Group:
        def __init__(self, kin=groups):
            self.i, self.size, self.done = len(kin), 0, False
            kin.append(self)

        def wait(self):
            if not self.done:
                self.done = True
                wait_bytes(recv_sems.at[self.i], self.size)

    def send(src, dst, where, group, source):
        size = src.dtype.itemsize
        for dim in src.shape:
            size *= dim
        group.size += size
        source.size += size
        pltpu.make_async_remote_copy(
            src_ref=src, dst_ref=dst, send_sem=send_sems.at[source.i], recv_sem=recv_sems.at[group.i],
            device_id=where, device_id_type=MESH,
        ).start()

    def send_one(src, dst, where):
        group = Group()
        send(src, dst, where, group, misc)
        return group

    misc = Group(sources)

    barrier = pltpu.get_barrier_semaphore()
    partners = [on_x(d) for d in (1, 2, 3)] + [on_z(d) for d in (1, 2, 3)] + [on_y(d) for d in (1, 2, 3)]
    partners += [on_y(d, False) for d in (0, 1, 2, 3)]
    for where in partners:
        pl.semaphore_signal(barrier, inc=1, device_id=where, device_id_type=MESH)

    loads = []

    def load(src, dst):
        copy = pltpu.make_async_copy(src, dst, copy_sems.at[len(loads)])
        copy.start()
        loads.append(copy)
        return copy

    load_tokens, load_cot = load(hbm_tokens, tokens), load(hbm_cot, cot)
    load_branch = [load(hbm_branch.at[k], w_branch.at[pl.ds(k * CP, C)]) for k in range(2)]
    load_gates, load_out = load(hbm_gates, gates), load(hbm_out, w_out.at[pl.ds(0, C)])
    load_down = load(hbm_down, w_down)
    load_up = [load(hbm_up.at[k], w_up.at[:, pl.ds(k * F, F)]) for k in range(2)]
    for rows in (w_branch.at[pl.ds(C, CP - C)], w_branch.at[pl.ds(CP + C, CP - C)], w_out.at[pl.ds(C, CP - C)], lhs):
        rows[...] = jnp.zeros(rows.shape, bf16)

    def finish():
        for group in groups:
            group.wait()
        for source in sources:
            wait_bytes(send_sems.at[source.i], source.size)

    def axis_of(h, phase):
        return (on_x, on_z)[(h + phase) % 2]

    def place(h, first_hop):
        return (turn(x, first_hop), z) if h == 0 else (x, turn(z, first_hop))

    class Gather:
        def __init__(self, buf, via, rows):
            self.buf, self.via, self.rows = buf, via, rows
            self.arrivals, self.last, self.source = [], Group(), Group(sources)
            for d in (1, 3, 2, 0):
                group = Group()
                for h in range(2):
                    send(self.view(buf, h, 0), self.view(via, h, 0), axis_of(h, 0)(d), group, self.source)
                    self.arrivals.append((h, d, group))

        def view(self, buf, h, d):
            return buf.at[h, *place(h, -d), pl.ds(0, self.rows[h])]

        def forward(self):
            for h, d, group in self.arrivals[-2:] + self.arrivals[:-2]:
                group.wait()
                src, dst = self.view(self.via, h, d), self.view(self.buf, h, d)
                for e in (1, 3, 2):
                    send(src, dst, axis_of(h, 1)(e), self.last, self.source)
                if d:
                    send(src, dst, other, self.last, self.source)

        def end(self):
            self.last.wait()

    class Scatter:
        def __init__(self, refs, rider=False, late=False):
            self.part, self.r1, self.s2, self.r2 = refs
            self.size = self.part.shape[3] - Q
            self.rider, self.late = rider, late
            self.source = Group(sources)
            self.hop1 = {(h, r): Group() for h in range(2) for r in range(4)}
            self.hop2 = dict.fromkeys(range(2), Group())
            if late:
                self.hop1.update({(2, r): Group() for r in range(4)})
                self.hop2[2] = Group()

        def rows(self, h, rider):
            first, size = ((0, self.size), (0, self.size - LATE if self.late else self.size), (self.size - LATE, LATE))[h]
            return pl.ds(first, size + (Q if rider and self.rides(h) else 0))

        def rides(self, h):
            return self.rider and h in ((0, 2) if self.late else (0, 1))

        def launch(self, g, halves):
            for h in halves:
                for k in FAR_FIRST + (0,):
                    if h == 0 or k:
                        r, d = (g, k) if h == 0 else (k, g)
                        self.pass_part(h, r, d)
            if g == 0 and not (self.late and 0 in halves):
                for h in (1, 2) if self.late else (1,):
                    for k in FAR_FIRST + (0,):
                        self.pass_part(h, 0, k)

        def pass_part(self, h, r, d):
            half = min(h, 1)
            spot = (turn(x, r), turn(z, d)) if half == 0 else (turn(x, d), turn(z, r))
            at = self.rows(h, r == 2)
            src, dst = self.part.at[half, *spot, at], self.r1.at[half, r, d, at]
            send(src, dst, axis_of(half, 1)(d), self.hop1[h, r], self.source)

        def produce(self, columns, halfway=None, launch=True):
            for g in FAR_FIRST + (0,):
                if g == 1 and halfway:
                    halfway()
                there = turn(x, g)
                low = columns(pl.multiple_of(there * 512, 512)).astype(bf16)
                for c in range(4):
                    piece = low[:, c * W : (c + 1) * W]
                    self.part[0, there, c, pl.ds(0, self.size)] = piece[: self.size]
                    at = self.rows(1, False)
                    self.part[1, there, c, at] = piece[self.size : self.size + at.size]
                if launch and g in (2, 0):
                    for k in (2,) if g == 2 else (1, 3, 0):
                        self.launch(k, (0, 1))

        def produce_late(self, columns):
            for g in FAR_FIRST + (0,):
                there = turn(x, g)
                low = columns(pl.multiple_of(there * 512, 512)).astype(bf16)
                for c in range(4):
                    self.part[1, there, c, self.rows(2, False)] = low[:, c * W : (c + 1) * W]
                self.launch(g, (2,))

        def ride(self, h, products):
            tile = rider_tile(jnp.sum(products.T, axis=0, keepdims=True))
            for c in range(4):
                spot = (0, turn(x, 2), c) if h == 0 else (1, c, turn(z, 2))
                self.part[*spot, pl.ds(self.size, Q)] = tile

        def step(self, h, r):
            half, extra = min(h, 1), pl.ds(self.size, Q)
            self.hop1[h, r].wait()

            def total(at):
                parts = [self.r1[half, r, d, at].astype(f32) for d in range(4)]
                return (parts[0] + parts[1]) + (parts[2] + parts[3])

            if r == 2 and self.rides(h):
                tile = rider_tile(jnp.sum(total(extra), axis=0, keepdims=True))
                for k in range(4):
                    self.s2[half, k, extra] = tile
            at = self.rows(h, False)
            self.s2[half, r, at] = total(at).astype(bf16)
            at = self.rows(h, True)
            send(self.s2.at[half, r, at], self.r2.at[half, r, at], axis_of(half, 0)(r), self.hop2[h], self.source)

        def middle(self, between=()):
            order = ((0, 2), (0, 1), (1, 2), (0, 3), (1, 1), (1, 3))
            if self.late:
                order += ((2, 2), (2, 1), (2, 3), (2, 0))
            order += ((0, 0), (1, 0))
            for i, (h, r) in enumerate(order):
                self.step(h, r)
                for work in between:
                    if work[0] == i:
                        for call in work[1:]:
                            call()

        def end(self):
            out, column = [], []
            for h in sorted(self.hop2):
                half, at = min(h, 1), self.rows(h, False)
                self.hop2[h].wait()
                parts = [self.r2[half, r, at].astype(f32) for r in range(4)]
                out.append((parts[0] + parts[1]) + (parts[2] + parts[3]))
                if self.rides(h):
                    rider = self.r2[half, 0, pl.ds(self.size, Q)].astype(f32)
                    for r in range(1, 4):
                        rider += self.r2[half, r, pl.ds(self.size, Q)].astype(f32)
                    row = jnp.sum(rider, axis=0, keepdims=True)
                    column.append(jnp.broadcast_to(row, (W, W)).T[: self.size])
            return jnp.concatenate(out, 0), (jnp.concatenate(column, 0) if column else None)

    def chunk(buf, c, size):
        return jnp.concatenate([buf[h, c // 4, c % 4, pl.ds(0, size)] for h in range(2)], 0)

    def gain_row(k, c):
        return tok_g[1, 0, c // 4, c % 4, pl.ds(S, Q)].astype(f32)[k : k + 1]

    def norm(buf, k, at):
        scale_ref, dst = ((scale1, first), (scale2, second))[k]
        total = jnp.zeros((at.size, W), f32)
        for c in range(16):
            v = chunk(buf, c, at.size // 2).astype(f32)
            total += v * v
        scale = lax.rsqrt(jnp.sum(total, axis=1, keepdims=True) * (1.0 / D) + EPS)
        scale_ref[at] = jnp.broadcast_to(scale, (at.size, W))
        for c in range(16):
            v = chunk(buf, c, at.size // 2).astype(f32)
            dst[at, c * W : (c + 1) * W] = (v * scale_ref[at] * gain_row(k, c)).astype(bf16)

    def dense(buf, dst, at):
        for c in range(16):
            dst[at, c * W : (c + 1) * W] = chunk(buf, c, at.size // 2)

    everything, streams = pl.ds(0, T), [pl.ds(0, H), pl.ds(H, H)]

    def block_at(there, core_there):
        return pl.multiple_of(((there % 2) * 4 + (there // 2) * 2 + core_there) * 256, 256)

    class Columns:
        def __init__(self, i, array):
            self.i, self.array, self.blocks = i, array, blocks.at[i]

        def start(self):
            self.group, source = Group(), Group(sources)
            for there in range(4):
                src = self.array.at[:, pl.ds(block_at(there, 1 - core), 256)]
                send(src, self.blocks.at[there, pl.ds(T, T)], other, self.group, source)
                src = self.array.at[:, pl.ds(block_at(there, core), 256)]
                pltpu.make_async_copy(src, self.blocks.at[there, pl.ds(0, T)], copy_sems.at[8 + self.i]).start()

        def ready(self):
            if not self.group.done:
                wait_bytes(copy_sems.at[8 + self.i], self.group.size)
            self.group.wait()

    class WeightGrad:
        def __init__(self, columns, left, g, relay, into):
            self.columns, self.left = columns, left
            self.g, self.relay, self.into, rows = g, relay, into, left.shape[0]
            cut = rows // 32 * 16 + (16 if rows % 32 else 0)
            self.a, self.b = pl.ds(0, cut), pl.ds(cut, rows - cut)

        def start(self, left=None):
            mine, peer = self.left.at[:, pl.ds(0, T)], self.left.at[:, pl.ds(T, T)]
            if left is not None:
                mine[...] = left
            self.source, self.pair = Group(sources), Group()
            send(mine, peer, other, self.pair, self.source)

        def make(self):
            self.pair.wait()
            self.columns.ready()
            self.last = Group()
            for there in range(4):
                self.g[there] = nn(self.left[...], self.columns.blocks[there]).astype(bf16)

        def compute(self):
            self.make()
            self.relayed = Group()
            far = turn(y, 2)
            send(self.g.at[far, self.a], self.relay.at[self.a], on_y(1), self.relayed, self.source)
            send(self.g.at[far, self.b], self.relay.at[self.b], on_y(-1), self.relayed, self.source)
            for k, at in ((1, self.b), (-1, self.a)):
                src = self.g.at[turn(y, k), at]
                send(src, self.into.at[(1 - k) // 2, at], on_y(k), self.last, self.source)

        def pass_on(self):
            self.relayed.wait()
            for k, at in ((1, self.a), (-1, self.b)):
                there = turn(y, k)
                self.g[there, at] = (self.g[there, at].astype(f32) + self.relay[at].astype(f32)).astype(bf16)
                send(self.g.at[there, at], self.into.at[(1 - k) // 2, at], on_y(k), self.last, self.source)

        def end(self):
            self.last.wait()
            return self.g[y].astype(f32) + self.into[0].astype(f32) + self.into[1].astype(f32)

        def compute_direct(self):
            self.make()
            for k in FAR_FIRST:
                send(self.g.at[turn(y, k)], self.into.at[k - 1], on_y(k), self.last, self.source)

        def end_direct(self):
            return self.end() + self.into[2].astype(f32)

    def transposed(value):
        tp[:, :C] = value
        return tp[...].T[:C]

    columns_cot, columns_second, columns_gm, columns_first = [
        Columns(i, array) for i, array in enumerate((cot_d, second, gm_d, first))
    ]

    def weight_grad(columns, i, rows):
        refs = (left_mlp, g_mlp, relay_mlp, y_mlp) if rows == F else (left_rec, g_rec, relay_rec, y_rec)
        return WeightGrad(columns, *[ref.at[i] for ref in refs])

    down, up = weight_grad(columns_cot, 0, F), [weight_grad(columns_second, 1 + k, F) for k in range(2)]
    out, branches = weight_grad(columns_gm, 0, C), [weight_grad(columns_first, 1 + k, C) for k in range(2)]

    gain_tile = jnp.concatenate([gains[...].astype(f32), jnp.zeros((Q - 2, W), f32)], 0).astype(bf16)
    tok_g[1, 0, x, z, pl.ds(S, Q)] = gain_tile
    load_tokens.wait()
    load_cot.wait()
    for h in range(2):
        for i in range(2):
            tok_g[i, h, x, z, pl.ds(0, S)] = tokens[pl.ds(i * H + h * S, S)]
        cot_g[h, x, z] = cot[pl.ds(h * H, H)]
    tp[...] = jnp.zeros_like(tp)
    pl.semaphore_wait(barrier, len(partners))
    tok_gathers = {i: Gather(tok_g.at[i], tok_v.at[i], (S + Q if i else S, S)) for i in (1, 0)}
    for i in (1, 0):
        tok_gathers[i].forward()
    cot_gather = Gather(cot_g, cot_v, (H, H))

    place_here = lax.broadcasted_iota(jnp.int32, (T, 1), 0) + seq * T
    start, begins = 0, [0]
    for j in range(3):
        start = start + lengths[0, j]
        begins.append(start)

    def begin_at(p):
        hit = p == begins[0]
        for b in begins[1:]:
            hit = jnp.logical_or(hit, p == b)
        return hit

    not_reset = jnp.where(begin_at(place_here), 0.0, 1.0)
    masks = [not_reset]
    for k in (1, 2):
        masks.append(masks[-1] * jnp.where(begin_at(place_here - k), 0.0, 1.0))

    for i in (1, 0):
        tok_gathers[i].end()
        at = streams[i]
        norm(tok_g.at[i], 0, at)
        if i:
            for copy in load_branch + [load_gates]:
                copy.wait()
        value = nt(first[at], w_branch[pl.ds(CP, CP)])[:, :C]
        p1[at] = value
        inner = value.astype(bf16).astype(f32)
        ext[pl.ds(8 + i * H, H)] = inner
        if i:
            halo_s[:, :C] = inner[H - 8 :]
            halo = send_one(halo_s, halo_r, on_seq(1))
    cot_gather.forward()
    columns_first.start()
    halo.wait()
    ext[pl.ds(0, 8)] = halo_r[:, :C]
    total = bias[0:1] + conv_w[0:1] * ext[pl.ds(8, T)]
    for k in (1, 2, 3):
        total = total + conv_w[k : k + 1] * (masks[k - 1] * ext[pl.ds(8 - k, T)])
    conv[...] = total
    conv_low = total.astype(bf16)
    rate = jax.nn.softplus(decay[...])
    r_gate = sigmoid(nn(conv_low, gates[0, 0]) + bias[1:2])
    rr[...] = r_gate
    a = jnp.exp(-8.0 * r_gate * rate)
    aa[...] = a
    coef[...] = a * not_reset
    i_gate = sigmoid(nn(conv_low, gates[1, 0]) + bias[2:3])
    ii[...] = i_gate
    root = jnp.sqrt(1.0 - a * a + 0.001)
    qq[...] = root

    def scan(A, B, reverse):
        step = 1
        while step < T:
            for ref, v, fill in ((pad_a, A, 1.0), (pad_b, B, 0.0)):
                ref[pl.ds(H, T)] = v
                ref[pl.ds(H + T if reverse else 0, H)] = jnp.full((H, C), fill, f32)
            at = pl.ds(H + step if reverse else H - step, T)
            B = B + A * pad_b[at]
            A = A * pad_a[at]
            step *= 2
        return A, B

    A, B = scan(coef[...], root * i_gate * conv[...], False)
    through[...] = A
    local[...] = B
    car_s[0:1, :C] = A[T - 1 :]
    car_s[1:2, :C] = B[T - 1 :]
    carries = Group()
    for d in (2, 1, 3):
        send(car_s, car_r.at[d - 1], on_seq(d), carries, misc)
    value = nt(first[...], w_branch[pl.ds(0, CP)])[:, :C]
    p0[...] = value
    act, slope = gelu_both(value)
    gel[...] = act
    dgel[...] = slope
    for copy in [load_out, load_down] + load_up:
        copy.wait()
    carries.wait()

    def fold(got, reverse):
        carried = jnp.zeros((1, C), f32)
        for d in (3, 2, 1):
            here = (seq + d < 4) if reverse else (seq - d >= 0)
            slot = 4 - d if reverse else d
            new = got[slot - 1, 0:1, :C] * carried + got[slot - 1, 1:2, :C]
            carried = jnp.where(here, new, carried)
        return carried

    carried = fold(car_r, False)
    value = local[...] + through[...] * carried
    state[...] = value
    prev[pl.ds(8, T)] = value
    prev[7:8] = carried
    mixed = gel[...] * value
    lhs[:, :C] = mixed.astype(bf16)

    def stream_refs(i):
        return [ref.at[i] for ref in (part_s, r1_s, s2_s, r2_s)]

    def part_refs(i):
        return [ref.at[i] for ref in (part_b, r1_b, s2_b, r2_b)]

    sums = [Scatter(stream_refs(i)) for i in range(2)]
    for at, scatter in zip(streams, sums):
        scatter.produce(lambda c: nn(lhs[at, :CP], w_out[:, pl.ds(c, 512)]))
    o_states[...] = value[T - 1 :]
    mixed_t = transposed(mixed).astype(bf16)
    cot_gather.end()
    dense(cot_g, cot_d, everything)
    sums[0].middle()
    columns_cot.start()
    sums[1].middle()
    gathers = []
    for i, at in enumerate(streams):
        branch, _ = sums[i].end()
        middle = tokens[at].astype(f32) + branch
        mid_own[at] = middle
        middle_low = middle.astype(bf16)
        for h in range(2):
            mid_g[i, h, x, z] = middle_low[h * S : (h + 1) * S]
        gathers.append(Gather(mid_g.at[i], mid_v.at[i], (S, S)))
    gathers[0].forward()
    ghid[...] = nt(cot_d[...], w_down[...])
    gathers[1].forward()

    sums = [Scatter(stream_refs(2 + i), True) for i in range(2)]
    for i, at in enumerate(streams):
        gathers[i].end()
        norm(mid_g.at[i], 1, at)
        pair = nn(second[at], w_up[...])
        pair0, pair1 = pair[:, :F], pair[:, F:]
        act, slope = gelu_both(pair0)
        hidden = act * pair1
        gh = ghid[at]
        gp0 = slope * pair1 * gh
        gp1 = act * gh
        products = gp0 * pair0 + gp1 * pair1
        products = products[:, :W] + products[:, W : 2 * W] + products[:, 2 * W :]
        gp_low = jnp.concatenate([gp0.astype(bf16), gp1.astype(bf16)], 1)
        for h in range(2):
            sums[i].ride(h, products[h * S : (h + 1) * S])
        sums[i].produce(lambda c: nt(gp_low, w_up[pl.ds(c, 512)]))
        hidden_low[at] = hidden.astype(bf16)
        for grad, left in ((down, hidden), (up[0], gp0), (up[1], gp1)):
            grad.left[:, at] = left.T.astype(bf16)
    down.start()
    columns_second.start()
    for grad in up:
        grad.start()
    sums[0].middle()
    down.compute()
    sums[1].middle()
    up[0].compute()

    gathers, gain_sum = [], jnp.zeros((1, W), f32)
    gain = gains[1:2].astype(f32)
    for i, at in enumerate(streams):
        grad_n, q = sums[i].end()
        v = mid_own[at].astype(bf16).astype(f32)
        s = scale2[at]
        grad_middle_own = cot[at].astype(f32) + s * gain * grad_n - v * s * s * q * (1.0 / D)
        gmid_own[at] = grad_middle_own
        low = grad_middle_own.astype(bf16)
        for h in range(2):
            gm_g[i, h, x, z] = low[h * S : (h + 1) * S]
        gathers.append(Gather(gm_g.at[i], gm_v.at[i], (S, S)))
        gain_sum += jnp.sum(grad_n * v * s, axis=0, keepdims=True)
    mine = small_own
    mine[...] = jnp.zeros((16, 256), f32)
    mine[1:2, :W] = gain_sum
    gathers[0].forward()
    up[1].compute()
    down.pass_on()
    gathers[1].forward()
    up[0].pass_on()
    scatter_out = Scatter(part_refs(0))
    scatter_out.produce(lambda c: nn(hidden_low[...], w_down[:, pl.ds(c, 512)]), launch=False)
    for i, at in enumerate(streams):
        gathers[i].end()
        dense(gm_g.at[i], gm_d, at)
        grad_mixed = nt(gm_d[at], w_out[...])[:, :C]
        grad_y_s[at] = dgel[at] * state[at] * grad_mixed
        grad_state_s[at] = gel[at] * grad_mixed
        if i == 0:
            for g in FAR_FIRST + (0,):
                scatter_out.launch(g, (0, 1))
    grad_y, grad_state = grad_y_s[...], grad_state_s[...]

    pad_a[pl.ds(0, T)] = coef[...]
    pad_a[pl.ds(T, 8)] = jnp.ones((8, C), f32)
    A, B = scan(pad_a[pl.ds(1, T)], grad_state, True)
    rev_s[0:1, :C] = through[T - 1 :]
    rev_s[1:2, :C] = coef[0:1] * B[0:1]
    carries = Group()
    for d in (2, 1, 3):
        send(rev_s, rev_r.at[d - 1], on_seq(d), carries, misc)
    columns_gm.start()
    up[1].pass_on()
    out.start(mixed_t)
    branches[0].start(transposed(grad_y).astype(bf16))
    out.compute()
    branches[0].compute()
    cv_t = transposed(conv[...]).astype(bf16)
    carries.wait()
    total = B + A * fold(rev_r, True)
    a, r_gate, i_gate, root, cv = aa[...], rr[...], ii[...], qq[...], conv[...]
    t_i = total * i_gate
    d_log = total * prev[pl.ds(7, T)] * coef[...] - t_i * cv * (a * a / root)
    d_gate = d_log * r_gate
    mine[9:10, :C] = -8.0 * sigmoid(decay[...]) * jnp.sum(d_gate, axis=0, keepdims=True)
    gpre0 = -8.0 * rate * d_gate * (1.0 - r_gate)
    direct = t_i * root
    gpre1 = direct * cv * (1.0 - i_gate)
    low0, low1 = gpre0.astype(bf16), gpre1.astype(bf16)
    mine[7:8, :C] = jnp.sum(low0.astype(f32), axis=0, keepdims=True)
    mine[8:9, :C] = jnp.sum(low1.astype(f32), axis=0, keepdims=True)
    grad_conv = direct + nt(low0, gates[0, 0]) + nt(low1, gates[1, 0])
    mine[6:7, :C] = jnp.sum(grad_conv, axis=0, keepdims=True)
    edge = jnp.zeros((8, C), f32)
    grad_inner = jnp.zeros((T, C), f32)
    for k in range(4):
        weighted = grad_conv if k == 0 else masks[k - 1] * grad_conv
        mine[2 + k : 3 + k, :C] = jnp.sum(weighted * ext[pl.ds(8 - k, T)], axis=0, keepdims=True)
        if k == 0:
            pad_a[pl.ds(0, 8)] = jnp.zeros((8, C), f32)
            pad_a[pl.ds(8 + T, 8)] = jnp.zeros((8, C), f32)
        pad_a[pl.ds(8, T)] = conv_w[k : k + 1] * weighted
        edge += pad_a[pl.ds(k, 8)]
        grad_inner += pad_a[pl.ds(8 + k, T)]
    back_s[:, :C] = edge
    back = send_one(back_s, back_r, on_seq(-1))
    lhs[:, :C] = grad_y.astype(bf16)
    lhs[:, CP : CP + C] = grad_inner.astype(bf16)
    scatter = Scatter(part_refs(1), True, True)
    tp[:, :C] = grad_y * p0[...] + grad_inner * p1[...]
    scatter.ride(0, tp[pl.ds(0, H), :W] + tp[pl.ds(0, H), W:])

    gg_pairs, gg_all = [], Group()

    def gates_grad():
        gg[0, :, :C] = nn(cv_t, low0).astype(bf16)
        gg[1, :, :C] = nn(cv_t, low1).astype(bf16)
        gg_pairs.append(send_one(gg.at[1 - core], gg_r, other))

    scatter.produce(lambda at: nn(lhs[...], w_branch[:, pl.ds(at, 512)]), gates_grad)
    small_pair = send_one(small_own, small_mate, other)
    gg_pairs[0].wait()
    gg_y[y] = (gg[core].astype(f32) + gg_r[...].astype(f32)).astype(bf16)
    for d in FAR_FIRST:
        send(gg_y.at[y], gg_y.at[y], on_y(d), gg_all, misc)
    back.wait()
    ext[pl.ds(0, T)] = grad_inner
    ext[pl.ds(T - 8, 8)] = grad_inner[T - 8 :] + back_r[:, :C]
    grad_inner = ext[pl.ds(0, T)]
    tp[:, :C] = grad_y * p0[...] + grad_inner * p1[...]
    scatter.ride(1, tp[pl.ds(H, H), :W] + tp[pl.ds(H, H), W:])
    late = pl.ds(T - LATE, LATE)
    lhs[late, CP : CP + C] = grad_inner[T - LATE :].astype(bf16)
    scatter.produce_late(lambda at: nn(lhs[late], w_branch[:, pl.ds(at, 512)]))
    branches[1].start(transposed(grad_inner).astype(bf16))
    others = ((2, False), (2, True), (1, False), (1, True), (3, False), (3, True), (0, False))
    smalls, gain_sums = Group(), Group()
    out.pass_on()
    branches[0].pass_on()
    small_pair.wait()
    small[y] = small_own[...] + small_mate[...]
    for d in FAR_FIRST:
        send(small.at[y], small.at[y], on_y(d), smalls, misc)
    scatter.middle(((3, branches[1].compute_direct),))
    scatter_out.middle()
    o_down[...] = down.end()
    for k in range(2):
        o_up[k] = up[k].end().T


    grad_n, q = scatter.end()
    v = tokens[...].astype(f32)
    s = scale1[...]
    gain = gains[0:1].astype(f32)
    mine = gain_one.at[dp * 4 + seq]
    mine[...] = jnp.broadcast_to(jnp.sum(grad_n * v * s, axis=0, keepdims=True), (8, W))
    for d, same in others:
        send(mine, mine, on_y(d, same), gain_sums, misc)
    gg_all.wait()
    gg_f[core] = gg_y[0].astype(f32) + gg_y[1].astype(f32) + gg_y[2].astype(f32) + gg_y[3].astype(f32)
    gg_share = send_one(gg_f.at[core], gg_f.at[core], other)
    o_tokens[...] = gmid_own[...] + s * gain * grad_n - v * s * s * q * (1.0 / D)
    o_out[...] = out.end()
    result, _ = scatter_out.end()
    o_block[...] = (mid_own[...] + result).astype(bf16)
    o_branch[0] = branches[0].end()
    o_branch[1] = branches[1].end_direct()
    gg_share.wait()
    for k in range(2):
        o_gates[k, 0] = gg_f[k, :, :C]
    smalls.wait()
    total = small[0]
    for j in range(1, 4):
        total += small[j]
    o_gains[1:2] = total[1:2, :W]
    o_conv[...] = total[2:6, :C]
    o_bias[...] = total[6:9, :C]
    o_decay[...] = total[9:10, :C]
    gain_sums.wait()
    total = gain_one[0, 0:1]
    for j in range(1, 8):
        total += gain_one[j, 0:1]
    o_gains[0:1] = total
    finish()


def hand_over(*refs):
    n = 12
    copies = [pltpu.make_async_copy(refs[i], refs[n + i], refs[-1].at[i]) for i in range(n)]
    for copy in copies:
        copy.start()
    for copy in copies:
        copy.wait()


def on_device(
    tokens, doc_lengths, cotangent, norm_gains, w_branch, conv_weight, lru_bias, decay, gate_weights, w_out, w_up, w_down
):
    def shape(dims, kind=f32):
        return jax.ShapeDtypeStruct(dims, kind)

    def vmem(*dims):
        return pltpu.VMEM(dims, f32)

    def low(*dims):
        return pltpu.VMEM(dims, bf16)

    near, far = pl.BlockSpec(memory_space=pltpu.VMEM), pl.BlockSpec(memory_space=pl.ANY)
    outs = [
        shape((T, W), bf16), shape((T, W)), shape((2, W)), shape((2, C, 256)), shape((4, C)), shape((3, C)),
        shape((1, C)), shape((2, 1, C, C)), shape((C, 256)), shape((2, 256, F)), shape((F, 256)), shape((1, C)),
    ]
    scratch = (
        [low(T, W), low(T, W), low(2 * CP, D), low(2, 1, C, C), low(CP, D), low(D, 2 * F), low(F, D)]
        + ([low(2, 2, 4, 4, S + Q, W), low(2, 4, 4, H, W)] + [low(2, 2, 4, 4, S, W)] * 2) * 2 + [low(T, D)] * 4
        + [low(4, 2, 4, 4, S + Q, W)] * 2 + [low(4, 2, 4, S + Q, W)] * 2
        + [low(2, 2, 4, 4, H + Q, W)] * 2 + [low(2, 2, 4, H + Q, W)] * 2
        + [low(T, F), vmem(T, C), vmem(T, C)]
        + [vmem(T + 8, C)] + [vmem(T, C)] * 13 + [vmem(T + 8, C), vmem(2 * H + T, C), vmem(2 * H + T, C), vmem(T, T)]
        + [vmem(T, F), vmem(T, W), vmem(T, W), vmem(T, W), vmem(T, W)]
        + [low(4, 4, 2 * T, 256)]
        + [low(3, F, 2 * T), low(3, 4, F, 256), low(3, F, 256), low(3, 2, F, 256)]
        + [low(3, C, 2 * T), low(3, 4, C, 256), low(3, C, 256), low(3, 3, C, 256), low(T, 2 * CP)]
        + [vmem(8, 256)] * 4 + [vmem(8, 256), vmem(3, 8, 256)] * 2
        + [low(2, C, 256), low(C, 256), low(4, C, 256), vmem(2, C, 256)]
        + [vmem(16, 256), vmem(16, 256), vmem(4, 16, 256), vmem(8, 8, W), vmem(3072, W)]
        + [pltpu.SemaphoreType.DMA((N_SENT,)), pltpu.SemaphoreType.DMA((N_SEMS,)), pltpu.SemaphoreType.DMA((12,))]
    )
    made = pl.pallas_call(
        kernel,
        out_shape=[pltpu.VMEM(o.shape, o.dtype) for o in outs],
        in_specs=[pl.BlockSpec(memory_space=pltpu.SMEM)] + [near] * 4 + [far] * 7,
        out_specs=[near] * 12,
        scratch_shapes=scratch,
        compiler_params=pltpu.CompilerParams(
            collective_id=0, has_side_effects=True, vmem_limit_bytes=56 * 2**20
        ),
    )(
        doc_lengths, norm_gains, conv_weight, lru_bias, decay.reshape(1, C), tokens.reshape(T, W),
        cotangent.reshape(T, W), jnp.swapaxes(w_branch, 1, 2), gate_weights, w_out, w_up, w_down,
    )
    made = list(pl.pallas_call(
        hand_over,
        out_shape=outs,
        in_specs=[near] * 12,
        out_specs=[far] * 12,
        scratch_shapes=[pltpu.SemaphoreType.DMA((12,))],
        compiler_params=pltpu.CompilerParams(vmem_limit_bytes=2 * 2**20),
    )(*made))
    made[0], made[1] = made[0].reshape(1, T, W), made[1].reshape(1, T, W)
    made[3] = jnp.swapaxes(made[3], 1, 2)
    made[6], made[11] = made[6].reshape(C), made[11].reshape(1, 1, C)
    return tuple(made)


def solution(mesh):
    in_specs = (
        P("dp", "seq", "mp"), P("dp", None), P("dp", "seq", "mp"), P(None, "mp"), P(None, None, "mp"), P(None, "mp"),
        P(None, "mp"), P("mp"), P(None, "mp", None, None), P("mp", None), P(None, None, "mp"), P("mp", None),
    )
    out_specs = (
        P("dp", "seq", "mp"), P("dp", "seq", "mp"), P(None, "mp"), P(None, ("dp", "seq"), "mp"), P(None, "mp"),
        P(None, "mp"), P("mp"), P(None, "mp", None, None), P("mp", ("dp", "seq")), P(None, ("dp", "seq"), "mp"),
        P("mp", ("dp", "seq")), P("dp", "seq", "mp"),
    )
    return jax.shard_map(on_device, mesh=mesh, in_specs=in_specs, out_specs=out_specs, check_vma=False)
```
